32 devices in a mesh: group: 8 (over y, x, core), peer: 4 (over z).
Axes of the slice: x: 2, y: 2, z: 4, core: 2. Of those that a mesh axis runs over, the one named last changes fastest.
Arguments:
- table: bfloat16 [131072, 256], P(('group', 'peer')), may hold values from -6 to 6
- behaviour_ids: int32 [64, 1024], P(('group', 'peer')), may hold values from 0 to 131071, as said below
- lengths: int32 [64], P(('group', 'peer')), may hold values from 256 to 1024, as said below
- candidates: bfloat16 [64, 64, 256], P('group', 'peer'), may hold values from -6 to 6
- labels: float32 [64, 64], P('group', 'peer'), may hold values from 0 to 1
- cand_counts: int32 [64], P(('group', 'peer')), may hold values from 4 to 64, as said below
- w_query: bfloat16 [256, 256], replicated, may hold values from -0.375 to 0.375
- w_key: bfloat16 [256, 256], replicated, may hold values from -0.375 to 0.375
- w_value: bfloat16 [256, 256], replicated, may hold values from -0.375 to 0.375
- w_out: bfloat16 [256, 256], replicated, may hold values from -0.375 to 0.375
Outputs:
- table_grad: bfloat16 [131072, 256], P(('group', 'peer'))
- weight_grads: float32 [4, 256, 256], replicated
The draws below stay inside these ranges and needn't reach their ends.
Inputs may be any that keep to these rules, and one draw needn't show every extreme that they name: `behaviour_ids`: device d of group+peer (group slowest) holds table rows 4096 * d to 4096 * (d + 1) - 1. Among the 2048 behaviour slots of the users of one device, at most 96 name rows held by any one device, and for every device some device's rows are named exactly 96 times. Ids may repeat. `lengths`: some user has 1024 live slots. `cand_counts`: some user has 64 live candidates.
All inputs are finite; a program needn't handle non-finite values.
Results may differ from the reference program's by a relative error of at most 0.018.
Values may be sent and summed in bfloat16 or wider, within the bound.
No kernel may reach another device: no remote copies, remote signals or barrier semaphores. Data moves between devices by JAX's collectives and lax.ppermute only.
A program may use at most 64 MiB of HBM per device.

```python
import jax
import jax.numpy as jnp
from jax import lax

E = 256
HEADS = 4
LMAX = 1024
CMAX = 64
CMIN = 4
USERS_DEV = 2
ROWS_DEV = 4096
HD = 64
NSHARD = 32
USERS = 64
TABLE = 131072
CAP = 96


def draw_behaviour_ids(key, part):
    key = jax.random.fold_in(key, 11)
    slots = USERS_DEV * LMAX

    def one_device(dev_key):
        key_a, key_b, key_c, key_d = jax.random.split(dev_key, 4)
        heavy = jax.random.randint(key_a, (), 0, NSHARD, dtype=jnp.int32)
        others = jnp.tile(jnp.arange(NSHARD - 1, dtype=jnp.int32), CAP)
        others = jax.random.permutation(key_b, others)[:slots - CAP]
        others = others + (others >= heavy).astype(jnp.int32)
        owners = jnp.concatenate([jnp.full((CAP,), heavy, jnp.int32), others])
        owners = jax.random.permutation(key_c, owners)
        local = jax.random.randint(key_d, (slots,), 0, ROWS_DEV, dtype=jnp.int32)
        return (owners * ROWS_DEV + local).reshape(USERS_DEV, LMAX)
    keys = jax.random.split(key, NSHARD)
    return jax.vmap(one_device)(keys).reshape(USERS, LMAX)


def draw_lengths(key, part):
    key = jax.random.fold_in(key, 23)
    drawn = jax.random.randint(key, (USERS,), LMAX // 4, LMAX + 1, dtype=jnp.int32)
    return drawn.at[0].set(LMAX)


def draw_cand_counts(key, part):
    key = jax.random.fold_in(key, 37)
    drawn = jax.random.randint(key, (USERS,), CMIN, CMAX + 1, dtype=jnp.int32)
    return drawn.at[0].set(CMAX)


def levels(own_key, extent, cuts, least, high):
    loudness = 1.0
    for axis_at, parts in cuts:
        steps = jax.random.uniform(jax.random.fold_in(jax.random.fold_in(own_key, 6), axis_at), (parts,), jnp.float32, least / len(cuts), high / len(cuts))
        loudness = loudness * jnp.repeat(jnp.exp(steps), extent[axis_at] // parts).reshape((-1,) + (1,) * (len(extent) - 1 - axis_at))
    return loudness


def noise(own_key, extent, deviation, limit, cuts=(), kind=jnp.bfloat16):
    values = jax.random.normal(own_key, extent, jnp.float32) * deviation
    if len(cuts) > 0:
        values = levels(own_key, extent, cuts, -0.22, 0.18) * values
    return jnp.clip(values, min=-limit, max=limit).astype(kind)


def setup_inputs(seed: int = 0) -> dict:
    streams_of = jax.random.split(jax.random.key(seed), 11)
    return {
        "table": noise(streams_of[0], (TABLE, E), 1.0, 6.0, ((0, 32),)),
        "behaviour_ids": draw_behaviour_ids(jax.random.fold_in(streams_of[10], 71), 0),
        "lengths": draw_lengths(jax.random.fold_in(streams_of[10], 71), 0),
        "candidates": noise(streams_of[3], (USERS, CMAX, E), 1.0, 6.0, ((0, 8), (1, 4))),
        "labels": jnp.clip(1.0 * jax.random.uniform(streams_of[4], (USERS, CMAX), jnp.float32) ** levels(streams_of[4], (USERS, CMAX), ((0, 8), (1, 4)), -0.2, 0.2), 0.0, 1.0),
        "cand_counts": draw_cand_counts(jax.random.fold_in(streams_of[10], 71), 0),
        "w_query": noise(streams_of[6], (E, E), E ** -0.5, 0.375),
        "w_key": noise(streams_of[7], (E, E), E ** -0.5, 0.375),
        "w_value": noise(streams_of[8], (E, E), E ** -0.5, 0.375),
        "w_out": noise(streams_of[9], (E, E), E ** -0.5, 0.375),
    }


def user_pass(rows, cand, label, length, count, w_query, w_key, w_value, w_out):
    seq = rows.shape[0]
    num = cand.shape[0]
    scale = float(HD) ** -0.5
    root = float(E) ** 0.5
    query = jnp.dot(cand, w_query, preferred_element_type=jnp.float32).astype(jnp.bfloat16)
    keys = jnp.dot(rows, w_key, preferred_element_type=jnp.float32).astype(jnp.bfloat16)
    values = jnp.dot(rows, w_value, preferred_element_type=jnp.float32).astype(jnp.bfloat16)
    q_heads = query.reshape(num, HEADS, HD).astype(jnp.float32)
    k_heads = keys.reshape(seq, HEADS, HD).astype(jnp.float32)
    v_heads = values.reshape(seq, HEADS, HD).astype(jnp.float32)
    scores = jnp.einsum("chd,lhd->hcl", q_heads, k_heads) * scale
    live_key = jnp.arange(seq, dtype=jnp.int32) < length
    scores = jnp.where(live_key[None, None, :], scores, jnp.float32(-1e30))
    probs = jax.nn.softmax(scores, axis=-1)
    probs_b = probs.astype(jnp.bfloat16)
    probs_f = probs_b.astype(jnp.float32)
    mixed = jnp.einsum("hcl,lhd->chd", probs_f, v_heads).reshape(num, E).astype(jnp.bfloat16)
    proj = jnp.dot(mixed, w_out, preferred_element_type=jnp.float32)
    cand_f = cand.astype(jnp.float32)
    logit = jnp.sum(proj * cand_f, axis=1) / root
    live_cand = (jnp.arange(num, dtype=jnp.int32) < count).astype(jnp.float32)
    grad_logit = (jax.nn.sigmoid(logit) - label) * live_cand / USERS_DEV
    grad_proj = (grad_logit[:, None] * cand_f / root).astype(jnp.bfloat16)
    grad_wo = jnp.dot(mixed.T, grad_proj, preferred_element_type=jnp.float32)
    grad_mixed = jnp.dot(grad_proj, w_out.T, preferred_element_type=jnp.float32).astype(jnp.bfloat16)
    g_heads = grad_mixed.reshape(num, HEADS, HD).astype(jnp.float32)
    grad_probs = jnp.einsum("chd,lhd->hcl", g_heads, v_heads)
    inner = jnp.sum(probs * grad_probs, axis=-1, keepdims=True)
    grad_scores = (probs * (grad_probs - inner) * scale).astype(jnp.bfloat16).astype(jnp.float32)
    grad_query = jnp.einsum("hcl,lhd->chd", grad_scores, k_heads).reshape(num, E).astype(jnp.bfloat16)
    grad_keys = jnp.einsum("hcl,chd->lhd", grad_scores, q_heads).reshape(seq, E).astype(jnp.bfloat16)
    grad_values = jnp.einsum("hcl,chd->lhd", probs_f, g_heads).reshape(seq, E).astype(jnp.bfloat16)
    grad_wq = jnp.dot(cand.T, grad_query, preferred_element_type=jnp.float32)
    grad_wk = jnp.dot(rows.T, grad_keys, preferred_element_type=jnp.float32)
    grad_wv = jnp.dot(rows.T, grad_values, preferred_element_type=jnp.float32)
    grad_rows = (jnp.dot(grad_keys, w_key.T, preferred_element_type=jnp.float32)
                 + jnp.dot(grad_values, w_value.T, preferred_element_type=jnp.float32)).astype(jnp.bfloat16)
    return jnp.stack([grad_wq, grad_wk, grad_wv, grad_wo]), grad_rows


def reference(table, behaviour_ids, lengths, candidates, labels, cand_counts, w_query, w_key, w_value, w_out):
    def advance(carry, inputs):
        weight_sum, table_sum = carry
        ids, cand, label, length, count = inputs
        rows = table[ids]
        grads, grad_rows = user_pass(rows, cand, label, length, count, w_query, w_key, w_value, w_out)
        table_sum = table_sum.at[ids].add(grad_rows.astype(jnp.float32))
        return (weight_sum + grads, table_sum), None

    start = (jnp.zeros((4, E, E), jnp.float32), jnp.zeros(table.shape, jnp.float32))
    (weight_sum, table_sum), _ = lax.scan(advance, start, (behaviour_ids, candidates, labels, lengths, cand_counts))
    return table_sum.astype(jnp.bfloat16), weight_sum
```

```python
import functools

import jax
import jax.numpy as jnp
from jax import lax
from jax.experimental import pallas as pl
from jax.experimental.pallas import tpu as pltpu
from jax.sharding import PartitionSpec as P

HEADS = 4
USERS_DEV = 2
ALL = ("group", "peer")
BF16 = jnp.bfloat16
F32 = jnp.float32
VMEM_LIMIT = 48 * 1024 * 1024


def nt(a, b):
    return lax.dot_general(a, b, (((1,), (1,)), ((), ())), preferred_element_type=F32)


def nn(a, b):
    return jnp.dot(a, b, preferred_element_type=F32)


def plan_kernel(rows_dev, lengths_ref, ids_ref, requests_ref, flags_ref):
    users, seq = ids_ref.shape
    shards, capacity = requests_ref.shape
    block = 256
    shift = rows_dev.bit_length() - 1
    before = (
        lax.broadcasted_iota(jnp.int32, (block, block), 0)
        < lax.broadcasted_iota(jnp.int32, (block, block), 1)
    ).astype(BF16)
    device = lax.broadcasted_iota(jnp.int32, (shards, block), 0)
    place = lax.broadcasted_iota(jnp.int32, (capacity, block), 0).astype(F32)
    lane = lax.broadcasted_iota(jnp.int32, (1, block), 1)
    count = jnp.zeros((shards, 1), F32)
    rows = jnp.zeros((2 * shards, capacity), F32)
    flags = jnp.zeros((capacity, shards), F32)
    for user in range(users):
        for start in range(0, seq, block):
            ids = ids_ref[user : user + 1, start : start + block]
            owner = lax.shift_right_logical(ids, shift)
            row = ids & (rows_dev - 1)
            live = lane + start < lengths_ref[user]
            owner = jnp.where(live, owner, shards)
            hot = (device == owner).astype(F32)
            hot_b = hot.astype(BF16)
            earlier = nn(hot_b, before) + count
            count = count + jnp.sum(hot, axis=1, keepdims=True)
            rank = jnp.sum(hot * earlier, axis=0, keepdims=True)
            ranked = (place == rank).astype(F32).astype(BF16)
            high = lax.shift_right_logical(row, 6).astype(F32)
            low = (row & 63).astype(F32)
            parts = jnp.concatenate([hot * high, hot * low], axis=0).astype(BF16)
            rows = rows + nt(parts, ranked)
            flags = flags + nt(ranked, (hot * float(user + 1)).astype(BF16))
    requests_ref[...] = (rows[:shards] * 64.0 + rows[shards:]).astype(jnp.int32)
    flags_ref[...] = flags


def plan(behaviour_ids, lengths, rows_dev, shards, capacity):
    return pl.pallas_call(
        functools.partial(plan_kernel, rows_dev),
        out_shape=(
            jax.ShapeDtypeStruct((shards, capacity), jnp.int32),
            jax.ShapeDtypeStruct((capacity, shards), F32),
        ),
        in_specs=[
            pl.BlockSpec(memory_space=pltpu.SMEM),
            pl.BlockSpec(memory_space=pltpu.VMEM),
        ],
        out_specs=(
            pl.BlockSpec(memory_space=pltpu.VMEM),
            pl.BlockSpec(memory_space=pltpu.VMEM),
        ),
        compiler_params=pltpu.CompilerParams(vmem_limit_bytes=VMEM_LIMIT),
        name="plan",
    )(lengths, behaviour_ids)


def gather_kernel(wanted_ref, table_ref, out_ref, wide, some):
    step = some.shape[0]
    wide[...] = table_ref[...].astype(F32)

    def body(t, carry):
        start = pl.multiple_of(t * step, step)
        for k in range(step):
            row = wanted_ref[start + k]
            some[pl.ds(k, 1), :] = wide[pl.ds(row, 1), :]
        out_ref[pl.ds(start, step), :] = some[...].astype(BF16)
        return carry

    lax.fori_loop(0, out_ref.shape[0] // step, body, 0)


def gather(wanted, table):
    slots = wanted.shape[0]
    width = table.shape[1]
    return pl.pallas_call(
        gather_kernel,
        out_shape=jax.ShapeDtypeStruct((slots, width), BF16),
        in_specs=[
            pl.BlockSpec(memory_space=pltpu.SMEM),
            pl.BlockSpec(memory_space=pltpu.VMEM),
        ],
        out_specs=pl.BlockSpec(memory_space=pltpu.VMEM),
        scratch_shapes=[pltpu.VMEM(table.shape, F32), pltpu.VMEM((64, width), F32)],
        compiler_params=pltpu.CompilerParams(vmem_limit_bytes=VMEM_LIMIT),
        name="gather_rows",
    )(wanted, table)


def scatter_kernel(wanted_ref, grads_ref, out_ref):
    tile = out_ref.shape[0]
    slots = grads_ref.shape[0]
    block = 256
    row = lax.broadcasted_iota(jnp.int32, (tile, block), 0) + pl.program_id(0) * tile
    total = jnp.zeros(out_ref.shape, F32)
    for start in range(0, slots, block):
        hot = (row == wanted_ref[:, start : start + block]).astype(F32).astype(BF16)
        total = total + nn(hot, grads_ref[start : start + block, :])
    out_ref[...] = total.astype(BF16)


def scatter(wanted, grads, rows_dev):
    slots, width = grads.shape
    tile = 512
    return pl.pallas_call(
        scatter_kernel,
        grid=(rows_dev // tile,),
        out_shape=jax.ShapeDtypeStruct((rows_dev, width), BF16),
        in_specs=[
            pl.BlockSpec((1, slots), lambda t: (0, 0)),
            pl.BlockSpec((slots, width), lambda t: (0, 0)),
        ],
        out_specs=pl.BlockSpec((tile, width), lambda t: (t, 0)),
        compiler_params=pltpu.CompilerParams(vmem_limit_bytes=VMEM_LIMIT),
        name="scatter_rows",
    )(wanted, grads)


def by_head(x):
    head_size = x.shape[1] // HEADS
    head = lax.broadcasted_iota(jnp.int32, x.shape, 1) // head_size
    return jnp.concatenate([jnp.where(head == h, x, 0.0) for h in range(HEADS)], axis=0)


def attend_kernel(
    num,
    counts_ref,
    rows_ref,
    flags_ref,
    cands_ref,
    label_ref,
    wq_ref,
    wk_ref,
    wv_ref,
    wo_ref,
    grad_rows_ref,
    weights_ref,
    turned,
    scores,
    expo,
):
    slots, width = rows_ref.shape
    capacity, shards = flags_ref.shape
    live = cands_ref.shape[0]
    users = live // num
    head_size = width // HEADS
    scale = float(head_size) ** (-0.5)
    root = float(width) ** 0.5
    cols = HEADS * live
    tile = 384
    tiles = range(0, slots, tile)
    per_tile = tile // capacity

    cands = cands_ref[...]
    cand_f = cands.astype(F32)
    wq, wk, wv, wo = wq_ref[...], wk_ref[...], wv_ref[...], wo_ref[...]
    query = by_head(nn(cands, wq).astype(BF16).astype(F32) * scale).astype(BF16)
    query_w = nt(query, wk).astype(BF16)

    user_of = lax.rem(lax.broadcasted_iota(jnp.int32, (1, cols), 1), live) // num + 1
    user_of = user_of.astype(F32)
    top = jnp.full((1, cols), -1e30, F32)
    for i, start in enumerate(tiles):
        rows = rows_ref[start : start + tile, :]
        turned[:, start : start + tile] = rows.T
        flag = jnp.concatenate(
            [flags_ref[:, o : o + 1] for o in range(i * per_tile, (i + 1) * per_tile)], axis=0
        )
        score = jnp.where(flag == user_of, nt(rows, query_w), -1e30)
        scores[start : start + tile, :] = score
        top = jnp.maximum(top, jnp.max(score, axis=0, keepdims=True))

    norm = jnp.zeros((1, cols), F32)
    rows_e = jnp.zeros((width, cols), F32)
    for start in tiles:
        e = jnp.exp(scores[start : start + tile, :] - top)
        norm = norm + jnp.sum(e, axis=0, keepdims=True)
        e = e.astype(BF16)
        expo[start : start + tile, :] = e
        rows_e = rows_e + nn(turned[:, start : start + tile], e)

    inv = 1.0 / norm
    rows_e = (rows_e * inv).astype(BF16)
    wv_t = wv.T
    mixed_t = jnp.concatenate(
        [
            nn(wv_t[h * head_size : (h + 1) * head_size, :], rows_e[:, h * live : (h + 1) * live])
            for h in range(HEADS)
        ],
        axis=0,
    )
    mixed_tb = mixed_t.astype(BF16)
    proj = nn(mixed_tb.T, wo)
    logit = jnp.sum(proj * cand_f, axis=1, keepdims=True) / root
    index = lax.broadcasted_iota(jnp.int32, (live, 1), 0)
    alive = jnp.zeros((live, 1), jnp.bool_)
    for user in range(users):
        alive = alive | ((index >= user * num) & (index < user * num + counts_ref[user]))
    grad_logit = jnp.where(alive, (jax.nn.sigmoid(logit) - label_ref[...]) / USERS_DEV, 0.0)
    grad_proj = (grad_logit * cand_f / root).astype(BF16)
    weights_ref[3 * width :, :] = nn(mixed_tb, grad_proj).astype(weights_ref.dtype)
    grad_mixed = nt(grad_proj, wo).astype(BF16).astype(F32)
    both = grad_mixed.T * mixed_t
    inner = jnp.concatenate(
        [
            jnp.sum(both[h * head_size : (h + 1) * head_size, :], axis=0, keepdims=True)
            for h in range(HEADS)
        ],
        axis=1,
    )
    inner = inner * inv
    inv_col = jnp.broadcast_to(inv, (128, cols)).T[:, :1]
    grad_heads = by_head(grad_mixed)
    grad_scaled = (grad_heads * inv_col).astype(BF16)
    grad_w = nt(grad_scaled, wv).astype(BF16)

    rows_s = jnp.zeros((width, cols), F32)
    for start in tiles:
        rows = rows_ref[start : start + tile, :]
        e = expo[start : start + tile, :]
        grad_score = (e.astype(F32) * (nt(rows, grad_w) - inner)).astype(BF16)
        rows_s = rows_s + nn(turned[:, start : start + tile], grad_score)
        grad_rows_ref[start : start + tile, :] = (
            nn(grad_score, query_w) + nn(e, grad_w)
        ).astype(BF16)

    rows_s = rows_s.astype(BF16)
    wk_t = wk.T
    grad_query_t = (
        jnp.concatenate(
            [
                nn(
                    wk_t[h * head_size : (h + 1) * head_size, :],
                    rows_s[:, h * live : (h + 1) * live],
                )
                for h in range(HEADS)
            ],
            axis=0,
        )
        * scale
    ).astype(BF16)
    weights_ref[:width, :] = nt(cands.T, grad_query_t).astype(weights_ref.dtype)
    weights_ref[width : 2 * width, :] = nn(rows_s, query).astype(weights_ref.dtype)
    weights_ref[2 * width : 3 * width, :] = nn(rows_e, grad_heads.astype(BF16)).astype(
        weights_ref.dtype
    )


def attend(rows, flags, cands, label, cand_counts, w_query, w_key, w_value, w_out):
    slots, width = rows.shape
    users, num, _ = cands.shape
    cols = HEADS * users * num
    vmem = pl.BlockSpec(memory_space=pltpu.VMEM)
    return pl.pallas_call(
        functools.partial(attend_kernel, num),
        out_shape=(
            jax.ShapeDtypeStruct((slots, width), BF16),
            jax.ShapeDtypeStruct((4 * width, width), BF16),
        ),
        in_specs=[pl.BlockSpec(memory_space=pltpu.SMEM)] + [vmem] * 8,
        out_specs=(vmem, vmem),
        scratch_shapes=[
            pltpu.VMEM((width, slots), BF16),
            pltpu.VMEM((slots, cols), F32),
            pltpu.VMEM((slots, cols), BF16),
        ],
        compiler_params=pltpu.CompilerParams(vmem_limit_bytes=VMEM_LIMIT),
        name="attend",
    )(
        cand_counts,
        rows,
        flags,
        cands.reshape(users * num, width),
        label.reshape(users * num, 1),
        w_query,
        w_key,
        w_value,
        w_out,
    )


def exchange(x):
    return lax.all_to_all(x, ALL, split_axis=0, concat_axis=0, tiled=True)


def local(
    table, behaviour_ids, lengths, candidates, labels, cand_counts, w_query, w_key, w_value, w_out
):
    shards = lax.axis_size(ALL)
    users, seq = behaviour_ids.shape
    rows_dev, width = table.shape
    total = users * seq
    capacity = total // shards + total // (2 * shards)
    slots = shards * capacity
    requests, flags = plan(behaviour_ids, lengths, rows_dev, shards, capacity)
    wanted = exchange(requests)
    served = gather(wanted.reshape(slots), table)
    arrived = exchange(served.reshape(shards, capacity, width)).reshape(slots, width)
    cands = lax.all_to_all(candidates, "peer", split_axis=0, concat_axis=1, tiled=True)
    label = lax.all_to_all(
        labels.astype(BF16), "peer", split_axis=0, concat_axis=1, tiled=True
    ).astype(F32)
    grad_rows, weights = attend(
        arrived, flags, cands, label, cand_counts, w_query, w_key, w_value, w_out
    )
    returned = exchange(grad_rows.reshape(shards, capacity, width)).reshape(slots, width)
    share = 4 * width // shards
    parts = exchange(weights.reshape(shards, share, width))
    part = jnp.sum(parts.astype(F32), axis=0).astype(BF16)
    weight_grads = exchange(jnp.broadcast_to(part[None], (shards, share, width)))
    table_grad = scatter(wanted.reshape(1, slots), returned, rows_dev)
    return table_grad, weight_grads.reshape(4, width, width).astype(F32)


def solution(mesh):
    in_specs = (
        P(ALL, None),
        P(ALL, None),
        P(ALL),
        P("group", "peer", None),
        P("group", "peer"),
        P(ALL),
        P(),
        P(),
        P(),
        P(),
    )
    out_specs = (P(ALL, None), P())
    return jax.shard_map(local, mesh=mesh, in_specs=in_specs, out_specs=out_specs, check_vma=False)
```

```python
import functools
import math

import jax
import jax.numpy as jnp
from jax import lax
from jax.experimental import pallas as pl
from jax.experimental.pallas import tpu as pltpu
from jax.sharding import Mesh
from jax.sharding import PartitionSpec as P

HEADS = 4
USERS_DEV = 2
ALL = ("group", "hi", "lo")
BY_HALF = ("hi", "group", "lo")
HALF = ("group", "lo")
PEERS = ("hi", "lo")
BF16 = jnp.bfloat16
F32 = jnp.float32
VMEM_LIMIT = 12 * 1024 * 1024
LOWEST = -1e30
LINE = 8


def nt(a, b):
    return lax.dot_general(a, b, (((1,), (1,)), ((), ())), preferred_element_type=F32)


def nn(a, b):
    return jnp.dot(a, b, preferred_element_type=F32)


def cost(flops, transcendentals):
    return pl.CostEstimate(flops=flops, bytes_accessed=0, transcendentals=transcendentals)


def log2(n):
    return n.bit_length() - 1


def plan_kernel(
    rows_dev,
    sizes,
    lengths_hbm,
    counts_hbm,
    ids_hbm,
    cands_hbm,
    labels_hbm,
    requests_ref,
    flags_ref,
    labelled_ref,
    lengths_ref,
    counts_ref,
    ids_ref,
    cands_ref,
    labels_ref,
    sems,
):
    copies = [
        pltpu.make_async_copy(source, target, sems.at[k])
        for k, (source, target) in enumerate(
            (
                (lengths_hbm, lengths_ref),
                (counts_hbm, counts_ref),
                (ids_hbm, ids_ref),
                (cands_hbm, cands_ref),
                (labels_hbm, labels_ref),
            )
        )
    ]
    for copy in copies:
        copy.start()
    for copy in copies:
        copy.wait()
    groups, low = sizes
    users, seq = ids_ref.shape
    shards = requests_ref.shape[0]
    capacity = requests_ref.shape[1] - LINE
    half = shards // 2
    block = 256
    before = (
        lax.broadcasted_iota(jnp.int32, (block, block), 0)
        < lax.broadcasted_iota(jnp.int32, (block, block), 1)
    ).astype(BF16)
    device = lax.broadcasted_iota(jnp.int32, (shards, block), 0)
    place = lax.broadcasted_iota(jnp.int32, (capacity, block), 0).astype(F32)
    lane = lax.broadcasted_iota(jnp.int32, (1, block), 1)
    count = jnp.zeros((shards, 1), F32)
    rows = jnp.zeros((2 * shards, capacity), F32)
    flags = jnp.zeros((capacity, shards), F32)
    for user in range(users):
        for start in range(0, seq, block):
            ids = ids_ref[user : user + 1, start : start + block]
            owner = lax.shift_right_logical(ids, log2(rows_dev))
            row = ids & (rows_dev - 1)
            group = lax.shift_right_logical(owner, log2(2 * low))
            high = lax.shift_right_logical(owner, log2(low)) & 1
            owner = high * half + group * low + (owner & (low - 1))
            live = lane + start < lengths_ref[user]
            owner = jnp.where(live, owner, shards)
            hot = (device == owner).astype(F32)
            hot_b = hot.astype(BF16)
            earlier = nn(hot_b, before) + count
            count = count + jnp.sum(hot, axis=1, keepdims=True)
            rank = jnp.sum(hot * earlier, axis=0, keepdims=True)
            ranked = (place == rank).astype(F32).astype(BF16)
            upper = lax.shift_right_logical(row, 6).astype(F32)
            lower = (row & 63).astype(F32)
            parts = jnp.concatenate([hot * upper, hot * lower], axis=0).astype(BF16)
            rows = rows + nt(parts, ranked)
            flags = flags + nt(ranked, (hot * float(user + 1)).astype(BF16))
    requests = jnp.concatenate(
        [rows[:shards] * 64.0 + rows[shards:], jnp.broadcast_to(count, (shards, LINE))], axis=1
    )
    requests_ref[...] = requests.astype(jnp.int32)
    below = lax.broadcasted_iota(jnp.int32, (8, half), 0)
    counts = jnp.zeros((8, half), F32)
    for user in range(users):
        counts = jnp.where(below == user, counts_ref[user].astype(F32), counts)
    for h in range(2):
        flags_ref[h, :capacity, :] = flags[:, h * half : (h + 1) * half]
        flags_ref[h, capacity:, :] = counts
    _, held, width = cands_ref.shape
    square = lax.broadcasted_iota(jnp.int32, (held, held), 0)
    square = square == lax.broadcasted_iota(jnp.int32, (held, held), 1)
    lane = lax.broadcasted_iota(jnp.int32, (held, 128), 1)
    for user in range(cands_ref.shape[0]):
        label = jnp.sum(
            jnp.where(square, labels_ref[user : user + 1, :], 0.0), axis=1, keepdims=True
        )
        labelled_ref[user, :, :width] = cands_ref[user]
        labelled_ref[user, :, width:] = jnp.where(lane == 0, label, 0.0).astype(BF16)


def plan(behaviour_ids, lengths, cand_counts, candidates, labels, rows_dev, sizes, capacity):
    half = sizes[0] * sizes[1]
    vmem = pl.BlockSpec(memory_space=pltpu.VMEM)
    operands = (lengths, cand_counts, behaviour_ids, candidates, labels)
    return pl.pallas_call(
        functools.partial(plan_kernel, rows_dev, sizes),
        out_shape=(
            jax.ShapeDtypeStruct((2 * half, capacity + LINE), jnp.int32),
            jax.ShapeDtypeStruct((2, capacity + 8, half), F32),
            jax.ShapeDtypeStruct(candidates.shape[:2] + (candidates.shape[2] + 128,), BF16),
        ),
        in_specs=[pl.BlockSpec(memory_space=pltpu.HBM)] * 5,
        out_specs=(vmem,) * 3,
        scratch_shapes=[
            pltpu.SMEM(lengths.shape, jnp.int32),
            pltpu.SMEM(cand_counts.shape, jnp.int32),
            pltpu.VMEM(behaviour_ids.shape, jnp.int32),
            pltpu.VMEM(candidates.shape, BF16),
            pltpu.VMEM(labels.shape, F32),
            pltpu.SemaphoreType.DMA((5,)),
        ],
        compiler_params=pltpu.CompilerParams(vmem_limit_bytes=VMEM_LIMIT),
        name="plan",
    )(*(pltpu.with_memory_space_constraint(x, pltpu.HBM) for x in operands))


def gather_kernel(blocks, wanted_ref, table_hbm, out_hbm, narrow, wide, out, in_sems, out_sems):
    slots = out.shape[0]
    capacity = slots // blocks
    line = capacity + LINE
    joint = 1 if capacity % 16 == 0 else math.lcm(capacity, 16) // capacity
    step = 16 if joint == 1 else joint * capacity
    loads = in_sems.shape[0]
    size = narrow.shape[0] // loads
    copies = []
    for k in range(loads):
        part = pl.ds(k * size, size)
        copies.append(pltpu.make_async_copy(table_hbm.at[part], narrow.at[part], in_sems.at[k]))
        copies[-1].start()
    out[...] = jnp.zeros(out.shape, BF16)
    for k, copy in enumerate(copies):
        copy.wait()
        part = slice(k * size, (k + 1) * size)
        wide[part, :] = narrow[part, :].astype(F32)

    def bucket(b, carry):
        first = b * joint * line

        def fetch(c, carry):
            at = c * step
            start = pl.multiple_of(b * joint * capacity + at, 16)
            for k in range(0, step, 16):
                rows = [
                    wide[pl.ds(wanted_ref[first + at + n + n // capacity * LINE], 1), :]
                    for n in range(k, k + 16)
                ]
                out[pl.ds(start + k, 16), :] = jnp.concatenate(rows, axis=0).astype(BF16)
            return carry

        steps = 1 if joint > 1 else lax.div(wanted_ref[first + capacity] + step - 1, step)
        return lax.fori_loop(0, steps, fetch, carry)

    copies = []
    groups = out_sems.shape[0]
    each = blocks // joint // groups
    for g in range(groups):
        lax.fori_loop(g * each, (g + 1) * each, bucket, 0)
        part = pl.ds(g * each * joint * capacity, each * joint * capacity)
        copies.append(pltpu.make_async_copy(out.at[part], out_hbm.at[part], out_sems.at[g]))
        copies[-1].start()
    for copy in copies:
        copy.wait()


def gather(wanted, table, blocks):
    width = table.shape[1]
    slots = wanted.shape[0] - blocks * LINE
    return pl.pallas_call(
        functools.partial(gather_kernel, blocks),
        out_shape=jax.ShapeDtypeStruct((slots, width), BF16),
        in_specs=[
            pl.BlockSpec(memory_space=pltpu.SMEM),
            pl.BlockSpec(memory_space=pltpu.HBM),
        ],
        out_specs=pl.BlockSpec(memory_space=pltpu.HBM),
        scratch_shapes=[
            pltpu.VMEM(table.shape, BF16),
            pltpu.VMEM(table.shape, F32),
            pltpu.VMEM((slots, width), BF16),
            pltpu.SemaphoreType.DMA((8,)),
            pltpu.SemaphoreType.DMA((4,)),
        ],
        compiler_params=pltpu.CompilerParams(vmem_limit_bytes=VMEM_LIMIT),
        name="gather_rows",
    )(wanted, pltpu.with_memory_space_constraint(table, pltpu.HBM))


def scatter_kernel(wanted_ref, returned_ref, out_ref, grads):
    tile = out_ref.shape[0]
    slots = grads.shape[0]
    blocks = returned_ref.shape[0]
    each = slots // blocks
    block = 256

    @pl.when(pl.program_id(0) == 0)
    def _():
        for b in range(blocks):
            grads[b * each : (b + 1) * each, :] = returned_ref[b, :each, :]

    row = lax.broadcasted_iota(jnp.int32, (tile, block), 0) + pl.program_id(0) * tile
    total = jnp.zeros(out_ref.shape, F32)
    for start in range(0, slots, block):
        hot = (row == wanted_ref[:, start : start + block]).astype(F32).astype(BF16)
        total = total + nn(hot, grads[start : start + block, :])
    out_ref[...] = total.astype(BF16)


def scatter(wanted, returned, rows_dev):
    slots = wanted.shape[1]
    width = returned.shape[-1]
    tile = 512
    return pl.pallas_call(
        scatter_kernel,
        grid=(rows_dev // tile,),
        out_shape=jax.ShapeDtypeStruct((rows_dev, width), BF16),
        in_specs=[
            pl.BlockSpec((1, slots), lambda t: (0, 0)),
            pl.BlockSpec(returned.shape, lambda t: (0, 0, 0)),
        ],
        out_specs=pl.BlockSpec((tile, width), lambda t: (t, 0)),
        scratch_shapes=[pltpu.VMEM((slots, width), BF16)],
        compiler_params=pltpu.CompilerParams(vmem_limit_bytes=VMEM_LIMIT),
        name="scatter_rows",
    )(wanted, returned)


def by_head(x):
    head_size = x.shape[1] // HEADS
    head = lax.broadcasted_iota(jnp.int32, x.shape, 1) // head_size
    return jnp.concatenate([jnp.where(head == h, x, 0.0) for h in range(HEADS)], axis=0)


def head_blocks(a_t, b, live):
    size = a_t.shape[0] // HEADS
    return jnp.concatenate(
        [nn(a_t[h * size : (h + 1) * size, :], b[:, h * live : (h + 1) * live]) for h in range(HEADS)],
        axis=0,
    )


def pieces(x):
    a = x.astype(BF16)
    x = x - a.astype(F32)
    b = x.astype(BF16)
    return [a, b, (x - b.astype(F32)).astype(BF16)]


def stacked(x, live):
    return jnp.concatenate([x[:, h * live : (h + 1) * live] for h in range(HEADS)], axis=0)


def flat(x):
    return jnp.concatenate([x[h : h + 1, :] for h in range(HEADS)], axis=1)


def query_kernel(cands_ref, wq_ref, wk_ref, query_ref, query_w_ref):
    width = wq_ref.shape[0]
    live = cands_ref.shape[1]
    scale = float(width // HEADS) ** (-0.5)
    cands = jnp.concatenate([cands_ref[r, :, :width] for r in range(2)], axis=0)
    query = nn(cands, wq_ref[...]).astype(BF16).astype(F32) * scale
    for r in range(2):
        heads = by_head(query[r * live : (r + 1) * live]).astype(BF16)
        query_ref[r] = heads
        query_w_ref[r] = nt(heads, wk_ref[...]).astype(BF16)


def queries(cands, w_query, w_key):
    width = w_query.shape[0]
    shape = jax.ShapeDtypeStruct((2, HEADS * cands.shape[1], width), BF16)
    vmem = pl.BlockSpec(memory_space=pltpu.VMEM)
    return pl.pallas_call(
        query_kernel,
        out_shape=(shape, shape),
        in_specs=[vmem] * 3,
        out_specs=(vmem, vmem),
        compiler_params=pltpu.CompilerParams(vmem_limit_bytes=VMEM_LIMIT),
        name="queries",
    )(cands, w_query, w_key)


def take_tile(rows_ref, r, t, per_tile, capacity):
    return jnp.concatenate(
        [
            rows_ref[b, r * capacity : (r + 1) * capacity, :]
            for b in range(t * per_tile, (t + 1) * per_tile)
        ],
        axis=0,
    )


TILE = 384


def forward_kernel(
    r, num, rows_ref, flags_ref, query_w_ref, wv_ref, expo_ref, part_ref, mean_ref, turned_ref, scores
):
    blocks, both, width = rows_ref.shape
    capacity = both // 2
    cols = query_w_ref.shape[1]
    live = cols // HEADS
    per_tile = TILE // capacity
    tiles = blocks // per_tile
    user_of = lax.rem(lax.broadcasted_iota(jnp.int32, (1, cols), 1), live) // num + 1
    user_of = user_of.astype(F32)
    query_w = query_w_ref[r]
    top = jnp.full((1, cols), LOWEST, F32)
    for t in range(tiles):
        rows = take_tile(rows_ref, r, t, per_tile, capacity)
        turned_ref[:, t * TILE : (t + 1) * TILE] = rows.T
        flag = jnp.concatenate(
            [flags_ref[r, :capacity, o : o + 1] for o in range(t * per_tile, (t + 1) * per_tile)],
            axis=0,
        )
        score = jnp.where(flag == user_of, nt(rows, query_w), LOWEST)
        scores[t * TILE : (t + 1) * TILE, :] = score
        top = jnp.maximum(top, jnp.max(score, axis=0, keepdims=True))
    norm = jnp.zeros((1, cols), F32)
    rows_e = jnp.zeros((width, cols), F32)
    for t in range(tiles):
        e = jnp.exp(scores[t * TILE : (t + 1) * TILE, :] - top)
        norm = norm + jnp.sum(e, axis=0, keepdims=True)
        e = e.astype(BF16)
        expo_ref[t * TILE : (t + 1) * TILE, :] = e
        rows_e = rows_e + nn(turned_ref[:, t * TILE : (t + 1) * TILE], e)
    mean = (rows_e * (1.0 / norm)).astype(BF16)
    mean_ref[...] = mean
    part_ref[:width, :] = head_blocks(wv_ref[...].T, mean, live).astype(BF16)
    rest = pieces(stacked(top, live)) + pieces(stacked(norm, live))
    rest.append(jnp.zeros((8, live), BF16))
    part_ref[width:, :] = jnp.concatenate([x.astype(F32) for x in rest], axis=0).astype(BF16)


def forward(r, rows, flags, query_w, num, w_value):
    blocks, both, width = rows.shape
    cols = query_w.shape[1]
    slots = blocks * both // 2
    vmem = pl.BlockSpec(memory_space=pltpu.VMEM)
    return pl.pallas_call(
        functools.partial(forward_kernel, r, num),
        out_shape=(
            jax.ShapeDtypeStruct((slots, cols), BF16),
            jax.ShapeDtypeStruct((width + 32, cols // HEADS), BF16),
            jax.ShapeDtypeStruct((width, cols), BF16),
            jax.ShapeDtypeStruct((width, slots), BF16),
        ),
        in_specs=[vmem] * 4,
        out_specs=(vmem,) * 4,
        scratch_shapes=[pltpu.VMEM((slots, cols), F32)],
        compiler_params=pltpu.CompilerParams(vmem_limit_bytes=VMEM_LIMIT),
        cost_estimate=cost(4 * slots * width * cols, slots * cols),
        name="forward",
    )(rows, flags, query_w, w_value)


def opened(part_ref, width):
    rest = part_ref[width:, :].astype(F32)
    top = rest[0:4] + rest[4:8] + rest[8:12]
    norm = rest[12:16] + rest[16:20] + rest[20:24]
    return part_ref[:width, :].astype(F32), top, norm


def backward_kernel(
    r,
    users,
    rows_ref,
    flags_ref,
    cands_ref,
    place_ref,
    query_ref,
    query_w_ref,
    wk_ref,
    wv_ref,
    wo_ref,
    expo_ref,
    own_ref,
    other_ref,
    mean_ref,
    turned_ref,
    *refs,
):
    if r == 0:
        out_ref, weights = refs
    else:
        first_ref, first_weights, out_ref, weights = refs
    blocks, both, width = rows_ref.shape
    capacity = both // 2
    live = cands_ref.shape[1]
    num = live // users
    cols = HEADS * live
    head_size = width // HEADS
    scale = float(head_size) ** (-0.5)
    root = float(width) ** 0.5
    per_tile = TILE // capacity
    tiles = blocks // per_tile
    wv, wo = wv_ref[...], wo_ref[...]

    mixed_own, top_own, norm_own = opened(own_ref, width)
    mixed_other, top_other, norm_other = opened(other_ref, width)
    top = jnp.maximum(top_own, top_other)
    factor = jnp.exp(top_own - top)
    part_own = norm_own * factor
    part_other = norm_other * jnp.exp(top_other - top)
    inv = 1.0 / (part_own + part_other)
    factor = factor * inv
    part_own = part_own * inv
    part_other = part_other * inv
    mixed_t = jnp.concatenate(
        [
            mixed_own[h * head_size : (h + 1) * head_size] * part_own[h : h + 1]
            + mixed_other[h * head_size : (h + 1) * head_size] * part_other[h : h + 1]
            for h in range(HEADS)
        ],
        axis=0,
    )
    mixed_tb = mixed_t.astype(BF16)
    cands = cands_ref[r, :, :width]
    cand_f = cands.astype(F32)
    proj = nn(mixed_tb.T, wo)
    logit = jnp.sum(proj * cand_f, axis=1, keepdims=True) / root
    label = cands_ref[r, :, width:].astype(F32)[:, 0:1]
    index = lax.broadcasted_iota(jnp.int32, (live, 1), 0)
    limit = jnp.zeros((live, 1), F32)
    for user in range(users):
        count = flags_ref[r, capacity + user : capacity + user + 1, 0:1]
        limit = jnp.where(index >= user * num, count, limit)
    alive = place_ref[...] < limit
    grad_logit = jnp.where(alive, (jax.nn.sigmoid(logit) - label) / USERS_DEV, 0.0)
    grad_proj = (grad_logit * cand_f / root).astype(BF16)
    grad_mixed = nt(grad_proj, wo).astype(BF16).astype(F32)
    joint = grad_mixed.T * mixed_t
    inner = jnp.concatenate(
        [
            jnp.sum(joint[h * head_size : (h + 1) * head_size, :], axis=0, keepdims=True)
            for h in range(HEADS)
        ],
        axis=0,
    )
    inner = flat(inner * factor)
    factor = flat(factor)
    factor_col = jnp.broadcast_to(factor, (128, cols)).T[:, :1]
    grad_heads = by_head(grad_mixed)
    grad_w = nt((grad_heads * factor_col).astype(BF16), wv).astype(BF16)

    query_w = query_w_ref[r]
    rows_s = jnp.zeros((width, cols), F32)
    for t in range(tiles):
        rows = take_tile(rows_ref, r, t, per_tile, capacity)
        e = expo_ref[t * TILE : (t + 1) * TILE, :]
        grad_score = (e.astype(F32) * (nt(rows, grad_w) - inner)).astype(BF16)
        rows_s = rows_s + nn(turned_ref[:, t * TILE : (t + 1) * TILE], grad_score)
        grad_rows = (nn(grad_score, query_w) + nn(e, grad_w)).astype(BF16)
        for k in range(per_tile):
            out_ref[t * per_tile + k, r * capacity : (r + 1) * capacity, :] = grad_rows[
                k * capacity : (k + 1) * capacity, :
            ]

    rows_s = rows_s.astype(BF16)
    grad_query_t = (head_blocks(wk_ref[...].T, rows_s, live) * scale).astype(BF16)
    share = flat(part_own)
    parts = (
        nt(cands.T, grad_query_t),
        nn(rows_s, query_ref[r]),
        nn((mean_ref[...].astype(F32) * share).astype(BF16), grad_heads.astype(BF16)),
        nn(mixed_tb, grad_proj) * 0.5,
    )
    for k, part in enumerate(parts):
        if r == 0:
            weights[k * width : (k + 1) * width, :] = part
        else:
            weights[k * width : (k + 1) * width, :] = (
                first_weights[k * width : (k + 1) * width, :] + part
            )
    if r == 1:
        rows_each = 4 * width // blocks
        for b in range(blocks):
            out_ref[b, :capacity, :] = first_ref[b]
            out_ref[b, both:, :] = weights[b * rows_each : (b + 1) * rows_each, :].astype(BF16)


def backward(r, users, rows, *operands):
    blocks, both, width = rows.shape
    vmem = pl.BlockSpec(memory_space=pltpu.VMEM)
    weights = jax.ShapeDtypeStruct((4 * width, width), F32)
    if r == 0:
        out_shape = (jax.ShapeDtypeStruct((blocks, both // 2, width), BF16), weights)
        scratch_shapes = []
    else:
        out_shape = jax.ShapeDtypeStruct((blocks, both + 4 * width // blocks, width), BF16)
        scratch_shapes = [pltpu.VMEM(weights.shape, F32)]
    return pl.pallas_call(
        functools.partial(backward_kernel, r, users),
        out_shape=out_shape,
        in_specs=[vmem] * (1 + len(operands)),
        out_specs=(vmem, vmem) if r == 0 else vmem,
        scratch_shapes=scratch_shapes,
        compiler_params=pltpu.CompilerParams(vmem_limit_bytes=VMEM_LIMIT),
        cost_estimate=cost(6 * blocks * both * width * width * HEADS, 0),
        name="backward",
    )(rows, *operands)


def exchange(x, axes):
    return lax.all_to_all(x, axes, split_axis=0, concat_axis=0, tiled=True)


def swap_halves(x):
    return lax.ppermute(x, "hi", [(0, 1), (1, 0)])


def swap(x):
    peers = lax.axis_size(PEERS)
    return lax.ppermute(x, PEERS, [(i, peers - 1 - i) for i in range(peers)])


def half_candidates(mine, users):
    peers, low = lax.axis_size(PEERS), lax.axis_size("lo")
    hi, lo = lax.axis_index("hi"), lax.axis_index("lo")
    mine = mine.reshape((peers, users) + mine.shape[1:])

    def for_pair(to):
        lower = jnp.minimum(to, peers - 1 - to)
        return jnp.stack(
            [
                lax.dynamic_index_in_dim(mine, lower, 0, keepdims=False),
                lax.dynamic_index_in_dim(mine, peers - 1 - lower, 0, keepdims=False),
            ]
        )

    got = [for_pair(hi * low + lo)]
    for step in range(1, low):
        got.append(
            lax.ppermute(
                for_pair(hi * low + lax.rem(lo + step, low)),
                "lo",
                [(i, (i + step) % low) for i in range(low)],
            )
        )
    return jnp.concatenate(got, axis=2)


def local(
    table, behaviour_ids, lengths, candidates, labels, cand_counts, w_query, w_key, w_value, w_out
):
    shards = lax.axis_size(ALL)
    half = shards // 2
    sizes = (lax.axis_size("group"), lax.axis_size("lo"))
    first = lax.axis_index("hi") == 0
    users, seq = behaviour_ids.shape
    rows_dev, width = table.shape
    total = users * seq
    capacity = total // shards + total // (2 * shards)
    slots = shards * capacity
    num = candidates.shape[1] * lax.axis_size("hi") * lax.axis_size("lo")

    requests, flags, mine = plan(
        behaviour_ids, lengths, cand_counts, candidates, labels, rows_dev, sizes, capacity
    )
    wanted = exchange(requests, BY_HALF)
    here = half_candidates(mine, users)
    there = swap(here)
    flags_kept = jnp.where(first, flags[0], flags[1])
    swapped = swap(jnp.where(first, flags[1], flags[0]))

    wanted = wanted.reshape(2, sizes[0], sizes[1], capacity + LINE)
    lower = jnp.where(first, wanted[0], wanted[0, :, ::-1])
    upper = jnp.where(first, wanted[1, :, ::-1], wanted[1])
    wanted = jnp.stack([lower, upper], axis=2).reshape(shards, capacity + LINE)
    served = gather(wanted.reshape(-1), table, shards)
    wanted = wanted[:, :capacity]
    served, there, swapped = lax.optimization_barrier((served, there, swapped))
    rows = exchange(served.reshape(half, 2 * capacity, width), HALF)
    flags = jnp.stack(
        [jnp.where(first, flags_kept, swapped), jnp.where(first, swapped, flags_kept)]
    )
    cands = jnp.concatenate([jnp.where(first, here, there), jnp.where(first, there, here)], axis=2)
    cands = cands.reshape(2, users * num, width + 128)
    query, query_w = queries(cands, w_query, w_key)
    low, held = lax.axis_size("lo"), candidates.shape[1]
    step = lax.broadcasted_iota(jnp.int32, (2, low, held), 1)
    upper_half = lax.broadcasted_iota(jnp.int32, (2, low, held), 0)
    start = jnp.where(first == (upper_half == 0), lax.axis_index("lo"), low - 1 - lax.axis_index("lo"))
    place = upper_half * low + lax.rem(start - step + low, low)
    place = place * held + lax.broadcasted_iota(jnp.int32, (2, low, held), 2)
    place = jnp.broadcast_to(place.astype(F32).reshape(1, num), (users, num)).reshape(users * num, 1)

    ahead = [forward(r, rows, flags, query_w, num, w_value) for r in range(2)]
    back = []
    for r, (expo, own, mean, turned) in enumerate(ahead):
        back = backward(
            r,
            users,
            rows,
            flags,
            cands,
            place,
            query,
            query_w,
            w_key,
            w_value,
            w_out,
            expo,
            own,
            swap(own),
            mean,
            turned,
            *back,
        )
    outgoing = back
    returned = exchange(outgoing, HALF)
    table_grad = scatter(wanted.reshape(1, slots), returned, rows_dev)

    part = jnp.sum(returned[:, 2 * capacity :, :].astype(F32), axis=0).astype(BF16)
    part = (part.astype(F32) + swap_halves(part).astype(F32)).astype(BF16)
    weight_grads = exchange(jnp.broadcast_to(part[None], (half,) + part.shape), HALF)
    return table_grad, weight_grads.reshape(4, width, width).astype(F32)


def solution(mesh):
    groups, peers = mesh.shape["group"], mesh.shape["peer"]
    mesh = Mesh(mesh.devices.reshape(groups, 2, peers // 2), ALL)
    in_specs = (
        P(ALL, None),
        P(ALL, None),
        P(ALL),
        P("group", ("hi", "lo"), None),
        P("group", ("hi", "lo")),
        P(ALL),
        P(),
        P(),
        P(),
        P(),
    )
    out_specs = (P(ALL, None), P())
    return jax.shard_map(local, mesh=mesh, in_specs=in_specs, out_specs=out_specs, check_vma=False)
```

```python
import functools
import math

import jax
import jax.numpy as jnp
from jax import lax
from jax.experimental import pallas as pl
from jax.experimental.pallas import tpu as pltpu
from jax.sharding import Mesh
from jax.sharding import PartitionSpec as P

HEADS = 4
USERS_DEV = 2
ALL = ("group", "hi", "lo")
BY_HALF = ("hi", "group", "lo")
HALF = ("group", "lo")
PEERS = ("hi", "lo")
BF16 = jnp.bfloat16
F32 = jnp.float32
VMEM_LIMIT = 12 * 1024 * 1024
LOWEST = -1e30
LINE = 8


def nt(a, b):
    return lax.dot_general(a, b, (((1,), (1,)), ((), ())), preferred_element_type=F32)


def nn(a, b):
    return jnp.dot(a, b, preferred_element_type=F32)


def cost(flops, transcendentals):
    return pl.CostEstimate(flops=flops, bytes_accessed=0, transcendentals=transcendentals)


def log2(n):
    return n.bit_length() - 1


def plan_kernel(
    rows_dev,
    sizes,
    lengths_hbm,
    counts_hbm,
    ids_hbm,
    cands_hbm,
    labels_hbm,
    requests_ref,
    flags_ref,
    labelled_ref,
    lengths_ref,
    counts_ref,
    ids_ref,
    cands_ref,
    labels_ref,
    sems,
):
    copies = [
        pltpu.make_async_copy(source, target, sems.at[k])
        for k, (source, target) in enumerate(
            (
                (lengths_hbm, lengths_ref),
                (counts_hbm, counts_ref),
                (ids_hbm, ids_ref),
                (cands_hbm, cands_ref),
                (labels_hbm, labels_ref),
            )
        )
    ]
    for copy in copies:
        copy.start()
    for copy in copies:
        copy.wait()
    groups, low = sizes
    users, seq = ids_ref.shape
    shards = requests_ref.shape[0]
    capacity = requests_ref.shape[1] - LINE
    half = shards // 2
    block = 256
    before = (
        lax.broadcasted_iota(jnp.int32, (block, block), 0)
        < lax.broadcasted_iota(jnp.int32, (block, block), 1)
    ).astype(BF16)
    device = lax.broadcasted_iota(jnp.int32, (shards, block), 0)
    place = lax.broadcasted_iota(jnp.int32, (capacity, block), 0).astype(F32)
    lane = lax.broadcasted_iota(jnp.int32, (1, block), 1)
    count = jnp.zeros((shards, 1), F32)
    rows = jnp.zeros((3 * shards, capacity), F32)
    for user in range(users):
        for start in range(0, seq, block):
            ids = ids_ref[user : user + 1, start : start + block]
            owner = lax.shift_right_logical(ids, log2(rows_dev))
            row = ids & (rows_dev - 1)
            group = lax.shift_right_logical(owner, log2(2 * low))
            high = lax.shift_right_logical(owner, log2(low)) & 1
            owner = high * half + group * low + (owner & (low - 1))
            live = lane + start < lengths_ref[user]
            owner = jnp.where(live, owner, shards)
            hot = (device == owner).astype(F32)
            hot_b = hot.astype(BF16)
            earlier = nn(hot_b, before) + count
            count = count + jnp.sum(hot, axis=1, keepdims=True)
            rank = jnp.sum(hot * earlier, axis=0, keepdims=True)
            ranked = (place == rank).astype(F32).astype(BF16)
            upper = lax.shift_right_logical(row, 6).astype(F32)
            lower = (row & 63).astype(F32)
            parts = jnp.concatenate([hot * upper, hot * lower, hot * float(user + 1)], axis=0)
            rows = rows + nt(parts.astype(BF16), ranked)
    requests = jnp.concatenate(
        [rows[:shards] * 64.0 + rows[shards : 2 * shards], jnp.broadcast_to(count, (shards, LINE))],
        axis=1,
    )
    requests_ref[...] = requests.astype(jnp.int32)
    lane = lax.broadcasted_iota(jnp.int32, (shards, 128 - capacity), 1)
    rest = jnp.zeros(lane.shape, F32)
    for user in range(users):
        rest = jnp.where(lane == user, counts_ref[user].astype(F32), rest)
    flags_ref[...] = jnp.concatenate([rows[2 * shards :], rest], axis=1).astype(BF16)
    _, held, width = cands_ref.shape
    square = lax.broadcasted_iota(jnp.int32, (held, held), 0)
    square = square == lax.broadcasted_iota(jnp.int32, (held, held), 1)
    lane = lax.broadcasted_iota(jnp.int32, (held, 128), 1)
    for user in range(cands_ref.shape[0]):
        label = jnp.sum(
            jnp.where(square, labels_ref[user : user + 1, :], 0.0), axis=1, keepdims=True
        )
        labelled_ref[user, :, :width] = cands_ref[user]
        labelled_ref[user, :, width:] = jnp.where(lane == 0, label, 0.0).astype(BF16)


def plan(behaviour_ids, lengths, cand_counts, candidates, labels, rows_dev, sizes, capacity):
    half = sizes[0] * sizes[1]
    vmem = pl.BlockSpec(memory_space=pltpu.VMEM)
    operands = (lengths, cand_counts, behaviour_ids, candidates, labels)
    return pl.pallas_call(
        functools.partial(plan_kernel, rows_dev, sizes),
        out_shape=(
            jax.ShapeDtypeStruct((2 * half, capacity + LINE), jnp.int32),
            jax.ShapeDtypeStruct((2 * half, 128), BF16),
            jax.ShapeDtypeStruct(candidates.shape[:2] + (candidates.shape[2] + 128,), BF16),
        ),
        in_specs=[pl.BlockSpec(memory_space=pltpu.HBM)] * 5,
        out_specs=(vmem,) * 3,
        scratch_shapes=[
            pltpu.SMEM(lengths.shape, jnp.int32),
            pltpu.SMEM(cand_counts.shape, jnp.int32),
            pltpu.VMEM(behaviour_ids.shape, jnp.int32),
            pltpu.VMEM(candidates.shape, BF16),
            pltpu.VMEM(labels.shape, F32),
            pltpu.SemaphoreType.DMA((5,)),
        ],
        compiler_params=pltpu.CompilerParams(vmem_limit_bytes=VMEM_LIMIT),
        cost_estimate=cost(2**24, 0),
        name="plan",
    )(*(pltpu.with_memory_space_constraint(x, pltpu.HBM) for x in operands))


def gather_kernel(blocks, wanted_ref, table_hbm, out_hbm, narrow, wide, out, in_sems, sems):
    slots = out.shape[0]
    capacity = slots // blocks
    line = capacity + LINE
    joint = 1 if capacity % 16 == 0 else math.lcm(capacity, 16) // capacity
    step = 16 if joint == 1 else joint * capacity
    loads = in_sems.shape[0]
    size = narrow.shape[0] // loads
    copies = []
    for k in range(loads):
        part = pl.ds(k * size, size)
        copies.append(pltpu.make_async_copy(table_hbm.at[part], narrow.at[part], in_sems.at[k]))
        copies[-1].start()
    out[...] = jnp.zeros(out.shape, BF16)
    for k, copy in enumerate(copies):
        copy.wait()
        part = slice(k * size, (k + 1) * size)
        wide[part, :] = narrow[part, :].astype(F32)

    def bucket(b, carry):
        first = b * joint * line

        def fetch(c, carry):
            at = c * step
            start = pl.multiple_of(b * joint * capacity + at, 16)
            for k in range(0, step, 16):
                rows = [
                    wide[pl.ds(wanted_ref[first + at + n + n // capacity * LINE], 1), :]
                    for n in range(k, k + 16)
                ]
                out[pl.ds(start + k, 16), :] = jnp.concatenate(rows, axis=0).astype(BF16)
            return carry

        steps = 1 if joint > 1 else lax.div(wanted_ref[first + capacity] + step - 1, step)
        return lax.fori_loop(0, steps, fetch, carry)

    copies = []
    groups = sems.shape[0]
    each = blocks // joint // groups
    for g in range(groups):
        lax.fori_loop(g * each, (g + 1) * each, bucket, 0)
        part = pl.ds(g * each * joint * capacity, each * joint * capacity)
        copies.append(pltpu.make_async_copy(out.at[part], out_hbm.at[part], sems.at[g]))
        copies[-1].start()
    for copy in copies:
        copy.wait()


def gather(wanted, table, blocks):
    width = table.shape[1]
    slots = wanted.shape[0] - blocks * LINE
    return pl.pallas_call(
        functools.partial(gather_kernel, blocks),
        out_shape=pltpu.HBM((slots, width), BF16),
        in_specs=[
            pl.BlockSpec(memory_space=pltpu.SMEM),
            pl.BlockSpec(memory_space=pltpu.HBM),
        ],
        out_specs=pl.BlockSpec(memory_space=pltpu.HBM),
        scratch_shapes=[
            pltpu.VMEM(table.shape, BF16),
            pltpu.VMEM(table.shape, F32),
            pltpu.VMEM((slots, width), BF16),
            pltpu.SemaphoreType.DMA((8,)),
            pltpu.SemaphoreType.DMA((4,)),
        ],
        compiler_params=pltpu.CompilerParams(vmem_limit_bytes=VMEM_LIMIT),
        cost_estimate=cost(slots * width, 0),
        name="gather_rows",
    )(wanted, pltpu.with_memory_space_constraint(table, pltpu.HBM))


def spread_kernel(own_ref, other_ref, out_ref):
    part = (own_ref[...].astype(F32) + other_ref[...].astype(F32)).astype(BF16)
    for k in range(out_ref.shape[0]):
        out_ref[k] = part


def spread(own, other, copies):
    vmem = pl.BlockSpec(memory_space=pltpu.VMEM)
    return pl.pallas_call(
        spread_kernel,
        out_shape=pltpu.VMEM((copies,) + own.shape, BF16),
        in_specs=[vmem, vmem],
        out_specs=vmem,
        compiler_params=pltpu.CompilerParams(vmem_limit_bytes=VMEM_LIMIT),
        cost_estimate=cost(own.size, 0),
        name="spread",
    )(own, other)


def scatter_kernel(wanted_ref, returned_ref, out_ref, grads):
    tile = out_ref.shape[0]
    slots = grads.shape[0]
    blocks = returned_ref.shape[0]
    each = slots // blocks
    block = 256

    @pl.when(pl.program_id(0) == 0)
    def _():
        for b in range(blocks):
            grads[b * each : (b + 1) * each, :] = returned_ref[b, :each, :]

    row = lax.broadcasted_iota(jnp.int32, (tile, block), 0) + pl.program_id(0) * tile
    total = jnp.zeros(out_ref.shape, F32)
    for start in range(0, slots, block):
        hot = (row == wanted_ref[:, start : start + block]).astype(F32).astype(BF16)
        total = total + nn(hot, grads[start : start + block, :])
    out_ref[...] = total.astype(BF16)


def scatter(wanted, returned, rows_dev):
    slots = wanted.shape[1]
    width = returned.shape[-1]
    tile = 512
    return pl.pallas_call(
        scatter_kernel,
        grid=(rows_dev // tile,),
        out_shape=jax.ShapeDtypeStruct((rows_dev, width), BF16),
        in_specs=[
            pl.BlockSpec((1, slots), lambda t: (0, 0)),
            pl.BlockSpec(returned.shape, lambda t: (0, 0, 0)),
        ],
        out_specs=pl.BlockSpec((tile, width), lambda t: (t, 0)),
        scratch_shapes=[pltpu.VMEM((slots, width), BF16)],
        compiler_params=pltpu.CompilerParams(vmem_limit_bytes=VMEM_LIMIT),
        cost_estimate=cost(2 * rows_dev * slots * width, 0),
        name="scatter_rows",
    )(wanted, returned)


def by_head(x):
    head_size = x.shape[1] // HEADS
    head = lax.broadcasted_iota(jnp.int32, x.shape, 1) // head_size
    return jnp.concatenate([jnp.where(head == h, x, 0.0) for h in range(HEADS)], axis=0)


def head_blocks(a_t, b, live):
    size = a_t.shape[0] // HEADS
    return jnp.concatenate(
        [nn(a_t[h * size : (h + 1) * size, :], b[:, h * live : (h + 1) * live]) for h in range(HEADS)],
        axis=0,
    )


def pieces(x):
    a = x.astype(BF16)
    x = x - a.astype(F32)
    b = x.astype(BF16)
    return [a, b, (x - b.astype(F32)).astype(BF16)]


def stacked(x, live):
    return jnp.concatenate([x[:, h * live : (h + 1) * live] for h in range(HEADS)], axis=0)


def flat(x):
    return jnp.concatenate([x[h : h + 1, :] for h in range(HEADS)], axis=1)


def query_kernel(cands_ref, wq_ref, wk_ref, query_ref, query_w_ref):
    width = wq_ref.shape[0]
    live = cands_ref.shape[1]
    scale = float(width // HEADS) ** (-0.5)
    cands = jnp.concatenate([cands_ref[r, :, :width] for r in range(2)], axis=0)
    query = nn(cands, wq_ref[...]).astype(BF16).astype(F32) * scale
    for r in range(2):
        heads = by_head(query[r * live : (r + 1) * live]).astype(BF16)
        query_ref[r] = heads
        query_w_ref[r] = nt(heads, wk_ref[...]).astype(BF16)


def queries(cands, w_query, w_key):
    width = w_query.shape[0]
    shape = jax.ShapeDtypeStruct((2, HEADS * cands.shape[1], width), BF16)
    vmem = pl.BlockSpec(memory_space=pltpu.VMEM)
    return pl.pallas_call(
        query_kernel,
        out_shape=(shape, shape),
        in_specs=[vmem] * 3,
        out_specs=(vmem, vmem),
        compiler_params=pltpu.CompilerParams(vmem_limit_bytes=VMEM_LIMIT),
        cost_estimate=cost(2**24, 0),
        name="queries",
    )(cands, w_query, w_key)


def take_tile(rows_ref, r, t, per_tile, capacity):
    return jnp.concatenate(
        [
            rows_ref[b, r * capacity : (r + 1) * capacity, :]
            for b in range(t * per_tile, (t + 1) * per_tile)
        ],
        axis=0,
    )


TILE = 768


def forward_kernel(
    r, num, rows_ref, flags_ref, query_w_ref, wv_ref, expo_ref, part_ref, mean_ref, turned_ref, scores
):
    blocks, both, width = rows_ref.shape
    capacity = both // 2
    cols = query_w_ref.shape[1]
    live = cols // HEADS
    per_tile = TILE // capacity
    tiles = blocks // per_tile
    user_of = lax.rem(lax.broadcasted_iota(jnp.int32, (1, cols), 1), live) // num + 1
    user_of = user_of.astype(F32)
    query_w = query_w_ref[r]
    flags = flags_ref[r].astype(F32).T
    top = jnp.full((1, cols), LOWEST, F32)
    for t in range(tiles):
        rows = take_tile(rows_ref, r, t, per_tile, capacity)
        turned_ref[:, t * TILE : (t + 1) * TILE] = rows.T
        flag = jnp.concatenate(
            [flags[:capacity, o : o + 1] for o in range(t * per_tile, (t + 1) * per_tile)], axis=0
        )
        score = jnp.where(flag == user_of, nt(rows, query_w), LOWEST)
        scores[t * TILE : (t + 1) * TILE, :] = score
        top = jnp.maximum(top, jnp.max(score, axis=0, keepdims=True))
    norm = jnp.zeros((1, cols), F32)
    rows_e = jnp.zeros((width, cols), F32)
    for t in range(tiles):
        e = jnp.exp(scores[t * TILE : (t + 1) * TILE, :] - top)
        norm = norm + jnp.sum(e, axis=0, keepdims=True)
        e = e.astype(BF16)
        expo_ref[t * TILE : (t + 1) * TILE, :] = e
        rows_e = rows_e + nn(turned_ref[:, t * TILE : (t + 1) * TILE], e)
    mean = (rows_e * (1.0 / norm)).astype(BF16)
    mean_ref[...] = mean
    part_ref[:width, :] = head_blocks(wv_ref[...].T, mean, live).astype(BF16)
    rest = pieces(stacked(top, live)) + pieces(stacked(norm, live))
    rest.append(jnp.zeros((8, live), BF16))
    part_ref[width:, :] = jnp.concatenate([x.astype(F32) for x in rest], axis=0).astype(BF16)


def forward(r, rows, flags, query_w, num, w_value):
    blocks, both, width = rows.shape
    cols = query_w.shape[1]
    slots = blocks * both // 2
    vmem = pl.BlockSpec(memory_space=pltpu.VMEM)
    return pl.pallas_call(
        functools.partial(forward_kernel, r, num),
        out_shape=(
            jax.ShapeDtypeStruct((slots, cols), BF16),
            jax.ShapeDtypeStruct((width + 32, cols // HEADS), BF16),
            jax.ShapeDtypeStruct((width, cols), BF16),
            jax.ShapeDtypeStruct((width, slots), BF16),
        ),
        in_specs=[vmem] * 4,
        out_specs=(vmem,) * 4,
        scratch_shapes=[pltpu.VMEM((slots, cols), F32)],
        compiler_params=pltpu.CompilerParams(vmem_limit_bytes=VMEM_LIMIT),
        cost_estimate=cost(4 * slots * width * cols, slots * cols),
        name="forward",
    )(rows, flags, query_w, w_value)


def opened(part_ref, width):
    rest = part_ref[width:, :].astype(F32)
    top = rest[0:4] + rest[4:8] + rest[8:12]
    norm = rest[12:16] + rest[16:20] + rest[20:24]
    return part_ref[:width, :].astype(F32), top, norm


def backward_kernel(
    r,
    users,
    rows_ref,
    flags_ref,
    cands_ref,
    place_ref,
    query_ref,
    query_w_ref,
    wk_ref,
    wv_ref,
    wo_ref,
    expo_ref,
    own_ref,
    other_ref,
    mean_ref,
    turned_ref,
    *refs,
):
    if r == 0:
        out_ref, weights = refs
    else:
        first_ref, first_weights, out_ref, weights = refs
    blocks, both, width = rows_ref.shape
    capacity = both // 2
    live = cands_ref.shape[1]
    num = live // users
    cols = HEADS * live
    head_size = width // HEADS
    scale = float(head_size) ** (-0.5)
    root = float(width) ** 0.5
    per_tile = TILE // capacity
    tiles = blocks // per_tile
    wv, wo = wv_ref[...], wo_ref[...]

    mixed_own, top_own, norm_own = opened(own_ref, width)
    mixed_other, top_other, norm_other = opened(other_ref, width)
    top = jnp.maximum(top_own, top_other)
    factor = jnp.exp(top_own - top)
    part_own = norm_own * factor
    part_other = norm_other * jnp.exp(top_other - top)
    inv = 1.0 / (part_own + part_other)
    factor = factor * inv
    part_own = part_own * inv
    part_other = part_other * inv
    mixed_t = jnp.concatenate(
        [
            mixed_own[h * head_size : (h + 1) * head_size] * part_own[h : h + 1]
            + mixed_other[h * head_size : (h + 1) * head_size] * part_other[h : h + 1]
            for h in range(HEADS)
        ],
        axis=0,
    )
    mixed_tb = mixed_t.astype(BF16)
    cands = cands_ref[r, :, :width]
    cand_f = cands.astype(F32)
    proj = nn(mixed_tb.T, wo)
    logit = jnp.sum(proj * cand_f, axis=1, keepdims=True) / root
    label = cands_ref[r, :, width:].astype(F32)[:, 0:1]
    index = lax.broadcasted_iota(jnp.int32, (live, 1), 0)
    limit = jnp.zeros((live, 1), F32)
    for user in range(users):
        count = flags_ref[r, 0:1, capacity + user : capacity + user + 1].astype(F32)
        limit = jnp.where(index >= user * num, count, limit)
    alive = place_ref[...] < limit
    grad_logit = jnp.where(alive, (jax.nn.sigmoid(logit) - label) / USERS_DEV, 0.0)
    grad_proj = (grad_logit * cand_f / root).astype(BF16)
    grad_mixed = nt(grad_proj, wo).astype(BF16).astype(F32)
    joint = grad_mixed.T * mixed_t
    inner = jnp.concatenate(
        [
            jnp.sum(joint[h * head_size : (h + 1) * head_size, :], axis=0, keepdims=True)
            for h in range(HEADS)
        ],
        axis=0,
    )
    inner = flat(inner * factor)
    factor = flat(factor)
    factor_col = jnp.broadcast_to(factor, (128, cols)).T[:, :1]
    grad_heads = by_head(grad_mixed)
    grad_w = nt((grad_heads * factor_col).astype(BF16), wv).astype(BF16)

    both_w = jnp.concatenate([query_w_ref[r], grad_w], axis=0)
    rows_s = jnp.zeros((width, cols), F32)
    for t in range(tiles):
        rows = take_tile(rows_ref, r, t, per_tile, capacity)
        e = expo_ref[t * TILE : (t + 1) * TILE, :]
        grad_score = (e.astype(F32) * (nt(rows, grad_w) - inner)).astype(BF16)
        rows_s = rows_s + nn(turned_ref[:, t * TILE : (t + 1) * TILE], grad_score)
        grad_rows = nn(jnp.concatenate([grad_score, e], axis=1), both_w).astype(BF16)
        for k in range(per_tile):
            out_ref[t * per_tile + k, r * capacity : (r + 1) * capacity, :] = grad_rows[
                k * capacity : (k + 1) * capacity, :
            ]

    rows_s = rows_s.astype(BF16)
    grad_query_t = (head_blocks(wk_ref[...].T, rows_s, live) * scale).astype(BF16)
    share = flat(part_own)
    parts = (
        nt(cands.T, grad_query_t),
        nn(rows_s, query_ref[r]),
        nn((mean_ref[...].astype(F32) * share).astype(BF16), grad_heads.astype(BF16)),
        nn(mixed_tb, grad_proj) * 0.5,
    )
    for k, part in enumerate(parts):
        if r == 0:
            weights[k * width : (k + 1) * width, :] = part
        else:
            weights[k * width : (k + 1) * width, :] = (
                first_weights[k * width : (k + 1) * width, :] + part
            )
    if r == 1:
        rows_each = 4 * width // blocks
        for b in range(blocks):
            out_ref[b, :capacity, :] = first_ref[b]
            out_ref[b, both:, :] = weights[b * rows_each : (b + 1) * rows_each, :].astype(BF16)


def backward(r, users, rows, *operands):
    blocks, both, width = rows.shape
    vmem = pl.BlockSpec(memory_space=pltpu.VMEM)
    weights = jax.ShapeDtypeStruct((4 * width, width), F32)
    if r == 0:
        out_shape = (jax.ShapeDtypeStruct((blocks, both // 2, width), BF16), weights)
        scratch_shapes = []
    else:
        out_shape = jax.ShapeDtypeStruct((blocks, both + 4 * width // blocks, width), BF16)
        scratch_shapes = [pltpu.VMEM(weights.shape, F32)]
    return pl.pallas_call(
        functools.partial(backward_kernel, r, users),
        out_shape=out_shape,
        in_specs=[vmem] * (1 + len(operands)),
        out_specs=(vmem, vmem) if r == 0 else vmem,
        scratch_shapes=scratch_shapes,
        compiler_params=pltpu.CompilerParams(vmem_limit_bytes=VMEM_LIMIT),
        cost_estimate=cost(6 * blocks * both * width * width * HEADS, 0),
        name="backward",
    )(rows, *operands)


def exchange(x, axes):
    return lax.all_to_all(x, axes, split_axis=0, concat_axis=0, tiled=True)


def swap_halves(x):
    return lax.ppermute(x, "hi", [(0, 1), (1, 0)])


def swap(x):
    peers = lax.axis_size(PEERS)
    return lax.ppermute(x, PEERS, [(i, peers - 1 - i) for i in range(peers)])


def pair_candidates(mine, users, flags):
    peers = lax.axis_size(PEERS)
    peer = lax.axis_index(PEERS)
    first = lax.axis_index("hi") == 0
    _, held, wide = mine.shape
    mine = mine.reshape(peers, users, held, wide)
    got = []
    for k in range(peers):
        to = peer ^ k
        lower = jnp.minimum(to, peers - 1 - to)
        piece = jnp.stack(
            [
                lax.dynamic_index_in_dim(mine, lower, 0, keepdims=False),
                lax.dynamic_index_in_dim(mine, peers - 1 - lower, 0, keepdims=False),
            ]
        )
        if k == peers - 1:
            piece = jnp.concatenate(
                [piece.reshape(-1, wide), jnp.pad(flags, ((0, 0), (0, wide - flags.shape[1])))], axis=0
            )
        if k > 0:
            piece = lax.ppermute(piece, PEERS, [(i, i ^ k) for i in range(peers)])
        got.append(piece)
    lines = 2 * users * held
    flags = got[-1][lines:, : flags.shape[1]]
    got[-1] = got[-1][:lines].reshape(got[0].shape)
    cands = jnp.concatenate(
        [jnp.where(first, got[k], got[peers - 1 - k]) for k in range(peers)], axis=2
    )
    return cands.reshape(2, -1, wide), flags


def local(
    table, behaviour_ids, lengths, candidates, labels, cand_counts, w_query, w_key, w_value, w_out
):
    shards = lax.axis_size(ALL)
    half = shards // 2
    sizes = (lax.axis_size("group"), lax.axis_size("lo"))
    first = lax.axis_index("hi") == 0
    users, seq = behaviour_ids.shape
    rows_dev, width = table.shape
    total = users * seq
    capacity = total // shards + total // (2 * shards)
    slots = shards * capacity
    num = candidates.shape[1] * lax.axis_size("hi") * lax.axis_size("lo")

    requests, flags, mine = plan(
        behaviour_ids, lengths, cand_counts, candidates, labels, rows_dev, sizes, capacity
    )
    wanted = exchange(requests, BY_HALF)
    flags = flags.reshape(2, half, -1)
    flags_kept = jnp.where(first, flags[0], flags[1])
    cands, swapped = pair_candidates(mine, users, jnp.where(first, flags[1], flags[0]))

    wanted = wanted.reshape(2, sizes[0], sizes[1], capacity + LINE)
    lower = jnp.where(first, wanted[0], wanted[0, :, ::-1])
    upper = jnp.where(first, wanted[1, :, ::-1], wanted[1])
    wanted = jnp.stack([lower, upper], axis=2).reshape(shards, capacity + LINE)
    served = gather(wanted.reshape(-1), table, shards)
    wanted = wanted[:, :capacity]
    served, cands, swapped = lax.optimization_barrier((served, cands, swapped))
    rows = exchange(served.reshape(half, 2 * capacity, width), HALF)
    flags = jnp.stack(
        [jnp.where(first, flags_kept, swapped), jnp.where(first, swapped, flags_kept)]
    )
    query, query_w = queries(cands, w_query, w_key)
    peers, held = lax.axis_size(PEERS), candidates.shape[1]
    peer = lax.axis_index(PEERS)
    place = jnp.minimum(peer, peers - 1 - peer) ^ jnp.arange(peers, dtype=jnp.int32)
    place = place[:, None] * held + jnp.arange(held, dtype=jnp.int32)[None]
    place = jnp.broadcast_to(place.astype(F32).reshape(1, num), (users, num)).reshape(users * num, 1)

    ahead = [forward(r, rows, flags, query_w, num, w_value) for r in range(2)]
    back = []
    for r, (expo, own, mean, turned) in enumerate(ahead):
        back = backward(
            r,
            users,
            rows,
            flags,
            cands,
            place,
            query,
            query_w,
            w_key,
            w_value,
            w_out,
            expo,
            own,
            swap(own),
            mean,
            turned,
            *back,
        )
    outgoing = back
    returned = exchange(outgoing, HALF)
    table_grad = scatter(wanted.reshape(1, slots), returned, rows_dev)

    part = jnp.sum(returned[:, 2 * capacity :, :].astype(F32), axis=0).astype(BF16)
    weight_grads = exchange(spread(part, swap_halves(part), half), HALF)
    return table_grad, weight_grads.reshape(4, width, width).astype(F32)


def solution(mesh):
    groups, peers = mesh.shape["group"], mesh.shape["peer"]
    mesh = Mesh(mesh.devices.reshape(groups, 2, peers // 2), ALL)
    in_specs = (
        P(ALL, None),
        P(ALL, None),
        P(ALL),
        P("group", ("hi", "lo"), None),
        P("group", ("hi", "lo")),
        P(ALL),
        P(),
        P(),
        P(),
        P(),
    )
    out_specs = (P(ALL, None), P())
    return jax.shard_map(local, mesh=mesh, in_specs=in_specs, out_specs=out_specs, check_vma=False)
```

```python
import functools
import math

import jax
import jax.numpy as jnp
from jax import lax
from jax.experimental import pallas as pl
from jax.experimental.pallas import tpu as pltpu
from jax.sharding import Mesh
from jax.sharding import PartitionSpec as P

HEADS = 4
USERS_DEV = 2
ALL = ("group", "hi", "lo")
BY_HALF = ("hi", "group", "lo")
HALF = ("group", "lo")
PEERS = ("hi", "lo")
BF16 = jnp.bfloat16
F32 = jnp.float32
VMEM_LIMIT = 12 * 1024 * 1024
LOWEST = -1e30
LINE = 8


def nt(a, b):
    return lax.dot_general(a, b, (((1,), (1,)), ((), ())), preferred_element_type=F32)


def nn(a, b):
    return jnp.dot(a, b, preferred_element_type=F32)


def cost(flops, transcendentals):
    return pl.CostEstimate(flops=flops, bytes_accessed=0, transcendentals=transcendentals)


def log2(n):
    return n.bit_length() - 1


def plan_kernel(
    rows_dev,
    sizes,
    lengths_hbm,
    counts_hbm,
    ids_hbm,
    cands_hbm,
    labels_hbm,
    requests_ref,
    flags_ref,
    labelled_ref,
    lengths_ref,
    counts_ref,
    ids_ref,
    cands_ref,
    labels_ref,
    sems,
):
    copies = [
        pltpu.make_async_copy(source, target, sems.at[k])
        for k, (source, target) in enumerate(
            (
                (lengths_hbm, lengths_ref),
                (counts_hbm, counts_ref),
                (ids_hbm, ids_ref),
                (cands_hbm, cands_ref),
                (labels_hbm, labels_ref),
            )
        )
    ]
    for copy in copies:
        copy.start()
    for copy in copies:
        copy.wait()
    groups, low = sizes
    users, seq = ids_ref.shape
    shards = requests_ref.shape[0]
    capacity = requests_ref.shape[1] - LINE
    half = shards // 2
    block = 256
    before = (
        lax.broadcasted_iota(jnp.int32, (block, block), 0)
        < lax.broadcasted_iota(jnp.int32, (block, block), 1)
    ).astype(BF16)
    device = lax.broadcasted_iota(jnp.int32, (shards, block), 0)
    place = lax.broadcasted_iota(jnp.int32, (capacity, block), 0).astype(F32)
    lane = lax.broadcasted_iota(jnp.int32, (1, block), 1)
    count = jnp.zeros((shards, 1), F32)
    rows = jnp.zeros((3 * shards, capacity), F32)
    for user in range(users):
        for start in range(0, seq, block):
            ids = ids_ref[user : user + 1, start : start + block]
            owner = lax.shift_right_logical(ids, log2(rows_dev))
            row = ids & (rows_dev - 1)
            group = lax.shift_right_logical(owner, log2(2 * low))
            high = lax.shift_right_logical(owner, log2(low)) & 1
            owner = high * half + group * low + (owner & (low - 1))
            live = lane + start < lengths_ref[user]
            owner = jnp.where(live, owner, shards)
            hot = (device == owner).astype(F32)
            hot_b = hot.astype(BF16)
            earlier = nn(hot_b, before) + count
            count = count + jnp.sum(hot, axis=1, keepdims=True)
            rank = jnp.sum(hot * earlier, axis=0, keepdims=True)
            ranked = (place == rank).astype(F32).astype(BF16)
            upper = lax.shift_right_logical(row, 6).astype(F32)
            lower = (row & 63).astype(F32)
            parts = jnp.concatenate([hot * upper, hot * lower, hot * float(user + 1)], axis=0)
            rows = rows + nt(parts.astype(BF16), ranked)
    requests = jnp.concatenate(
        [rows[:shards] * 64.0 + rows[shards : 2 * shards], jnp.broadcast_to(count, (shards, LINE))],
        axis=1,
    )
    requests_ref[...] = requests.astype(jnp.int32)
    lane = lax.broadcasted_iota(jnp.int32, (shards, 128 - capacity), 1)
    rest = jnp.zeros(lane.shape, F32)
    for user in range(users):
        rest = jnp.where(lane == user, counts_ref[user].astype(F32), rest)
    flags_ref[...] = jnp.concatenate([rows[2 * shards :], rest], axis=1).astype(BF16)
    _, held, width = cands_ref.shape
    square = lax.broadcasted_iota(jnp.int32, (held, held), 0)
    square = square == lax.broadcasted_iota(jnp.int32, (held, held), 1)
    lane = lax.broadcasted_iota(jnp.int32, (held, 128), 1)
    for user in range(cands_ref.shape[0]):
        label = jnp.sum(
            jnp.where(square, labels_ref[user : user + 1, :], 0.0), axis=1, keepdims=True
        )
        labelled_ref[user, :, :width] = cands_ref[user]
        labelled_ref[user, :, width:] = jnp.where(lane == 0, label, 0.0).astype(BF16)


def plan(behaviour_ids, lengths, cand_counts, candidates, labels, rows_dev, sizes, capacity):
    half = sizes[0] * sizes[1]
    vmem = pl.BlockSpec(memory_space=pltpu.VMEM)
    operands = (lengths, cand_counts, behaviour_ids, candidates, labels)
    return pl.pallas_call(
        functools.partial(plan_kernel, rows_dev, sizes),
        out_shape=(
            jax.ShapeDtypeStruct((2 * half, capacity + LINE), jnp.int32),
            jax.ShapeDtypeStruct((2 * half, 128), BF16),
            jax.ShapeDtypeStruct(candidates.shape[:2] + (candidates.shape[2] + 128,), BF16),
        ),
        in_specs=[pl.BlockSpec(memory_space=pltpu.HBM)] * 5,
        out_specs=(vmem,) * 3,
        scratch_shapes=[
            pltpu.SMEM(lengths.shape, jnp.int32),
            pltpu.SMEM(cand_counts.shape, jnp.int32),
            pltpu.VMEM(behaviour_ids.shape, jnp.int32),
            pltpu.VMEM(candidates.shape, BF16),
            pltpu.VMEM(labels.shape, F32),
            pltpu.SemaphoreType.DMA((5,)),
        ],
        compiler_params=pltpu.CompilerParams(vmem_limit_bytes=VMEM_LIMIT),
        cost_estimate=cost(2**24, 0),
        name="plan",
    )(*(pltpu.with_memory_space_constraint(x, pltpu.HBM) for x in operands))


def gather_kernel(blocks, wanted_ref, table_hbm, out, narrow, wide, in_sems):
    slots = out.shape[0]
    capacity = slots // blocks
    line = capacity + LINE
    joint = 1 if capacity % 32 == 0 else math.lcm(capacity, 16) // capacity
    step = 32 if joint == 1 else joint * capacity
    halves, _, lanes = wide.shape
    loads = in_sems.shape[0]
    size = narrow.shape[0] // loads
    copies = []
    for k in range(loads):
        part = pl.ds(k * size, size)
        copies.append(pltpu.make_async_copy(table_hbm.at[part], narrow.at[part], in_sems.at[k]))
        copies[-1].start()
    out[...] = jnp.zeros(out.shape, BF16)
    for k, copy in enumerate(copies):
        copy.wait()
        part = slice(k * size, (k + 1) * size)
        for h in range(halves):
            wide[h, part, :] = narrow[part, h * lanes : (h + 1) * lanes].astype(F32)

    def bucket(b, carry):
        first = b * joint * line

        def fetch(c, carry):
            at = c * step
            start = pl.multiple_of(b * joint * capacity + at, 16)
            for k in range(0, step, 16):
                ids = [wanted_ref[first + at + n + n // capacity * LINE] for n in range(k, k + 16)]
                for h in range(halves):
                    rows = [wide[h, pl.ds(row, 1), :] for row in ids]
                    out[pl.ds(start + k, 16), h * lanes : (h + 1) * lanes] = jnp.concatenate(
                        rows, axis=0
                    ).astype(BF16)
            return carry

        steps = 1 if joint > 1 else lax.div(wanted_ref[first + capacity] + step - 1, step)
        return lax.fori_loop(0, steps, fetch, carry)

    lax.fori_loop(0, blocks // joint, bucket, 0)


def gather(wanted, table, blocks):
    width = table.shape[1]
    slots = wanted.shape[0] - blocks * LINE
    return pl.pallas_call(
        functools.partial(gather_kernel, blocks),
        out_shape=jax.ShapeDtypeStruct((slots, width), BF16),
        in_specs=[
            pl.BlockSpec(memory_space=pltpu.SMEM),
            pl.BlockSpec(memory_space=pltpu.HBM),
        ],
        out_specs=pl.BlockSpec(memory_space=pltpu.VMEM),
        scratch_shapes=[
            pltpu.VMEM(table.shape, BF16),
            pltpu.VMEM((width // 128, table.shape[0], 128), F32),
            pltpu.SemaphoreType.DMA((8,)),
        ],
        compiler_params=pltpu.CompilerParams(vmem_limit_bytes=VMEM_LIMIT),
        cost_estimate=cost(slots * width, 0),
        name="gather_rows",
    )(wanted, pltpu.with_memory_space_constraint(table, pltpu.HBM))


def spread_kernel(own_ref, other_ref, out_ref):
    part = (own_ref[...].astype(F32) + other_ref[...].astype(F32)).astype(BF16)
    for k in range(out_ref.shape[0]):
        out_ref[k] = part


def spread(own, other, copies):
    vmem = pl.BlockSpec(memory_space=pltpu.VMEM)
    return pl.pallas_call(
        spread_kernel,
        out_shape=pltpu.VMEM((copies,) + own.shape, BF16),
        in_specs=[vmem, vmem],
        out_specs=vmem,
        compiler_params=pltpu.CompilerParams(vmem_limit_bytes=VMEM_LIMIT),
        cost_estimate=cost(own.size, 0),
        name="spread",
    )(own, other)


def scatter_kernel(wanted_ref, returned_ref, out_ref, grads):
    tile = out_ref.shape[0]
    slots = grads.shape[0]
    blocks = returned_ref.shape[0]
    each = slots // blocks
    block = 256

    @pl.when(pl.program_id(0) == 0)
    def _():
        for b in range(blocks):
            grads[b * each : (b + 1) * each, :] = returned_ref[b, :each, :]

    row = lax.broadcasted_iota(jnp.int32, (tile, block), 0) + pl.program_id(0) * tile
    total = jnp.zeros(out_ref.shape, F32)
    for start in range(0, slots, block):
        hot = (row == wanted_ref[:, start : start + block]).astype(F32).astype(BF16)
        total = total + nn(hot, grads[start : start + block, :])
    out_ref[...] = total.astype(BF16)


def scatter(wanted, returned, rows_dev):
    slots = wanted.shape[1]
    width = returned.shape[-1]
    tile = 1024
    return pl.pallas_call(
        scatter_kernel,
        grid=(rows_dev // tile,),
        out_shape=jax.ShapeDtypeStruct((rows_dev, width), BF16),
        in_specs=[
            pl.BlockSpec((1, slots), lambda t: (0, 0)),
            pl.BlockSpec(returned.shape, lambda t: (0, 0, 0)),
        ],
        out_specs=pl.BlockSpec((tile, width), lambda t: (t, 0)),
        scratch_shapes=[pltpu.VMEM((slots, width), BF16)],
        compiler_params=pltpu.CompilerParams(vmem_limit_bytes=VMEM_LIMIT),
        cost_estimate=cost(2 * rows_dev * slots * width, 0),
        name="scatter_rows",
    )(wanted, returned)


def by_head(x):
    head_size = x.shape[1] // HEADS
    head = lax.broadcasted_iota(jnp.int32, x.shape, 1) // head_size
    return jnp.concatenate([jnp.where(head == h, x, 0.0) for h in range(HEADS)], axis=0)


def head_blocks(a_t, b, live):
    size = a_t.shape[0] // HEADS
    return jnp.concatenate(
        [nn(a_t[h * size : (h + 1) * size, :], b[:, h * live : (h + 1) * live]) for h in range(HEADS)],
        axis=0,
    )


def pieces(x):
    a = x.astype(BF16)
    x = x - a.astype(F32)
    b = x.astype(BF16)
    return [a, b, (x - b.astype(F32)).astype(BF16)]


def stacked(x, live):
    return jnp.concatenate([x[:, h * live : (h + 1) * live] for h in range(HEADS)], axis=0)


def flat(x):
    return jnp.concatenate([x[h : h + 1, :] for h in range(HEADS)], axis=1)


def take_tile(rows_ref, r, t, per_tile, capacity):
    return jnp.concatenate(
        [
            rows_ref[b, r * capacity : (r + 1) * capacity, :]
            for b in range(t * per_tile, (t + 1) * per_tile)
        ],
        axis=0,
    )


TILE = 768
FORWARD_TILE = 256


def forward_kernel(
    r,
    num,
    rows_ref,
    flags_ref,
    cands_ref,
    wq_ref,
    wk_ref,
    wv_ref,
    expo_ref,
    part_ref,
    mean_ref,
    turned_ref,
    query_ref,
    query_w_ref,
    scores,
    mine,
):
    blocks, both, width = rows_ref.shape
    capacity = both // 2
    live = cands_ref.shape[1]
    cols = HEADS * live
    tiles = blocks * capacity // FORWARD_TILE
    for b in range(blocks):
        mine[b * capacity : (b + 1) * capacity, :] = rows_ref[b, r * capacity : (r + 1) * capacity, :]
    user_of = lax.rem(lax.broadcasted_iota(jnp.int32, (1, cols), 1), live) // num + 1
    user_of = user_of.astype(F32)
    scale = float(width // HEADS) ** (-0.5)
    query = nn(cands_ref[r, :, :width], wq_ref[...]).astype(BF16).astype(F32) * scale
    query = by_head(query).astype(BF16)
    query_w = nt(query, wk_ref[...]).astype(BF16)
    query_ref[...] = query
    query_w_ref[...] = query_w
    flags = flags_ref[r].astype(F32).T
    top = jnp.full((1, cols), LOWEST, F32)
    flags = jnp.concatenate([flags[:capacity, o : o + 1] for o in range(blocks)], axis=0)
    for t in range(tiles):
        part = slice(t * FORWARD_TILE, (t + 1) * FORWARD_TILE)
        rows = mine[part, :]
        turned_ref[:, part] = rows.T
        score = jnp.where(flags[part] == user_of, nt(rows, query_w), LOWEST)
        scores[part, :] = score
        top = jnp.maximum(top, jnp.max(score, axis=0, keepdims=True))
    norm = jnp.zeros((1, cols), F32)
    rows_e = jnp.zeros((width, cols), F32)
    for t in range(tiles):
        part = slice(t * FORWARD_TILE, (t + 1) * FORWARD_TILE)
        e = jnp.exp(scores[part, :] - top)
        norm = norm + jnp.sum(e, axis=0, keepdims=True)
        e = e.astype(BF16)
        expo_ref[part, :] = e
        rows_e = rows_e + nn(turned_ref[:, part], e)
    mean = (rows_e * (1.0 / norm)).astype(BF16)
    mean_ref[...] = mean
    part_ref[:width, :] = head_blocks(wv_ref[...].T, mean, live).astype(BF16)
    rest = pieces(stacked(top, live)) + pieces(stacked(norm, live))
    rest.append(jnp.zeros((8, live), BF16))
    part_ref[width:, :] = jnp.concatenate([x.astype(F32) for x in rest], axis=0).astype(BF16)


def forward(r, rows, flags, cands, num, w_query, w_key, w_value):
    blocks, both, width = rows.shape
    live = cands.shape[1]
    cols = HEADS * live
    slots = blocks * both // 2
    vmem = pl.BlockSpec(memory_space=pltpu.VMEM)
    shapes = (
        (slots, cols),
        (width + 32, live),
        (width, cols),
        (width, slots),
        (cols, width),
        (cols, width),
    )
    return pl.pallas_call(
        functools.partial(forward_kernel, r, num),
        out_shape=tuple(jax.ShapeDtypeStruct(shape, BF16) for shape in shapes),
        in_specs=[vmem] * 6,
        out_specs=(vmem,) * len(shapes),
        scratch_shapes=[pltpu.VMEM((slots, cols), F32), pltpu.VMEM((slots, width), BF16)],
        compiler_params=pltpu.CompilerParams(vmem_limit_bytes=VMEM_LIMIT),
        cost_estimate=cost(4 * slots * width * cols, slots * cols),
        name="forward",
    )(rows, flags, cands, w_query, w_key, w_value)


def opened(part_ref, width):
    rest = part_ref[width:, :].astype(F32)
    top = rest[0:4] + rest[4:8] + rest[8:12]
    norm = rest[12:16] + rest[16:20] + rest[20:24]
    return part_ref[:width, :].astype(F32), top, norm


def backward_kernel(
    r,
    users,
    low,
    rows_ref,
    flags_ref,
    cands_ref,
    wk_ref,
    wv_ref,
    wo_ref,
    other_ref,
    expo_ref,
    own_ref,
    mean_ref,
    turned_ref,
    query_ref,
    query_w_ref,
    *refs,
):
    if r == 0:
        out_ref, weights = refs
    else:
        first_ref, first_weights, out_ref, weights = refs
    blocks, both, width = rows_ref.shape
    capacity = both // 2
    live = cands_ref.shape[1]
    num = live // users
    cols = HEADS * live
    head_size = width // HEADS
    scale = float(head_size) ** (-0.5)
    root = float(width) ** 0.5
    per_tile = TILE // capacity
    tiles = blocks // per_tile
    wv, wo = wv_ref[...], wo_ref[...]

    mixed_own, top_own, norm_own = opened(own_ref, width)
    mixed_other, top_other, norm_other = opened(other_ref, width)
    top = jnp.maximum(top_own, top_other)
    factor = jnp.exp(top_own - top)
    part_own = norm_own * factor
    part_other = norm_other * jnp.exp(top_other - top)
    inv = 1.0 / (part_own + part_other)
    factor = factor * inv
    part_own = part_own * inv
    part_other = part_other * inv
    mixed_t = jnp.concatenate(
        [
            mixed_own[h * head_size : (h + 1) * head_size] * part_own[h : h + 1]
            + mixed_other[h * head_size : (h + 1) * head_size] * part_other[h : h + 1]
            for h in range(HEADS)
        ],
        axis=0,
    )
    mixed_tb = mixed_t.astype(BF16)
    cands = cands_ref[r, :, :width]
    cand_f = cands.astype(F32)
    proj = nn(mixed_tb.T, wo)
    logit = jnp.sum(proj * cand_f, axis=1, keepdims=True) / root
    label = cands_ref[r, :, width:].astype(F32)[:, 0:1]
    lo = lax.axis_index("lo")
    lower = jnp.where(lax.axis_index("hi") == 0, lo, low - 1 - lo)
    index = lax.broadcasted_iota(jnp.int32, (live, 1), 0)
    held = num // (2 * low)
    place = lax.rem(index, num)
    place = (lax.div(place, held) ^ lower) * held + lax.rem(place, held)
    limit = jnp.zeros((live, 1), F32)
    for user in range(users):
        count = flags_ref[r, 0:1, capacity + user : capacity + user + 1].astype(F32)
        limit = jnp.where(index >= user * num, count, limit)
    alive = place.astype(F32) < limit
    grad_logit = jnp.where(alive, (jax.nn.sigmoid(logit) - label) / USERS_DEV, 0.0)
    grad_proj = (grad_logit * cand_f / root).astype(BF16)
    grad_mixed = nt(grad_proj, wo).astype(BF16).astype(F32)
    joint = grad_mixed.T * mixed_t
    inner = jnp.concatenate(
        [
            jnp.sum(joint[h * head_size : (h + 1) * head_size, :], axis=0, keepdims=True)
            for h in range(HEADS)
        ],
        axis=0,
    )
    inner = flat(inner * factor)
    factor = flat(factor)
    factor_col = jnp.broadcast_to(factor, (128, cols)).T[:, :1]
    grad_heads = by_head(grad_mixed)
    grad_w = nt((grad_heads * factor_col).astype(BF16), wv).astype(BF16)

    both_w = jnp.concatenate([query_w_ref[...], grad_w], axis=0)
    rows_s = jnp.zeros((width, cols), F32)
    for t in range(tiles):
        rows = take_tile(rows_ref, r, t, per_tile, capacity)
        e = expo_ref[t * TILE : (t + 1) * TILE, :]
        grad_score = (e.astype(F32) * (nt(rows, grad_w) - inner)).astype(BF16)
        rows_s = rows_s + nn(turned_ref[:, t * TILE : (t + 1) * TILE], grad_score)
        grad_rows = nn(jnp.concatenate([grad_score, e], axis=1), both_w).astype(BF16)
        for k in range(per_tile):
            out_ref[t * per_tile + k, r * capacity : (r + 1) * capacity, :] = grad_rows[
                k * capacity : (k + 1) * capacity, :
            ]

    rows_s = rows_s.astype(BF16)
    grad_query_t = (head_blocks(wk_ref[...].T, rows_s, live) * scale).astype(BF16)
    share = flat(part_own)
    parts = (
        nt(cands.T, grad_query_t),
        nn(rows_s, query_ref[...]),
        nn((mean_ref[...].astype(F32) * share).astype(BF16), grad_heads.astype(BF16)),
        nn(mixed_tb, grad_proj) * 0.5,
    )
    for k, part in enumerate(parts):
        if r == 0:
            weights[k * width : (k + 1) * width, :] = part
        else:
            weights[k * width : (k + 1) * width, :] = (
                first_weights[k * width : (k + 1) * width, :] + part
            )
    if r == 1:
        rows_each = 4 * width // blocks
        for b in range(blocks):
            out_ref[b, :capacity, :] = first_ref[b]
            out_ref[b, both:, :] = weights[b * rows_each : (b + 1) * rows_each, :].astype(BF16)


def backward(r, users, low, rows, *operands):
    blocks, both, width = rows.shape
    vmem = pl.BlockSpec(memory_space=pltpu.VMEM)
    weights = jax.ShapeDtypeStruct((4 * width, width), F32)
    if r == 0:
        out_shape = (jax.ShapeDtypeStruct((blocks, both // 2, width), BF16), weights)
        scratch_shapes = []
    else:
        out_shape = jax.ShapeDtypeStruct((blocks, both + 4 * width // blocks, width), BF16)
        scratch_shapes = [pltpu.VMEM(weights.shape, F32)]
    return pl.pallas_call(
        functools.partial(backward_kernel, r, users, low),
        out_shape=out_shape,
        in_specs=[vmem] * (1 + len(operands)),
        out_specs=(vmem, vmem) if r == 0 else vmem,
        scratch_shapes=scratch_shapes,
        compiler_params=pltpu.CompilerParams(vmem_limit_bytes=VMEM_LIMIT),
        cost_estimate=cost(6 * blocks * both * width * width * HEADS, 0),
        name="backward",
    )(rows, *operands)


def exchange(x, axes):
    return lax.all_to_all(x, axes, split_axis=0, concat_axis=0, tiled=True)


def swap_halves(x):
    return lax.ppermute(x, "hi", [(0, 1), (1, 0)])


def swap(x):
    peers = lax.axis_size(PEERS)
    return lax.ppermute(x, PEERS, [(i, peers - 1 - i) for i in range(peers)])


def pair_candidates(mine, users, flags):
    peers = lax.axis_size(PEERS)
    peer = lax.axis_index(PEERS)
    first = lax.axis_index("hi") == 0
    _, held, wide = mine.shape
    mine = mine.reshape(peers, users, held, wide)
    got = []
    for k in range(peers):
        to = peer ^ k
        lower = jnp.minimum(to, peers - 1 - to)
        piece = jnp.stack(
            [
                lax.dynamic_index_in_dim(mine, lower, 0, keepdims=False),
                lax.dynamic_index_in_dim(mine, peers - 1 - lower, 0, keepdims=False),
            ]
        )
        if k == peers - 1:
            piece = jnp.concatenate(
                [piece.reshape(-1, wide), jnp.pad(flags, ((0, 0), (0, wide - flags.shape[1])))], axis=0
            )
        if k > 0:
            piece = lax.ppermute(piece, PEERS, [(i, i ^ k) for i in range(peers)])
        got.append(piece)
    lines = 2 * users * held
    flags = got[-1][lines:, : flags.shape[1]]
    got[-1] = got[-1][:lines].reshape(got[0].shape)
    cands = jnp.concatenate(
        [jnp.where(first, got[k], got[peers - 1 - k]) for k in range(peers)], axis=2
    )
    return cands.reshape(2, -1, wide), flags


def local(
    table, behaviour_ids, lengths, candidates, labels, cand_counts, w_query, w_key, w_value, w_out
):
    shards = lax.axis_size(ALL)
    half = shards // 2
    sizes = (lax.axis_size("group"), lax.axis_size("lo"))
    first = lax.axis_index("hi") == 0
    users, seq = behaviour_ids.shape
    rows_dev, width = table.shape
    total = users * seq
    capacity = total // shards + total // (2 * shards)
    slots = shards * capacity
    num = candidates.shape[1] * lax.axis_size("hi") * lax.axis_size("lo")

    requests, flags, mine = plan(
        behaviour_ids, lengths, cand_counts, candidates, labels, rows_dev, sizes, capacity
    )
    wanted = exchange(requests, BY_HALF)
    flags = flags.reshape(2, half, -1)
    flags_kept = jnp.where(first, flags[0], flags[1])
    cands, swapped = pair_candidates(mine, users, jnp.where(first, flags[1], flags[0]))

    wanted = wanted.reshape(2, sizes[0], sizes[1], capacity + LINE)
    lower = jnp.where(first, wanted[0], wanted[0, :, ::-1])
    upper = jnp.where(first, wanted[1, :, ::-1], wanted[1])
    wanted = jnp.stack([lower, upper], axis=2).reshape(shards, capacity + LINE)
    served = gather(wanted.reshape(-1), table, shards)
    wanted = wanted[:, :capacity]
    served, cands, swapped = lax.optimization_barrier((served, cands, swapped))
    rows = exchange(served.reshape(half, 2 * capacity, width), HALF)
    rows, cands, swapped, flags_kept = lax.optimization_barrier((rows, cands, swapped, flags_kept))
    flags = jnp.stack(
        [jnp.where(first, flags_kept, swapped), jnp.where(first, swapped, flags_kept)]
    )
    ahead = [forward(r, rows, flags, cands, num, w_query, w_key, w_value) for r in range(2)]
    back = []
    for r, (expo, own, *kept) in enumerate(ahead):
        other = swap(own)
        back = backward(
            r,
            users,
            sizes[1],
            rows,
            flags,
            cands,
            w_key,
            w_value,
            w_out,
            other,
            expo,
            own,
            *kept,
            *back,
        )
    outgoing = back
    returned = exchange(outgoing, HALF)
    table_grad = scatter(wanted.reshape(1, slots), returned, rows_dev)

    part = jnp.sum(returned[:, 2 * capacity :, :].astype(F32), axis=0).astype(BF16)
    weight_grads = exchange(spread(part, swap_halves(part), half), HALF)
    return table_grad, weight_grads.reshape(4, width, width).astype(F32)


def solution(mesh):
    groups, peers = mesh.shape["group"], mesh.shape["peer"]
    mesh = Mesh(mesh.devices.reshape(groups, 2, peers // 2), ALL)
    in_specs = (
        P(ALL, None),
        P(ALL, None),
        P(ALL),
        P("group", ("hi", "lo"), None),
        P("group", ("hi", "lo")),
        P(ALL),
        P(),
        P(),
        P(),
        P(),
    )
    out_specs = (P(ALL, None), P())
    return jax.shard_map(local, mesh=mesh, in_specs=in_specs, out_specs=out_specs, check_vma=False)
```

```python
import functools
import math

import jax
import jax.numpy as jnp
from jax import lax
from jax.experimental import pallas as pl
from jax.experimental.pallas import tpu as pltpu
from jax.sharding import Mesh
from jax.sharding import PartitionSpec as P

HEADS = 4
USERS_DEV = 2
ALL = ("group", "hi", "lo")
BY_HALF = ("hi", "group", "lo")
HALF = ("group", "lo")
PEERS = ("hi", "lo")
BF16 = jnp.bfloat16
F32 = jnp.float32
VMEM_LIMIT = 12 * 1024 * 1024
LOWEST = -1e30
LINE = 8


def nt(a, b):
    return lax.dot_general(a, b, (((1,), (1,)), ((), ())), preferred_element_type=F32)


def nn(a, b):
    return jnp.dot(a, b, preferred_element_type=F32)


def cost(flops, transcendentals):
    return pl.CostEstimate(flops=flops, bytes_accessed=0, transcendentals=transcendentals)


def log2(n):
    return n.bit_length() - 1


def plan_kernel(
    rows_dev,
    sizes,
    lengths_hbm,
    counts_hbm,
    ids_hbm,
    cands_hbm,
    labels_hbm,
    requests_ref,
    flags_ref,
    labelled_ref,
    lengths_ref,
    counts_ref,
    ids_ref,
    cands_ref,
    labels_ref,
    sems,
):
    copies = [
        pltpu.make_async_copy(source, target, sems.at[k])
        for k, (source, target) in enumerate(
            (
                (lengths_hbm, lengths_ref),
                (counts_hbm, counts_ref),
                (ids_hbm, ids_ref),
                (cands_hbm, cands_ref),
                (labels_hbm, labels_ref),
            )
        )
    ]
    for copy in copies:
        copy.start()
    for copy in copies:
        copy.wait()
    groups, low = sizes
    users, seq = ids_ref.shape
    shards = requests_ref.shape[0]
    capacity = requests_ref.shape[1] - LINE
    half = shards // 2
    block = 256
    before = (
        lax.broadcasted_iota(jnp.int32, (block, block), 0)
        < lax.broadcasted_iota(jnp.int32, (block, block), 1)
    ).astype(BF16)
    device = lax.broadcasted_iota(jnp.int32, (shards, block), 0)
    place = lax.broadcasted_iota(jnp.int32, (capacity, block), 0).astype(F32)
    lane = lax.broadcasted_iota(jnp.int32, (1, block), 1)
    count = jnp.zeros((shards, 1), F32)
    rows = jnp.zeros((3 * shards, capacity), F32)
    for user in range(users):
        for start in range(0, seq, block):
            ids = ids_ref[user : user + 1, start : start + block]
            owner = lax.shift_right_logical(ids, log2(rows_dev))
            row = ids & (rows_dev - 1)
            group = lax.shift_right_logical(owner, log2(2 * low))
            high = lax.shift_right_logical(owner, log2(low)) & 1
            owner = high * half + group * low + (owner & (low - 1))
            live = lane + start < lengths_ref[user]
            owner = jnp.where(live, owner, shards)
            hot = (device == owner).astype(F32)
            hot_b = hot.astype(BF16)
            earlier = nn(hot_b, before) + count
            count = count + jnp.sum(hot, axis=1, keepdims=True)
            rank = jnp.sum(hot * earlier, axis=0, keepdims=True)
            ranked = (place == rank).astype(F32).astype(BF16)
            upper = lax.shift_right_logical(row, 6).astype(F32)
            lower = (row & 63).astype(F32)
            parts = jnp.concatenate([hot * upper, hot * lower, hot * float(user + 1)], axis=0)
            rows = rows + nt(parts.astype(BF16), ranked)
    requests = jnp.concatenate(
        [rows[:shards] * 64.0 + rows[shards : 2 * shards], jnp.broadcast_to(count, (shards, LINE))],
        axis=1,
    )
    requests_ref[...] = requests.astype(jnp.int32)
    lane = lax.broadcasted_iota(jnp.int32, (shards, 128 - capacity), 1)
    rest = jnp.zeros(lane.shape, F32)
    for user in range(users):
        rest = jnp.where(lane == user, counts_ref[user].astype(F32), rest)
    flags_ref[...] = jnp.concatenate([rows[2 * shards :], rest], axis=1).astype(BF16)
    _, held, width = cands_ref.shape
    square = lax.broadcasted_iota(jnp.int32, (held, held), 0)
    square = square == lax.broadcasted_iota(jnp.int32, (held, held), 1)
    lane = lax.broadcasted_iota(jnp.int32, (held, 128), 1)
    for user in range(cands_ref.shape[0]):
        label = jnp.sum(
            jnp.where(square, labels_ref[user : user + 1, :], 0.0), axis=1, keepdims=True
        )
        labelled_ref[user, :, :width] = cands_ref[user]
        labelled_ref[user, :, width:] = jnp.where(lane == 0, label, 0.0).astype(BF16)


def plan(behaviour_ids, lengths, cand_counts, candidates, labels, rows_dev, sizes, capacity):
    half = sizes[0] * sizes[1]
    vmem = pl.BlockSpec(memory_space=pltpu.VMEM)
    operands = (lengths, cand_counts, behaviour_ids, candidates, labels)
    return pl.pallas_call(
        functools.partial(plan_kernel, rows_dev, sizes),
        out_shape=(
            jax.ShapeDtypeStruct((2 * half, capacity + LINE), jnp.int32),
            jax.ShapeDtypeStruct((2 * half, 128), BF16),
            jax.ShapeDtypeStruct(candidates.shape[:2] + (candidates.shape[2] + 128,), BF16),
        ),
        in_specs=[pl.BlockSpec(memory_space=pltpu.HBM)] * 5,
        out_specs=(vmem,) * 3,
        scratch_shapes=[
            pltpu.SMEM(lengths.shape, jnp.int32),
            pltpu.SMEM(cand_counts.shape, jnp.int32),
            pltpu.VMEM(behaviour_ids.shape, jnp.int32),
            pltpu.VMEM(candidates.shape, BF16),
            pltpu.VMEM(labels.shape, F32),
            pltpu.SemaphoreType.DMA((5,)),
        ],
        compiler_params=pltpu.CompilerParams(vmem_limit_bytes=VMEM_LIMIT),
        cost_estimate=cost(2**24, 0),
        name="plan",
    )(*(pltpu.with_memory_space_constraint(x, pltpu.HBM) for x in operands))


def gather_kernel(blocks, wanted_ref, table_hbm, out, narrow, wide, in_sems):
    slots = out.shape[0]
    capacity = slots // blocks
    line = capacity + LINE
    joint = 1 if capacity % 32 == 0 else math.lcm(capacity, 16) // capacity
    step = 32 if joint == 1 else joint * capacity
    halves, _, lanes = wide.shape
    loads = in_sems.shape[0]
    size = narrow.shape[0] // loads
    copies = []
    for k in range(loads):
        part = pl.ds(k * size, size)
        copies.append(pltpu.make_async_copy(table_hbm.at[part], narrow.at[part], in_sems.at[k]))
        copies[-1].start()
    out[...] = jnp.zeros(out.shape, BF16)
    for k, copy in enumerate(copies):
        copy.wait()
        part = slice(k * size, (k + 1) * size)
        for h in range(halves):
            wide[h, part, :] = narrow[part, h * lanes : (h + 1) * lanes].astype(F32)

    def bucket(b, carry):
        first = b * joint * line

        def fetch(c, carry):
            at = c * step
            start = pl.multiple_of(b * joint * capacity + at, 16)
            for k in range(0, step, 16):
                ids = [wanted_ref[first + at + n + n // capacity * LINE] for n in range(k, k + 16)]
                for h in range(halves):
                    rows = [wide[h, pl.ds(row, 1), :] for row in ids]
                    out[pl.ds(start + k, 16), h * lanes : (h + 1) * lanes] = jnp.concatenate(
                        rows, axis=0
                    ).astype(BF16)
            return carry

        steps = 1 if joint > 1 else lax.div(wanted_ref[first + capacity] + step - 1, step)
        return lax.fori_loop(0, steps, fetch, carry)

    lax.fori_loop(0, blocks // joint, bucket, 0)


def gather(wanted, table, blocks):
    width = table.shape[1]
    slots = wanted.shape[0] - blocks * LINE
    return pl.pallas_call(
        functools.partial(gather_kernel, blocks),
        out_shape=jax.ShapeDtypeStruct((slots, width), BF16),
        in_specs=[
            pl.BlockSpec(memory_space=pltpu.SMEM),
            pl.BlockSpec(memory_space=pltpu.HBM),
        ],
        out_specs=pl.BlockSpec(memory_space=pltpu.VMEM),
        scratch_shapes=[
            pltpu.VMEM(table.shape, BF16),
            pltpu.VMEM((width // 128, table.shape[0], 128), F32),
            pltpu.SemaphoreType.DMA((8,)),
        ],
        compiler_params=pltpu.CompilerParams(vmem_limit_bytes=VMEM_LIMIT),
        cost_estimate=cost(slots * width, 0),
        name="gather_rows",
    )(wanted, pltpu.with_memory_space_constraint(table, pltpu.HBM))


def spread_kernel(own_ref, other_ref, out_ref):
    part = (own_ref[...].astype(F32) + other_ref[...].astype(F32)).astype(BF16)
    for k in range(out_ref.shape[0]):
        out_ref[k] = part


def spread(own, other, copies):
    vmem = pl.BlockSpec(memory_space=pltpu.VMEM)
    return pl.pallas_call(
        spread_kernel,
        out_shape=pltpu.VMEM((copies,) + own.shape, BF16),
        in_specs=[vmem, vmem],
        out_specs=vmem,
        compiler_params=pltpu.CompilerParams(vmem_limit_bytes=VMEM_LIMIT),
        cost_estimate=cost(own.size, 0),
        name="spread",
    )(own, other)


def scatter_kernel(wanted_ref, returned_ref, out_ref, grads):
    tile = out_ref.shape[0]
    slots = grads.shape[0]
    blocks = returned_ref.shape[0]
    each = slots // blocks
    block = 256

    @pl.when(pl.program_id(0) == 0)
    def _():
        for b in range(blocks):
            grads[b * each : (b + 1) * each, :] = returned_ref[b, :each, :]

    row = lax.broadcasted_iota(jnp.int32, (tile, block), 0) + pl.program_id(0) * tile
    total = jnp.zeros(out_ref.shape, F32)
    for start in range(0, slots, block):
        hot = (row == wanted_ref[:, start : start + block]).astype(F32).astype(BF16)
        total = total + nn(hot, grads[start : start + block, :])
    out_ref[...] = total.astype(BF16)


def scatter(wanted, returned, rows_dev):
    slots = wanted.shape[1]
    width = returned.shape[-1]
    tile = 1024
    return pl.pallas_call(
        scatter_kernel,
        grid=(rows_dev // tile,),
        out_shape=jax.ShapeDtypeStruct((rows_dev, width), BF16),
        in_specs=[
            pl.BlockSpec((1, slots), lambda t: (0, 0)),
            pl.BlockSpec(returned.shape, lambda t: (0, 0, 0)),
        ],
        out_specs=pl.BlockSpec((tile, width), lambda t: (t, 0)),
        scratch_shapes=[pltpu.VMEM((slots, width), BF16)],
        compiler_params=pltpu.CompilerParams(vmem_limit_bytes=VMEM_LIMIT),
        cost_estimate=cost(2 * rows_dev * slots * width, 0),
        name="scatter_rows",
    )(wanted, returned)


def by_head(x):
    head_size = x.shape[1] // HEADS
    head = lax.broadcasted_iota(jnp.int32, x.shape, 1) // head_size
    return jnp.concatenate([jnp.where(head == h, x, 0.0) for h in range(HEADS)], axis=0)


def head_blocks(a_t, b, live):
    size = a_t.shape[0] // HEADS
    return jnp.concatenate(
        [nn(a_t[h * size : (h + 1) * size, :], b[:, h * live : (h + 1) * live]) for h in range(HEADS)],
        axis=0,
    )


def head_sums(x):
    size = x.shape[0] // HEADS
    return jnp.concatenate(
        [jnp.sum(x[h * size : (h + 1) * size], axis=0, keepdims=True) for h in range(HEADS)], axis=0
    )


def stacked(x, live):
    return jnp.concatenate([x[:, h * live : (h + 1) * live] for h in range(HEADS)], axis=0)


def flat(x):
    return jnp.concatenate([x[h : h + 1, :] for h in range(HEADS)], axis=1)


def take_tile(rows_ref, r, t, per_tile, capacity):
    return jnp.concatenate(
        [
            rows_ref[b, r * capacity : (r + 1) * capacity, :]
            for b in range(t * per_tile, (t + 1) * per_tile)
        ],
        axis=0,
    )


TILE = 768
FORWARD_TILE = 256


def forward_kernel(
    r,
    num,
    rows_ref,
    flags_ref,
    cands_ref,
    wq_ref,
    wk_ref,
    wv_ref,
    wo_ref,
    expo_ref,
    part_ref,
    mean_ref,
    turned_ref,
    query_ref,
    query_w_ref,
    mixed_ref,
    turned_out_ref,
    scores,
    mine,
):
    blocks, both, width = rows_ref.shape
    capacity = both // 2
    live = cands_ref.shape[1]
    cols = HEADS * live
    tiles = blocks * capacity // FORWARD_TILE
    for b in range(blocks):
        mine[b * capacity : (b + 1) * capacity, :] = rows_ref[b, r * capacity : (r + 1) * capacity, :]
    user_of = lax.rem(lax.broadcasted_iota(jnp.int32, (1, cols), 1), live) // num + 1
    user_of = user_of.astype(F32)
    scale = float(width // HEADS) ** (-0.5)
    query = nn(cands_ref[r, :, :width], wq_ref[...]).astype(BF16).astype(F32) * scale
    query = by_head(query).astype(BF16)
    query_w = nt(query, wk_ref[...]).astype(BF16)
    query_ref[...] = query
    query_w_ref[...] = query_w
    flags = flags_ref[r].astype(F32).T
    top = jnp.full((1, cols), LOWEST, F32)
    flags = jnp.concatenate([flags[:capacity, o : o + 1] for o in range(blocks)], axis=0)
    for t in range(tiles):
        part = slice(t * FORWARD_TILE, (t + 1) * FORWARD_TILE)
        rows = mine[part, :]
        turned_ref[:, part] = rows.T
        score = jnp.where(flags[part] == user_of, nt(rows, query_w), LOWEST)
        scores[part, :] = score
        top = jnp.maximum(top, jnp.max(score, axis=0, keepdims=True))
    norm = jnp.zeros((1, cols), F32)
    rows_e = jnp.zeros((width, cols), F32)
    for t in range(tiles):
        part = slice(t * FORWARD_TILE, (t + 1) * FORWARD_TILE)
        e = jnp.exp(scores[part, :] - top)
        norm = norm + jnp.sum(e, axis=0, keepdims=True)
        e = e.astype(BF16)
        expo_ref[part, :] = e
        rows_e = rows_e + nn(turned_ref[:, part], e)
    mean = (rows_e * (1.0 / norm)).astype(BF16)
    mean_ref[...] = mean
    mixed = head_blocks(wv_ref[...].T, mean, live)
    mixed_ref[...] = mixed.astype(BF16)
    out = nt(wo_ref[...], cands_ref[r, :, :width])
    turned_out_ref[...] = out
    part_ref[...] = jnp.concatenate(
        [head_sums(mixed * out), stacked(top, live), stacked(norm, live), jnp.zeros((4, live), F32)],
        axis=0,
    )


def forward(r, rows, flags, cands, num, *weights):
    blocks, both, width = rows.shape
    live = cands.shape[1]
    cols = HEADS * live
    slots = blocks * both // 2
    vmem = pl.BlockSpec(memory_space=pltpu.VMEM)
    shapes = (
        ((slots, cols), BF16),
        ((16, live), F32),
        ((width, cols), BF16),
        ((width, slots), BF16),
        ((cols, width), BF16),
        ((cols, width), BF16),
        ((width, live), BF16),
        ((width, live), F32),
    )
    return pl.pallas_call(
        functools.partial(forward_kernel, r, num),
        out_shape=tuple(jax.ShapeDtypeStruct(*shape) for shape in shapes),
        in_specs=[vmem] * (3 + len(weights)),
        out_specs=(vmem,) * len(shapes),
        scratch_shapes=[pltpu.VMEM((slots, cols), F32), pltpu.VMEM((slots, width), BF16)],
        compiler_params=pltpu.CompilerParams(vmem_limit_bytes=VMEM_LIMIT),
        cost_estimate=cost(4 * slots * width * cols, slots * cols),
        name="forward",
    )(rows, flags, cands, *weights)


def backward_kernel(
    r,
    users,
    low,
    rows_ref,
    flags_ref,
    cands_ref,
    wk_ref,
    wv_ref,
    other_ref,
    expo_ref,
    own_ref,
    mean_ref,
    turned_ref,
    query_ref,
    query_w_ref,
    mixed_ref,
    turned_out_ref,
    *refs,
):
    if r == 0:
        out_ref, weights = refs
    else:
        first_ref, first_weights, out_ref, weights = refs
    blocks, both, width = rows_ref.shape
    capacity = both // 2
    live = cands_ref.shape[1]
    num = live // users
    cols = HEADS * live
    head_size = width // HEADS
    scale = float(head_size) ** (-0.5)
    root = float(width) ** 0.5
    per_tile = TILE // capacity
    tiles = blocks // per_tile

    top_own, top_other = own_ref[4:8, :], other_ref[4:8, :]
    top = jnp.maximum(top_own, top_other)
    factor = jnp.exp(top_own - top)
    part_own = own_ref[8:12, :] * factor
    part_other = other_ref[8:12, :] * jnp.exp(top_other - top)
    inv = 1.0 / (part_own + part_other)
    factor = factor * inv
    part_own = part_own * inv
    part_other = part_other * inv
    dots = own_ref[0:4, :] * part_own + other_ref[0:4, :] * part_other
    logit = jnp.sum(dots, axis=0, keepdims=True) / root

    cands = cands_ref[r, :, :width]
    label = cands_ref[r, :, width:].astype(F32).T[0:1, :]
    lo = lax.axis_index("lo")
    lower = jnp.where(lax.axis_index("hi") == 0, lo, low - 1 - lo)
    index = lax.broadcasted_iota(jnp.int32, (1, live), 1)
    held = num // (2 * low)
    place = lax.rem(index, num)
    place = (lax.div(place, held) ^ lower) * held + lax.rem(place, held)
    limit = jnp.zeros((1, live), F32)
    for user in range(users):
        count = flags_ref[r, 0:1, capacity + user : capacity + user + 1].astype(F32)
        limit = jnp.where(index >= user * num, count, limit)
    alive = place.astype(F32) < limit
    grad_logit = jnp.where(alive, (jax.nn.sigmoid(logit) - label) / USERS_DEV, 0.0)
    grad_mixed = (turned_out_ref[...] * (grad_logit / root)).T.astype(BF16).astype(F32)
    inner = flat(dots * (grad_logit / root) * factor)
    factor = flat(factor)
    factor_col = jnp.broadcast_to(factor, (128, cols)).T[:, :1]
    grad_heads = by_head(grad_mixed)
    grad_w = nt((grad_heads * factor_col).astype(BF16), wv_ref[...]).astype(BF16)

    both_w = jnp.concatenate([query_w_ref[...], grad_w], axis=0)
    rows_s = jnp.zeros((width, cols), F32)
    for t in range(tiles):
        rows = take_tile(rows_ref, r, t, per_tile, capacity)
        e = expo_ref[t * TILE : (t + 1) * TILE, :]
        grad_score = (e.astype(F32) * (nt(rows, grad_w) - inner)).astype(BF16)
        rows_s = rows_s + nn(turned_ref[:, t * TILE : (t + 1) * TILE], grad_score)
        grad_rows = nn(jnp.concatenate([grad_score, e], axis=1), both_w).astype(BF16)
        for k in range(per_tile):
            out_ref[t * per_tile + k, r * capacity : (r + 1) * capacity, :] = grad_rows[
                k * capacity : (k + 1) * capacity, :
            ]

    rows_s = rows_s.astype(BF16)
    grad_query_t = (head_blocks(wk_ref[...].T, rows_s, live) * scale).astype(BF16)
    grad_col = jnp.broadcast_to(grad_logit, (128, live)).T[:, :1]
    grad_proj = (grad_col * cands.astype(F32) / root).astype(BF16)
    mixed = jnp.concatenate(
        [
            mixed_ref[h * head_size : (h + 1) * head_size, :].astype(F32) * part_own[h : h + 1]
            for h in range(HEADS)
        ],
        axis=0,
    )
    parts = (
        nt(cands.T, grad_query_t),
        nn(rows_s, query_ref[...]),
        nn((mean_ref[...].astype(F32) * flat(part_own)).astype(BF16), grad_heads.astype(BF16)),
        nn(mixed.astype(BF16), grad_proj),
    )
    for k, part in enumerate(parts):
        if r == 0:
            weights[k * width : (k + 1) * width, :] = part
        else:
            weights[k * width : (k + 1) * width, :] = (
                first_weights[k * width : (k + 1) * width, :] + part
            )
    if r == 1:
        rows_each = 4 * width // blocks
        for b in range(blocks):
            out_ref[b, :capacity, :] = first_ref[b]
            out_ref[b, both:, :] = weights[b * rows_each : (b + 1) * rows_each, :].astype(BF16)


def backward(r, users, low, rows, *operands):
    blocks, both, width = rows.shape
    vmem = pl.BlockSpec(memory_space=pltpu.VMEM)
    weights = jax.ShapeDtypeStruct((4 * width, width), F32)
    if r == 0:
        out_shape = (jax.ShapeDtypeStruct((blocks, both // 2, width), BF16), weights)
        scratch_shapes = []
    else:
        out_shape = jax.ShapeDtypeStruct((blocks, both + 4 * width // blocks, width), BF16)
        scratch_shapes = [pltpu.VMEM(weights.shape, F32)]
    return pl.pallas_call(
        functools.partial(backward_kernel, r, users, low),
        out_shape=out_shape,
        in_specs=[vmem] * (1 + len(operands)),
        out_specs=(vmem, vmem) if r == 0 else vmem,
        scratch_shapes=scratch_shapes,
        compiler_params=pltpu.CompilerParams(vmem_limit_bytes=VMEM_LIMIT),
        cost_estimate=cost(6 * blocks * both * width * width * HEADS, 0),
        name="backward",
    )(rows, *operands)


def exchange(x, axes):
    return lax.all_to_all(x, axes, split_axis=0, concat_axis=0, tiled=True)


def swap_halves(x):
    return lax.ppermute(x, "hi", [(0, 1), (1, 0)])


def swap(x):
    peers = lax.axis_size(PEERS)
    return lax.ppermute(x, PEERS, [(i, peers - 1 - i) for i in range(peers)])


def pair_candidates(mine, users, flags):
    peers = lax.axis_size(PEERS)
    peer = lax.axis_index(PEERS)
    first = lax.axis_index("hi") == 0
    _, held, wide = mine.shape
    mine = mine.reshape(peers, users, held, wide)
    got = []
    for k in range(peers):
        to = peer ^ k
        lower = jnp.minimum(to, peers - 1 - to)
        piece = jnp.stack(
            [
                lax.dynamic_index_in_dim(mine, lower, 0, keepdims=False),
                lax.dynamic_index_in_dim(mine, peers - 1 - lower, 0, keepdims=False),
            ]
        )
        if k == peers - 1:
            piece = jnp.concatenate(
                [piece.reshape(-1, wide), jnp.pad(flags, ((0, 0), (0, wide - flags.shape[1])))], axis=0
            )
        if k > 0:
            piece = lax.ppermute(piece, PEERS, [(i, i ^ k) for i in range(peers)])
        got.append(piece)
    lines = 2 * users * held
    flags = got[-1][lines:, : flags.shape[1]]
    got[-1] = got[-1][:lines].reshape(got[0].shape)
    cands = jnp.concatenate(
        [jnp.where(first, got[k], got[peers - 1 - k]) for k in range(peers)], axis=2
    )
    return cands.reshape(2, -1, wide), flags


def local(
    table, behaviour_ids, lengths, candidates, labels, cand_counts, w_query, w_key, w_value, w_out
):
    shards = lax.axis_size(ALL)
    half = shards // 2
    sizes = (lax.axis_size("group"), lax.axis_size("lo"))
    first = lax.axis_index("hi") == 0
    users, seq = behaviour_ids.shape
    rows_dev, width = table.shape
    total = users * seq
    capacity = total // shards + total // (2 * shards)
    slots = shards * capacity
    num = candidates.shape[1] * lax.axis_size("hi") * lax.axis_size("lo")

    requests, flags, mine = plan(
        behaviour_ids, lengths, cand_counts, candidates, labels, rows_dev, sizes, capacity
    )
    wanted = exchange(requests, BY_HALF)
    flags = flags.reshape(2, half, -1)
    flags_kept = jnp.where(first, flags[0], flags[1])
    cands, swapped = pair_candidates(mine, users, jnp.where(first, flags[1], flags[0]))

    wanted = wanted.reshape(2, sizes[0], sizes[1], capacity + LINE)
    lower = jnp.where(first, wanted[0], wanted[0, :, ::-1])
    upper = jnp.where(first, wanted[1, :, ::-1], wanted[1])
    wanted = jnp.stack([lower, upper], axis=2).reshape(shards, capacity + LINE)
    served = gather(wanted.reshape(-1), table, shards)
    wanted = wanted[:, :capacity]
    served, cands, swapped = lax.optimization_barrier((served, cands, swapped))
    rows = exchange(served.reshape(half, 2 * capacity, width), HALF)
    rows, cands, swapped, flags_kept = lax.optimization_barrier((rows, cands, swapped, flags_kept))
    flags = jnp.stack(
        [jnp.where(first, flags_kept, swapped), jnp.where(first, swapped, flags_kept)]
    )
    ahead = [
        forward(r, rows, flags, cands, num, w_query, w_key, w_value, w_out) for r in range(2)
    ]
    back = []
    for r, (expo, own, *kept) in enumerate(ahead):
        other = swap(own)
        back = backward(
            r,
            users,
            sizes[1],
            rows,
            flags,
            cands,
            w_key,
            w_value,
            other,
            expo,
            own,
            *kept,
            *back,
        )
    outgoing = back
    returned = exchange(outgoing, HALF)
    table_grad = scatter(wanted.reshape(1, slots), returned, rows_dev)

    part = jnp.sum(returned[:, 2 * capacity :, :].astype(F32), axis=0).astype(BF16)
    weight_grads = exchange(spread(part, swap_halves(part), half), HALF)
    return table_grad, weight_grads.reshape(4, width, width).astype(F32)


def solution(mesh):
    groups, peers = mesh.shape["group"], mesh.shape["peer"]
    mesh = Mesh(mesh.devices.reshape(groups, 2, peers // 2), ALL)
    in_specs = (
        P(ALL, None),
        P(ALL, None),
        P(ALL),
        P("group", ("hi", "lo"), None),
        P("group", ("hi", "lo")),
        P(ALL),
        P(),
        P(),
        P(),
        P(),
    )
    out_specs = (P(ALL, None), P())
    return jax.shard_map(local, mesh=mesh, in_specs=in_specs, out_specs=out_specs, check_vma=False)
```

```python
import functools
import math

import jax
import jax.numpy as jnp
from jax import lax
from jax.experimental import pallas as pl
from jax.experimental.pallas import tpu as pltpu
from jax.sharding import Mesh
from jax.sharding import PartitionSpec as P

HEADS = 4
USERS_DEV = 2
PEERS = ("hi", "lo")
ALL = ("ga", "core") + PEERS
COLUMN = ("ga",) + PEERS
BY_CORE = ("core",) + COLUMN
HALF = ("ga", "core", "lo")
BF16 = jnp.bfloat16
F32 = jnp.float32
VMEM_LIMIT = 16 * 1024 * 1024
LOWEST = -1e30
LINE = 8
TILE = 768
SENDS = 4


def nt(a, b):
    return lax.dot_general(a, b, (((1,), (1,)), ((), ())), preferred_element_type=F32)


def nn(a, b):
    return jnp.dot(a, b, preferred_element_type=F32)


def cost(flops, transcendentals):
    return pl.CostEstimate(flops=flops, bytes_accessed=0, transcendentals=transcendentals)


def log2(n):
    return n.bit_length() - 1


def plan_kernel(
    rows_dev, peers, lengths_hbm, ids_hbm, requests_ref, lengths_ref, ids_ref, sems
):
    copies = [
        pltpu.make_async_copy(source, target, sems.at[k])
        for k, (source, target) in enumerate(((lengths_hbm, lengths_ref), (ids_hbm, ids_ref)))
    ]
    for copy in copies:
        copy.start()
    for copy in copies:
        copy.wait()
    users, seq = ids_ref.shape
    shards = requests_ref.shape[0]
    capacity = requests_ref.shape[1] - LINE
    block = 256
    before = (
        lax.broadcasted_iota(jnp.int32, (block, block), 0)
        < lax.broadcasted_iota(jnp.int32, (block, block), 1)
    ).astype(BF16)
    device = lax.broadcasted_iota(jnp.int32, (shards, block), 0)
    place = lax.broadcasted_iota(jnp.int32, (capacity, block), 0).astype(F32)
    lane = lax.broadcasted_iota(jnp.int32, (1, block), 1)
    count = jnp.zeros((shards, 1), F32)
    rows = jnp.zeros((3 * shards, capacity), F32)
    for user in range(users):
        for start in range(0, seq, block):
            ids = ids_ref[user : user + 1, start : start + block]
            owner = lax.shift_right_logical(ids, log2(rows_dev))
            row = ids & (rows_dev - 1)
            group = lax.shift_right_logical(owner, log2(peers))
            owner = (
                (group & 1) * (shards // 2)
                + lax.shift_right_logical(group, 1) * peers
                + (owner & (peers - 1))
            )
            live = lane + start < lengths_ref[user]
            owner = jnp.where(live, owner, shards)
            hot = (device == owner).astype(F32)
            hot_b = hot.astype(BF16)
            earlier = nn(hot_b, before) + count
            count = count + jnp.sum(hot, axis=1, keepdims=True)
            rank = jnp.sum(hot * earlier, axis=0, keepdims=True)
            ranked = (place == rank).astype(F32).astype(BF16)
            upper = lax.shift_right_logical(row, 6).astype(F32)
            lower = (row & 63).astype(F32)
            parts = jnp.concatenate([hot * upper, hot * lower, hot * float(user + 1)], axis=0)
            rows = rows + nt(parts.astype(BF16), ranked)
    row = rows[:shards] * 64.0 + rows[shards : 2 * shards]
    requests = jnp.concatenate(
        [row * 4.0 + rows[2 * shards :], jnp.broadcast_to(count, (shards, LINE))], axis=1
    )
    requests_ref[...] = requests.astype(jnp.int32)


def plan(behaviour_ids, lengths, rows_dev, shards, peers, capacity):
    operands = (lengths, behaviour_ids)
    return pl.pallas_call(
        functools.partial(plan_kernel, rows_dev, peers),
        out_shape=jax.ShapeDtypeStruct((shards, capacity + LINE), jnp.int32),
        in_specs=[pl.BlockSpec(memory_space=pltpu.HBM)] * 2,
        out_specs=pl.BlockSpec(memory_space=pltpu.VMEM),
        scratch_shapes=[
            pltpu.SMEM(lengths.shape, jnp.int32),
            pltpu.VMEM(behaviour_ids.shape, jnp.int32),
            pltpu.SemaphoreType.DMA((2,)),
        ],
        compiler_params=pltpu.CompilerParams(vmem_limit_bytes=VMEM_LIMIT),
        cost_estimate=cost(2**24, 0),
        name="plan",
    )(*(pltpu.with_memory_space_constraint(x, pltpu.HBM) for x in operands))


def gather_kernel(blocks, wanted_ref, table_hbm, *refs):
    keep, *sends, narrow, wide, in_sems = refs
    slots = 2 * keep.shape[0]
    capacity = slots // blocks
    line = capacity + LINE
    joint = 1 if capacity % 32 == 0 else math.lcm(capacity, 16) // capacity
    step = 32 if joint == 1 else joint * capacity
    halves, _, lanes = wide.shape
    loads = in_sems.shape[0]
    size = narrow.shape[0] // loads
    copies = []
    for k in range(loads):
        part = pl.ds(k * size, size)
        copies.append(pltpu.make_async_copy(table_hbm.at[part], narrow.at[part], in_sems.at[k]))
        copies[-1].start()
    for out in (keep, *sends):
        out[...] = jnp.zeros(out.shape, BF16)
    for k, copy in enumerate(copies):
        copy.wait()
        part = slice(k * size, (k + 1) * size)
        for h in range(halves):
            wide[h, part, :] = narrow[part, h * lanes : (h + 1) * lanes].astype(F32)

    def bucket(out, skip, b, carry):
        first = (skip + b) * joint * line

        def fetch(c, carry):
            at = c * step
            start = pl.multiple_of(b * joint * capacity + at, 16)
            for k in range(0, step, 16):
                ids = [wanted_ref[first + at + n + n // capacity * LINE] for n in range(k, k + 16)]
                ids = [lax.shift_right_logical(row, 2) for row in ids]
                for h in range(halves):
                    rows = [wide[h, pl.ds(row, 1), :] for row in ids]
                    out[pl.ds(start + k, 16), h * lanes : (h + 1) * lanes] = jnp.concatenate(
                        rows, axis=0
                    ).astype(BF16)
            return carry

        steps = 1 if joint > 1 else lax.div(wanted_ref[first + capacity] + step - 1, step)
        return lax.fori_loop(0, steps, fetch, carry)

    each = blocks // joint // 2
    some = each // len(sends)
    for k, send in enumerate(sends):
        lax.fori_loop(0, some, functools.partial(bucket, send, each + k * some), 0)
    lax.fori_loop(0, each, functools.partial(bucket, keep, 0), 0)


def gather(wanted, table, blocks):
    width = table.shape[1]
    slots = wanted.shape[0] - blocks * LINE
    half = jax.ShapeDtypeStruct((slots // 2, width), BF16)
    part = jax.ShapeDtypeStruct((slots // 2 // SENDS, width), BF16)
    vmem = pl.BlockSpec(memory_space=pltpu.VMEM)
    return pl.pallas_call(
        functools.partial(gather_kernel, blocks),
        out_shape=(half,) + (part,) * SENDS,
        in_specs=[
            pl.BlockSpec(memory_space=pltpu.SMEM),
            pl.BlockSpec(memory_space=pltpu.HBM),
        ],
        out_specs=(vmem,) * (1 + SENDS),
        scratch_shapes=[
            pltpu.VMEM(table.shape, BF16),
            pltpu.VMEM((width // 128, table.shape[0], 128), F32),
            pltpu.SemaphoreType.DMA((8,)),
        ],
        compiler_params=pltpu.CompilerParams(vmem_limit_bytes=VMEM_LIMIT),
        cost_estimate=cost(6 * 10**9, 0),
        name="gather_rows",
    )(wanted, pltpu.with_memory_space_constraint(table, pltpu.HBM))


def spread_kernel(own_ref, other_ref, out_ref):
    part = (own_ref[...].astype(F32) + other_ref[...].astype(F32)).astype(BF16)
    for k in range(out_ref.shape[0]):
        out_ref[k] = part


def spread(own, other, copies):
    vmem = pl.BlockSpec(memory_space=pltpu.VMEM)
    return pl.pallas_call(
        spread_kernel,
        out_shape=pltpu.VMEM((copies,) + own.shape, BF16),
        in_specs=[vmem, vmem],
        out_specs=vmem,
        compiler_params=pltpu.CompilerParams(vmem_limit_bytes=VMEM_LIMIT),
        cost_estimate=cost(own.size, 0),
        name="spread",
    )(own, other)


def scatter_kernel(wanted_ref, keep_ref, back_ref, out_ref):
    tile = out_ref.shape[0]
    block = 256
    row = lax.broadcasted_iota(jnp.int32, (tile, block), 0) + pl.program_id(0) * tile
    total = jnp.zeros(out_ref.shape, F32)
    for k, grads in enumerate((keep_ref, back_ref)):
        slots = grads.shape[0]
        for start in range(0, slots, block):
            at = k * slots + start
            hot = (row == wanted_ref[:, at : at + block]).astype(F32).astype(BF16)
            total = total + nn(hot, grads[start : start + block, :])
    out_ref[...] = total.astype(BF16)


def scatter(wanted, keep, back, rows_dev):
    slots, width = keep.shape
    tile = 1024
    return pl.pallas_call(
        scatter_kernel,
        grid=(rows_dev // tile,),
        out_shape=jax.ShapeDtypeStruct((rows_dev, width), BF16),
        in_specs=[
            pl.BlockSpec((1, 2 * slots), lambda t: (0, 0)),
            pl.BlockSpec((slots, width), lambda t: (0, 0)),
            pl.BlockSpec((slots, width), lambda t: (0, 0)),
        ],
        out_specs=pl.BlockSpec((tile, width), lambda t: (t, 0)),
        compiler_params=pltpu.CompilerParams(vmem_limit_bytes=VMEM_LIMIT),
        cost_estimate=cost(4 * rows_dev * slots * width, 0),
        name="scatter_rows",
    )(wanted, keep, back)


def by_head(x):
    head_size = x.shape[1] // HEADS
    head = lax.broadcasted_iota(jnp.int32, x.shape, 1) // head_size
    return jnp.concatenate([jnp.where(head == h, x, 0.0) for h in range(HEADS)], axis=0)


def head_sums(x):
    size = x.shape[0] // HEADS
    return jnp.concatenate(
        [jnp.sum(x[h * size : (h + 1) * size], axis=0, keepdims=True) for h in range(HEADS)], axis=0
    )


def stacked(x, live):
    return jnp.concatenate([x[:, h * live : (h + 1) * live] for h in range(HEADS)], axis=0)


def flat(x):
    return jnp.concatenate([x[h : h + 1, :] for h in range(HEADS)], axis=1)


def diagonal(x, live):
    size = x.shape[0] // HEADS
    return jnp.concatenate(
        [x[h * size : (h + 1) * size, h * live : (h + 1) * live] for h in range(HEADS)], axis=0
    )


def tn(a, b):
    return lax.dot_general(a, b, (((0,), (0,)), ((), ())), preferred_element_type=F32)


def prepare_kernel(low, *refs):
    *sources, wq_ref, wo_ref, all_ref, query_ref, out_ref, wide = refs
    groups = len(sources)
    peers, group_users, held, width = sources[0].shape
    users = group_users // peers
    num = peers * held
    scale = float(width // HEADS) ** (-0.5)
    ga = lax.axis_index("ga")
    peer = lax.axis_index("hi") * low + lax.axis_index("lo")
    for n, source in enumerate(sources):
        to = (ga ^ n) * peers
        for k in range(peers):
            first = pl.multiple_of((peer ^ k) * held, held)
            for owner in range(peers):
                for user in range(users):
                    wide[to + owner, pl.ds(first + user * num, held), :] = source[
                        k, owner * users + user
                    ].astype(F32)
    for r in range(groups * peers):
        cands = wide[r].astype(BF16)
        all_ref[r] = cands
        query_ref[r] = (nn(cands, wq_ref[...]).astype(BF16).astype(F32) * scale).astype(BF16)
        out_ref[r] = nt(cands, wo_ref[...]).astype(BF16)


def prepare(sources, low, w_query, w_out):
    groups = len(sources)
    peers, group_users, held, width = sources[0].shape
    live = group_users * held
    shape = (groups * peers, live, width)
    out = jax.ShapeDtypeStruct(shape, BF16)
    vmem = pl.BlockSpec(memory_space=pltpu.VMEM)
    return pl.pallas_call(
        functools.partial(prepare_kernel, low),
        out_shape=(out,) * 3,
        in_specs=[vmem] * (groups + 2),
        out_specs=(vmem,) * 3,
        scratch_shapes=[pltpu.VMEM(shape, F32)],
        compiler_params=pltpu.CompilerParams(vmem_limit_bytes=VMEM_LIMIT),
        cost_estimate=cost(4 * groups * peers * live * width * width, 0),
        name="prepare",
    )(*sources, w_query, w_out)


def forward_kernel(
    peers,
    low,
    keep_ref,
    lists_ref,
    other_lists_ref,
    query_ref,
    out_ref,
    labels_ref,
    wk_ref,
    wv_ref,
    *refs,
):
    *others, expo_ref, dots_ref, part_ref, rows_ref, keys_ref, values_ref = refs
    sources, both, width = rows_ref.shape
    capacity = both // 2
    live = query_ref.shape[1]
    cols = HEADS * live
    some = sources // len(others)
    group_users, held = labels_ref.shape
    users = group_users // peers
    num = peers * held
    ga = lax.axis_index("ga")
    peer = lax.axis_index("hi") * low + lax.axis_index("lo")
    here = lax.div(lax.rem(lax.broadcasted_iota(jnp.int32, (1, live), 1), num), held) == peer
    user_of = lax.rem(lax.broadcasted_iota(jnp.int32, (1, cols), 1), live) // num + 1
    user_of = user_of.astype(F32)
    flags = [
        (ref[:, :capacity] & 3).astype(F32).T if capacity % 128 == 0 else
        jnp.concatenate(
            [(ref[:, :capacity] & 3).astype(F32), jnp.zeros((sources, 128 - capacity), F32)], axis=1
        ).T
        for ref in (lists_ref, other_lists_ref)
    ]
    for r in range(sources):
        rows_ref[r, :capacity, :] = keep_ref[r]
        rows_ref[r, capacity:, :] = others[r // some][r % some]
    per_tile = TILE // both
    for t in range(sources // per_tile):
        part = slice(t * per_tile, (t + 1) * per_tile)
        rows = rows_ref[part].reshape(TILE, width)
        keys_ref[part] = nn(rows, wk_ref[...]).astype(BF16).reshape(per_tile, both, width)
        values_ref[part] = nn(rows, wv_ref[...]).astype(BF16).reshape(per_tile, both, width)
    for r in range(sources):
        query = by_head(query_ref[r].astype(F32)).astype(BF16)
        out = by_head(out_ref[r].astype(F32)).astype(BF16)
        flag = jnp.concatenate([f[:capacity, r : r + 1] for f in flags], axis=0)
        score = jnp.where(flag == user_of, nt(keys_ref[r], query), LOWEST)
        top = jnp.max(score, axis=0, keepdims=True)
        e = jnp.exp(score - top)
        norm = jnp.sum(e, axis=0, keepdims=True)
        dots = nt(values_ref[r], out)
        mixed = jnp.sum(e * dots, axis=0, keepdims=True) / norm
        expo_ref[r] = e.astype(BF16)
        dots_ref[r] = dots.astype(BF16)
        label = jnp.concatenate(
            [
                labels_ref[r % peers * users + user : r % peers * users + user + 1, :]
                for user in range(users)
                for _ in range(peers)
            ],
            axis=1,
        )
        label = jnp.where(here & (ga == r // peers), label, 0.0)
        part_ref[r] = jnp.concatenate(
            [stacked(x, live) for x in (mixed, top, norm)] + [jnp.broadcast_to(label, (4, live))], axis=0
        )


def forward(keep, other, lists, other_lists, query, out, labels, peers, w_key, w_value):
    sources, capacity, width = keep.shape
    live = query.shape[1]
    cols = HEADS * live
    both = 2 * capacity
    vmem = pl.BlockSpec(memory_space=pltpu.VMEM)
    shapes = (
        ((sources, both, cols), BF16),
        ((sources, both, cols), BF16),
        ((sources, 16, live), F32),
        ((sources, both, width), BF16),
        ((sources, both, width), BF16),
        ((sources, both, width), BF16),
    )
    return pl.pallas_call(
        functools.partial(forward_kernel, peers, peers // 2),
        out_shape=tuple(jax.ShapeDtypeStruct(*shape) for shape in shapes),
        in_specs=[vmem] * (8 + len(other)),
        out_specs=(vmem,) * len(shapes),
        compiler_params=pltpu.CompilerParams(vmem_limit_bytes=VMEM_LIMIT),
        cost_estimate=cost(8 * sources * both * width * cols, sources * both * cols),
        name="forward",
    )(keep, lists, other_lists, query, out, labels, w_key, w_value, *other)


def combine_kernel(users, root, counts_ref, parts_ref, out_ref):
    sources, _, live = parts_ref.shape
    num = live // users
    top = parts_ref[0, 4:8, :]
    for k in range(1, sources):
        top = jnp.maximum(top, parts_ref[k, 4:8, :])
    norm = jnp.zeros((HEADS, live), F32)
    dots = jnp.zeros((HEADS, live), F32)
    label = jnp.zeros((1, live), F32)
    for k in range(sources):
        label = label + parts_ref[k, 12:13, :]
        share = parts_ref[k, 8:12, :] * jnp.exp(parts_ref[k, 4:8, :] - top)
        norm = norm + share
        dots = dots + share * parts_ref[k, 0:4, :]
    inv = 1.0 / norm
    dots = dots * inv
    logit = jnp.sum(dots, axis=0, keepdims=True) / root
    index = lax.broadcasted_iota(jnp.int32, (1, live), 1)
    alive = index < 0
    for user in range(users):
        alive = alive | ((index >= user * num) & (index < user * num + counts_ref[user]))
    grad = jnp.where(alive, (jax.nn.sigmoid(logit) - label) / USERS_DEV, 0.0) / root
    result = jnp.concatenate([top, inv, dots, jnp.broadcast_to(grad, (HEADS, live))], axis=0)
    for k in range(sources):
        out_ref[k] = result


def combine(parts, cand_counts, root):
    vmem = pl.BlockSpec(memory_space=pltpu.VMEM)
    return pl.pallas_call(
        functools.partial(combine_kernel, cand_counts.shape[0], root),
        out_shape=jax.ShapeDtypeStruct(parts.shape, F32),
        in_specs=[pl.BlockSpec(memory_space=pltpu.SMEM), vmem],
        out_specs=vmem,
        compiler_params=pltpu.CompilerParams(vmem_limit_bytes=VMEM_LIMIT),
        cost_estimate=cost(64 * parts.size, parts.size),
        name="combine",
    )(cand_counts, parts)


def backward_kernel(
    total_ref,
    part_ref,
    expo_ref,
    dots_ref,
    rows_ref,
    keys_ref,
    values_ref,
    cands_ref,
    query_ref,
    out_ref,
    wk_ref,
    wv_ref,
    keep_ref,
    other_ref,
    weights_ref,
    grads,
    grad_query,
    grad_out,
    weights,
):
    sources, both, width = rows_ref.shape
    capacity = both // 2
    live = query_ref.shape[1]
    scale = float(width // HEADS) ** (-0.5)
    for r in range(sources):
        query = by_head(query_ref[r].astype(F32)).astype(BF16)
        out = by_head(out_ref[r].astype(F32)).astype(BF16)
        factor = jnp.exp(part_ref[r, 4:8, :] - total_ref[r, 0:4, :]) * total_ref[r, 4:8, :]
        factor = factor * total_ref[r, 12:16, :]
        inner = flat(total_ref[r, 8:12, :])
        probs = expo_ref[r].astype(F32) * flat(factor)
        score = (probs * (dots_ref[r].astype(F32) - inner)).astype(BF16)
        probs = probs.astype(BF16)
        grads[r * both : (r + 1) * both, :width] = nn(score, query).astype(BF16)
        grads[r * both : (r + 1) * both, width:] = nn(probs, out).astype(BF16)
        mine = slice(r * live, (r + 1) * live)
        grad_query[:, mine] = (diagonal(tn(keys_ref[r], score), live) * scale).astype(BF16)
        grad_out[:, mine] = diagonal(tn(values_ref[r], probs), live).astype(BF16)
    per_tile = TILE // both
    back = jnp.concatenate([wk_ref[...].T, wv_ref[...].T], axis=0)
    by_rows = jnp.zeros((width, 2 * width), F32)
    for t in range(sources // per_tile):
        part = grads[t * TILE : (t + 1) * TILE, :]
        rows = rows_ref[t * per_tile : (t + 1) * per_tile].reshape(TILE, width)
        by_rows = by_rows + nn(rows.T, part)
        result = nn(part, back).astype(BF16)
        for k in range(per_tile):
            at = k * both
            keep_ref[t * per_tile + k] = result[at : at + capacity]
            other_ref[t * per_tile + k] = result[at + capacity : at + both]
    cands = cands_ref[...].reshape(sources * live, width)
    weights[:width, :] = nn(grad_query[...], cands).T
    weights[width : 2 * width, :] = by_rows[:, :width]
    weights[2 * width : 3 * width, :] = by_rows[:, width:]
    weights[3 * width :, :] = nn(grad_out[...], cands)
    each = 4 * width // sources
    for k in range(sources):
        weights_ref[k] = weights[k * each : (k + 1) * each, :].astype(BF16)


def backward(total, part, expo, dots, rows, keys, values, cands, query, out, w_key, w_value):
    sources, both, width = rows.shape
    live = query.shape[1]
    vmem = pl.BlockSpec(memory_space=pltpu.VMEM)
    half = jax.ShapeDtypeStruct((sources, both // 2, width), BF16)
    weights = jax.ShapeDtypeStruct((sources, 4 * width // sources, width), BF16)
    return pl.pallas_call(
        backward_kernel,
        out_shape=(half, half, weights),
        in_specs=[vmem] * 12,
        out_specs=(vmem,) * 3,
        scratch_shapes=[
            pltpu.VMEM((sources * both, 2 * width), BF16),
            pltpu.VMEM((width, sources * live), BF16),
            pltpu.VMEM((width, sources * live), BF16),
            pltpu.VMEM((4 * width, width), F32),
        ],
        compiler_params=pltpu.CompilerParams(vmem_limit_bytes=VMEM_LIMIT),
        cost_estimate=cost(16 * sources * both * width * HEADS * live, sources * both * live),
        name="backward",
    )(total, part, expo, dots, rows, keys, values, cands, query, out, w_key, w_value)


def exchange(x, axes):
    return lax.all_to_all(x, axes, split_axis=0, concat_axis=0, tiled=True)


def swap_cores(x):
    return lax.ppermute(x, "core", [(0, 1), (1, 0)])


def swap_halves(x):
    return lax.ppermute(x, "hi", [(0, 1), (1, 0)])


def gather_column(mine):
    peers, groups = lax.axis_size(PEERS), lax.axis_size("ga")
    line = jnp.stack(
        [mine]
        + [lax.ppermute(mine, PEERS, [(i, i ^ k) for i in range(peers)]) for k in range(1, peers)]
    )
    return [line] + [
        lax.ppermute(line, "ga", [(i, i ^ k) for i in range(groups)]) for k in range(1, groups)
    ]


def local(
    table, behaviour_ids, lengths, candidates, labels, cand_counts, w_query, w_key, w_value, w_out
):
    shards, peers = lax.axis_size(ALL), lax.axis_size(PEERS)
    sources = shards // 2
    first = lax.axis_index("core") == 0
    users, seq = behaviour_ids.shape
    rows_dev, width = table.shape
    total = users * seq
    capacity = total // shards + total // (2 * shards)
    held = candidates.shape[1]
    num = held * peers

    requests = plan(behaviour_ids, lengths, rows_dev, shards, peers, capacity)
    wanted = exchange(requests, BY_CORE).reshape(2, sources, capacity + LINE)
    wanted = jnp.where(first, wanted, wanted[::-1])

    column = gather_column(candidates)

    keep, *sends = gather(wanted.reshape(-1), table, shards)
    other = [swap_cores(send).reshape(-1, capacity, width) for send in sends]
    other_lists = swap_cores(wanted[1])
    keep = keep.reshape(sources, capacity, width)

    all_cands, query, out = prepare(column, lax.axis_size("lo"), w_query, w_out)
    keep, other, own_lists, other_lists = lax.optimization_barrier(
        (keep, other, wanted[0], other_lists)
    )
    expo, dots, part, rows, keys, values = forward(
        keep, other, own_lists, other_lists, query, out, labels, peers, w_key, w_value
    )
    summed = combine(exchange(part, COLUMN), cand_counts, float(width) ** 0.5)
    summed = exchange(summed, COLUMN)
    grad_keep, grad_other, weights = backward(
        summed, part, expo, dots, rows, keys, values, all_cands, query, out, w_key, w_value
    )
    back = swap_cores(grad_other)
    slots = sources * capacity
    place = lax.shift_right_logical(wanted[:, :, :capacity], 2).reshape(1, 2 * slots)
    table_grad = scatter(place, grad_keep.reshape(slots, width), back.reshape(slots, width), rows_dev)

    part = jnp.sum(exchange(weights, HALF).astype(F32), axis=0).astype(BF16)
    weight_grads = exchange(spread(part, swap_halves(part), sources), HALF)
    return table_grad, weight_grads.reshape(4, width, width).astype(F32)


def solution(mesh):
    groups, peers = mesh.shape["group"], mesh.shape["peer"]
    mesh = Mesh(mesh.devices.reshape(groups // 2, 2, 2, peers // 2), ALL)
    in_specs = (
        P(ALL, None),
        P(ALL, None),
        P(ALL),
        P(("ga", "core"), PEERS, None),
        P(("ga", "core"), PEERS),
        P(ALL),
        P(),
        P(),
        P(),
        P(),
    )
    out_specs = (P(ALL, None), P())
    return jax.shard_map(local, mesh=mesh, in_specs=in_specs, out_specs=out_specs, check_vma=False)
```

```python
import functools
import math

import jax
import jax.numpy as jnp
from jax import lax
from jax.experimental import pallas as pl
from jax.experimental.pallas import tpu as pltpu
from jax.sharding import Mesh
from jax.sharding import PartitionSpec as P

HEADS = 4
USERS_DEV = 2
PEERS = ("hi", "lo")
ALL = ("ga", "core") + PEERS
COLUMN = ("ga",) + PEERS
BY_CORE = ("core",) + COLUMN
HALF = ("ga", "core", "lo")
BF16 = jnp.bfloat16
F32 = jnp.float32
VMEM_LIMIT = 16 * 1024 * 1024
LOWEST = -1e30
LINE = 8
TILE = 768
SENDS = 2


def nt(a, b):
    return lax.dot_general(a, b, (((1,), (1,)), ((), ())), preferred_element_type=F32)


def nn(a, b):
    return jnp.dot(a, b, preferred_element_type=F32)


def cost(flops, transcendentals):
    return pl.CostEstimate(flops=flops, bytes_accessed=0, transcendentals=transcendentals)


def log2(n):
    return n.bit_length() - 1


def plan_kernel(
    rows_dev, peers, lengths_hbm, ids_hbm, requests_ref, lengths_ref, ids_ref, sems
):
    copies = [
        pltpu.make_async_copy(source, target, sems.at[k])
        for k, (source, target) in enumerate(((lengths_hbm, lengths_ref), (ids_hbm, ids_ref)))
    ]
    for copy in copies:
        copy.start()
    for copy in copies:
        copy.wait()
    users, seq = ids_ref.shape
    shards = requests_ref.shape[0]
    capacity = requests_ref.shape[1] - LINE
    block = 256
    before = (
        lax.broadcasted_iota(jnp.int32, (block, block), 0)
        < lax.broadcasted_iota(jnp.int32, (block, block), 1)
    ).astype(BF16)
    device = lax.broadcasted_iota(jnp.int32, (shards, block), 0)
    place = lax.broadcasted_iota(jnp.int32, (capacity, block), 0).astype(F32)
    lane = lax.broadcasted_iota(jnp.int32, (1, block), 1)
    count = jnp.zeros((shards, 1), F32)
    rows = jnp.zeros((3 * shards, capacity), F32)
    for user in range(users):
        for start in range(0, seq, block):
            ids = ids_ref[user : user + 1, start : start + block]
            owner = lax.shift_right_logical(ids, log2(rows_dev))
            row = ids & (rows_dev - 1)
            group = lax.shift_right_logical(owner, log2(peers))
            owner = (
                (group & 1) * (shards // 2)
                + lax.shift_right_logical(group, 1) * peers
                + (owner & (peers - 1))
            )
            live = lane + start < lengths_ref[user]
            owner = jnp.where(live, owner, shards)
            hot = (device == owner).astype(F32)
            hot_b = hot.astype(BF16)
            earlier = nn(hot_b, before) + count
            count = count + jnp.sum(hot, axis=1, keepdims=True)
            rank = jnp.sum(hot * earlier, axis=0, keepdims=True)
            ranked = (place == rank).astype(F32).astype(BF16)
            upper = lax.shift_right_logical(row, 6).astype(F32)
            lower = (row & 63).astype(F32)
            parts = jnp.concatenate([hot * upper, hot * lower, hot * float(user + 1)], axis=0)
            rows = rows + nt(parts.astype(BF16), ranked)
    row = rows[:shards] * 64.0 + rows[shards : 2 * shards]
    requests = jnp.concatenate(
        [row * 4.0 + rows[2 * shards :], jnp.broadcast_to(count, (shards, LINE))], axis=1
    )
    other = jnp.concatenate([requests[shards // 2 :], requests[: shards // 2]], axis=0)
    requests_ref[...] = requests.astype(jnp.int32) + other.astype(jnp.int32) * 65536


def plan(behaviour_ids, lengths, rows_dev, shards, peers, capacity):
    operands = (lengths, behaviour_ids)
    return pl.pallas_call(
        functools.partial(plan_kernel, rows_dev, peers),
        out_shape=jax.ShapeDtypeStruct((shards, capacity + LINE), jnp.int32),
        in_specs=[pl.BlockSpec(memory_space=pltpu.HBM)] * 2,
        out_specs=pl.BlockSpec(memory_space=pltpu.VMEM),
        scratch_shapes=[
            pltpu.SMEM(lengths.shape, jnp.int32),
            pltpu.VMEM(behaviour_ids.shape, jnp.int32),
            pltpu.SemaphoreType.DMA((2,)),
        ],
        compiler_params=pltpu.CompilerParams(vmem_limit_bytes=VMEM_LIMIT),
        cost_estimate=cost(2**24, 0),
        name="plan",
    )(*(pltpu.with_memory_space_constraint(x, pltpu.HBM) for x in operands))


def gather_kernel(blocks, wanted_ref, table_hbm, *refs):
    keep, *sends, narrow, wide, in_sems = refs
    slots = 2 * keep.shape[0]
    capacity = slots // blocks
    line = capacity + LINE
    joint = 1 if capacity % 32 == 0 else math.lcm(capacity, 16) // capacity
    step = 32 if joint == 1 else joint * capacity
    halves, _, lanes = wide.shape
    loads = in_sems.shape[0]
    size = narrow.shape[0] // loads
    copies = []
    for k in range(loads):
        part = pl.ds(k * size, size)
        copies.append(pltpu.make_async_copy(table_hbm.at[part], narrow.at[part], in_sems.at[k]))
        copies[-1].start()
    for out in (keep, *sends):
        out[...] = jnp.zeros(out.shape, BF16)
    for k, copy in enumerate(copies):
        copy.wait()
        part = slice(k * size, (k + 1) * size)
        for h in range(halves):
            wide[h, part, :] = narrow[part, h * lanes : (h + 1) * lanes].astype(F32)

    def bucket(out, skip, b, carry):
        first = (skip + b) * joint * line

        def fetch(c, carry):
            at = c * step
            start = pl.multiple_of(b * joint * capacity + at, 16)
            for k in range(0, step, 16):
                ids = [wanted_ref[first + at + n + n // capacity * LINE] for n in range(k, k + 16)]
                ids = [lax.shift_right_logical(row, 2) for row in ids]
                for h in range(halves):
                    rows = [wide[h, pl.ds(row, 1), :] for row in ids]
                    out[pl.ds(start + k, 16), h * lanes : (h + 1) * lanes] = jnp.concatenate(
                        rows, axis=0
                    ).astype(BF16)
            return carry

        steps = 1 if joint > 1 else lax.div(wanted_ref[first + capacity] + step - 1, step)
        return lax.fori_loop(0, steps, fetch, carry)

    each = blocks // joint // 2
    some = each // len(sends)
    for k, send in enumerate(sends):
        lax.fori_loop(0, some, functools.partial(bucket, send, each + k * some), 0)
    lax.fori_loop(0, each, functools.partial(bucket, keep, 0), 0)


def gather(wanted, table, blocks):
    width = table.shape[1]
    slots = wanted.shape[0] - blocks * LINE
    half = jax.ShapeDtypeStruct((slots // 2, width), BF16)
    part = jax.ShapeDtypeStruct((slots // 2 // SENDS, width), BF16)
    vmem = pl.BlockSpec(memory_space=pltpu.VMEM)
    return pl.pallas_call(
        functools.partial(gather_kernel, blocks),
        out_shape=(half,) + (part,) * SENDS,
        in_specs=[
            pl.BlockSpec(memory_space=pltpu.SMEM),
            pl.BlockSpec(memory_space=pltpu.HBM),
        ],
        out_specs=(vmem,) * (1 + SENDS),
        scratch_shapes=[
            pltpu.VMEM(table.shape, BF16),
            pltpu.VMEM((width // 128, table.shape[0], 128), F32),
            pltpu.SemaphoreType.DMA((8,)),
        ],
        compiler_params=pltpu.CompilerParams(vmem_limit_bytes=VMEM_LIMIT),
        cost_estimate=cost(6 * 10**9, 0),
        name="gather_rows",
    )(wanted, pltpu.with_memory_space_constraint(table, pltpu.HBM))


def spread_kernel(own_ref, other_ref, out_ref):
    part = (own_ref[...].astype(F32) + other_ref[...].astype(F32)).astype(BF16)
    for k in range(out_ref.shape[0]):
        out_ref[k] = part


def spread(own, other, copies):
    vmem = pl.BlockSpec(memory_space=pltpu.VMEM)
    return pl.pallas_call(
        spread_kernel,
        out_shape=pltpu.VMEM((copies,) + own.shape, BF16),
        in_specs=[vmem, vmem],
        out_specs=vmem,
        compiler_params=pltpu.CompilerParams(vmem_limit_bytes=VMEM_LIMIT),
        cost_estimate=cost(own.size, 0),
        name="spread",
    )(own, other)


def scatter_kernel(wanted_ref, keep_ref, back_ref, out_ref):
    tile = out_ref.shape[0]
    block = 256
    row = lax.broadcasted_iota(jnp.int32, (tile, block), 0) + pl.program_id(0) * tile
    total = jnp.zeros(out_ref.shape, F32)
    for k, grads in enumerate((keep_ref, back_ref)):
        slots = grads.shape[0]
        for start in range(0, slots, block):
            at = k * slots + start
            hot = (row == wanted_ref[:, at : at + block]).astype(F32).astype(BF16)
            total = total + nn(hot, grads[start : start + block, :])
    out_ref[...] = total.astype(BF16)


def scatter(wanted, keep, back, rows_dev):
    slots, width = keep.shape
    tile = 1024
    return pl.pallas_call(
        scatter_kernel,
        grid=(rows_dev // tile,),
        out_shape=jax.ShapeDtypeStruct((rows_dev, width), BF16),
        in_specs=[
            pl.BlockSpec((1, 2 * slots), lambda t: (0, 0)),
            pl.BlockSpec((slots, width), lambda t: (0, 0)),
            pl.BlockSpec((slots, width), lambda t: (0, 0)),
        ],
        out_specs=pl.BlockSpec((tile, width), lambda t: (t, 0)),
        compiler_params=pltpu.CompilerParams(vmem_limit_bytes=VMEM_LIMIT),
        cost_estimate=cost(4 * rows_dev * slots * width, 0),
        name="scatter_rows",
    )(wanted, keep, back)


def by_head(x):
    head_size = x.shape[1] // HEADS
    head = lax.broadcasted_iota(jnp.int32, x.shape, 1) // head_size
    return jnp.concatenate([jnp.where(head == h, x, 0.0) for h in range(HEADS)], axis=0)


def head_sums(x):
    size = x.shape[0] // HEADS
    return jnp.concatenate(
        [jnp.sum(x[h * size : (h + 1) * size], axis=0, keepdims=True) for h in range(HEADS)], axis=0
    )


def stacked(x, live):
    return jnp.concatenate([x[:, h * live : (h + 1) * live] for h in range(HEADS)], axis=0)


def flat(x):
    return jnp.concatenate([x[h : h + 1, :] for h in range(HEADS)], axis=1)


def diagonal(x, live):
    size = x.shape[0] // HEADS
    return jnp.concatenate(
        [x[h * size : (h + 1) * size, h * live : (h + 1) * live] for h in range(HEADS)], axis=0
    )


def tn(a, b):
    return lax.dot_general(a, b, (((0,), (0,)), ((), ())), preferred_element_type=F32)


def prepare_kernel(low, *refs):
    *sources, wq_ref, wo_ref, all_ref, query_ref, out_ref, wide = refs
    groups = len(sources)
    peers, group_users, held, width = sources[0].shape
    users = group_users // peers
    num = peers * held
    scale = float(width // HEADS) ** (-0.5)
    ga = lax.axis_index("ga")
    peer = lax.axis_index("hi") * low + lax.axis_index("lo")
    for n, source in enumerate(sources):
        to = (ga ^ n) * peers
        for k in range(peers):
            first = pl.multiple_of((peer ^ k) * held, held)
            for owner in range(peers):
                for user in range(users):
                    wide[to + owner, pl.ds(first + user * num, held), :] = source[
                        k, owner * users + user
                    ].astype(F32)
    for r in range(groups * peers):
        cands = wide[r].astype(BF16)
        all_ref[r] = cands
        query_ref[r] = (nn(cands, wq_ref[...]).astype(BF16).astype(F32) * scale).astype(BF16)
        out_ref[r] = nt(cands, wo_ref[...]).astype(BF16)


def prepare(sources, low, w_query, w_out):
    groups = len(sources)
    peers, group_users, held, width = sources[0].shape
    live = group_users * held
    shape = (groups * peers, live, width)
    out = jax.ShapeDtypeStruct(shape, BF16)
    vmem = pl.BlockSpec(memory_space=pltpu.VMEM)
    return pl.pallas_call(
        functools.partial(prepare_kernel, low),
        out_shape=(out,) * 3,
        in_specs=[vmem] * (groups + 2),
        out_specs=(vmem,) * 3,
        scratch_shapes=[pltpu.VMEM(shape, F32)],
        compiler_params=pltpu.CompilerParams(vmem_limit_bytes=VMEM_LIMIT),
        cost_estimate=cost(4 * groups * peers * live * width * width, 0),
        name="prepare",
    )(*sources, w_query, w_out)


def forward_kernel(
    peers,
    low,
    keep_ref,
    lists_ref,
    other_lists_ref,
    query_ref,
    out_ref,
    labels_ref,
    wk_ref,
    wv_ref,
    *refs,
):
    *others, expo_ref, dots_ref, part_ref, rows_ref, keys_ref, values_ref = refs
    sources, both, width = rows_ref.shape
    capacity = both // 2
    live = query_ref.shape[1]
    cols = HEADS * live
    some = sources // len(others)
    group_users, held = labels_ref.shape
    users = group_users // peers
    num = peers * held
    ga = lax.axis_index("ga")
    peer = lax.axis_index("hi") * low + lax.axis_index("lo")
    here = lax.div(lax.rem(lax.broadcasted_iota(jnp.int32, (1, live), 1), num), held) == peer
    user_of = lax.rem(lax.broadcasted_iota(jnp.int32, (1, cols), 1), live) // num + 1
    user_of = user_of.astype(F32)
    flags = [
        (ref[:, :capacity] & 3).astype(F32).T if capacity % 128 == 0 else
        jnp.concatenate(
            [(ref[:, :capacity] & 3).astype(F32), jnp.zeros((sources, 128 - capacity), F32)], axis=1
        ).T
        for ref in (lists_ref, other_lists_ref)
    ]
    for r in range(sources):
        rows_ref[r, :capacity, :] = keep_ref[r]
        rows_ref[r, capacity:, :] = others[r // some][r % some]
    per_tile = TILE // both
    for t in range(sources // per_tile):
        part = slice(t * per_tile, (t + 1) * per_tile)
        rows = rows_ref[part].reshape(TILE, width)
        keys_ref[part] = nn(rows, wk_ref[...]).astype(BF16).reshape(per_tile, both, width)
        values_ref[part] = nn(rows, wv_ref[...]).astype(BF16).reshape(per_tile, both, width)
    for r in range(sources):
        query = by_head(query_ref[r].astype(F32)).astype(BF16)
        out = by_head(out_ref[r].astype(F32)).astype(BF16)
        flag = jnp.concatenate([f[:capacity, r : r + 1] for f in flags], axis=0)
        score = jnp.where(flag == user_of, nt(keys_ref[r], query), LOWEST)
        top = jnp.max(score, axis=0, keepdims=True)
        e = jnp.exp(score - top)
        norm = jnp.sum(e, axis=0, keepdims=True)
        dots = nt(values_ref[r], out)
        mixed = jnp.sum(e * dots, axis=0, keepdims=True) / norm
        expo_ref[r] = e.astype(BF16)
        dots_ref[r] = dots.astype(BF16)
        label = jnp.concatenate(
            [
                labels_ref[r % peers * users + user : r % peers * users + user + 1, :]
                for user in range(users)
                for _ in range(peers)
            ],
            axis=1,
        )
        label = jnp.where(here & (ga == r // peers), label, 0.0)
        part_ref[r] = jnp.concatenate(
            [stacked(x, live) for x in (mixed, top, norm)] + [jnp.broadcast_to(label, (4, live))], axis=0
        )


def forward(keep, other, lists, other_lists, query, out, labels, peers, w_key, w_value):
    sources, capacity, width = keep.shape
    live = query.shape[1]
    cols = HEADS * live
    both = 2 * capacity
    vmem = pl.BlockSpec(memory_space=pltpu.VMEM)
    shapes = (
        ((sources, both, cols), BF16),
        ((sources, both, cols), BF16),
        ((sources, 16, live), F32),
        ((sources, both, width), BF16),
        ((sources, both, width), BF16),
        ((sources, both, width), BF16),
    )
    return pl.pallas_call(
        functools.partial(forward_kernel, peers, peers // 2),
        out_shape=tuple(jax.ShapeDtypeStruct(*shape) for shape in shapes),
        in_specs=[vmem] * (8 + len(other)),
        out_specs=(vmem,) * len(shapes),
        compiler_params=pltpu.CompilerParams(vmem_limit_bytes=VMEM_LIMIT),
        cost_estimate=cost(8 * sources * both * width * cols, sources * both * cols),
        name="forward",
    )(keep, lists, other_lists, query, out, labels, w_key, w_value, *other)


def combine_kernel(users, root, counts_ref, parts_ref, out_ref):
    sources, _, live = parts_ref.shape
    num = live // users
    top = parts_ref[0, 4:8, :]
    for k in range(1, sources):
        top = jnp.maximum(top, parts_ref[k, 4:8, :])
    norm = jnp.zeros((HEADS, live), F32)
    dots = jnp.zeros((HEADS, live), F32)
    label = jnp.zeros((1, live), F32)
    for k in range(sources):
        label = label + parts_ref[k, 12:13, :]
        share = parts_ref[k, 8:12, :] * jnp.exp(parts_ref[k, 4:8, :] - top)
        norm = norm + share
        dots = dots + share * parts_ref[k, 0:4, :]
    inv = 1.0 / norm
    dots = dots * inv
    logit = jnp.sum(dots, axis=0, keepdims=True) / root
    index = lax.broadcasted_iota(jnp.int32, (1, live), 1)
    alive = index < 0
    for user in range(users):
        alive = alive | ((index >= user * num) & (index < user * num + counts_ref[user]))
    grad = jnp.where(alive, (jax.nn.sigmoid(logit) - label) / USERS_DEV, 0.0) / root
    result = jnp.concatenate([top, inv, dots, jnp.broadcast_to(grad, (HEADS, live))], axis=0)
    for k in range(sources):
        out_ref[k] = result


def combine(parts, cand_counts, root):
    vmem = pl.BlockSpec(memory_space=pltpu.VMEM)
    return pl.pallas_call(
        functools.partial(combine_kernel, cand_counts.shape[0], root),
        out_shape=jax.ShapeDtypeStruct(parts.shape, F32),
        in_specs=[pl.BlockSpec(memory_space=pltpu.SMEM), vmem],
        out_specs=vmem,
        compiler_params=pltpu.CompilerParams(vmem_limit_bytes=VMEM_LIMIT),
        cost_estimate=cost(64 * parts.size, parts.size),
        name="combine",
    )(cand_counts, parts)


def backward_kernel(
    total_ref,
    part_ref,
    expo_ref,
    dots_ref,
    rows_ref,
    keys_ref,
    values_ref,
    cands_ref,
    query_ref,
    out_ref,
    wk_ref,
    wv_ref,
    keep_ref,
    other_ref,
    weights_ref,
    grads,
    grad_query,
    grad_out,
    weights,
):
    sources, both, width = rows_ref.shape
    capacity = both // 2
    live = query_ref.shape[1]
    scale = float(width // HEADS) ** (-0.5)
    for r in range(sources):
        query = by_head(query_ref[r].astype(F32)).astype(BF16)
        out = by_head(out_ref[r].astype(F32)).astype(BF16)
        factor = jnp.exp(part_ref[r, 4:8, :] - total_ref[r, 0:4, :]) * total_ref[r, 4:8, :]
        factor = factor * total_ref[r, 12:16, :]
        inner = flat(total_ref[r, 8:12, :])
        probs = expo_ref[r].astype(F32) * flat(factor)
        score = (probs * (dots_ref[r].astype(F32) - inner)).astype(BF16)
        probs = probs.astype(BF16)
        grads[r * both : (r + 1) * both, :width] = nn(score, query).astype(BF16)
        grads[r * both : (r + 1) * both, width:] = nn(probs, out).astype(BF16)
        mine = slice(r * live, (r + 1) * live)
        grad_query[:, mine] = (diagonal(tn(keys_ref[r], score), live) * scale).astype(BF16)
        grad_out[:, mine] = diagonal(tn(values_ref[r], probs), live).astype(BF16)
    per_tile = TILE // both
    back = jnp.concatenate([wk_ref[...].T, wv_ref[...].T], axis=0)
    by_rows = jnp.zeros((width, 2 * width), F32)
    for t in range(sources // per_tile):
        part = grads[t * TILE : (t + 1) * TILE, :]
        rows = rows_ref[t * per_tile : (t + 1) * per_tile].reshape(TILE, width)
        by_rows = by_rows + nn(rows.T, part)
        result = nn(part, back).astype(BF16)
        for k in range(per_tile):
            at = k * both
            keep_ref[t * per_tile + k] = result[at : at + capacity]
            other_ref[t * per_tile + k] = result[at + capacity : at + both]
    cands = cands_ref[...].reshape(sources * live, width)
    weights[:width, :] = nn(grad_query[...], cands).T
    weights[width : 2 * width, :] = by_rows[:, :width]
    weights[2 * width : 3 * width, :] = by_rows[:, width:]
    weights[3 * width :, :] = nn(grad_out[...], cands)
    each = 4 * width // sources
    for k in range(sources):
        weights_ref[k] = weights[k * each : (k + 1) * each, :].astype(BF16)


def backward(total, part, expo, dots, rows, keys, values, cands, query, out, w_key, w_value):
    sources, both, width = rows.shape
    live = query.shape[1]
    vmem = pl.BlockSpec(memory_space=pltpu.VMEM)
    half = jax.ShapeDtypeStruct((sources, both // 2, width), BF16)
    weights = jax.ShapeDtypeStruct((sources, 4 * width // sources, width), BF16)
    return pl.pallas_call(
        backward_kernel,
        out_shape=(half, half, weights),
        in_specs=[vmem] * 12,
        out_specs=(vmem,) * 3,
        scratch_shapes=[
            pltpu.VMEM((sources * both, 2 * width), BF16),
            pltpu.VMEM((width, sources * live), BF16),
            pltpu.VMEM((width, sources * live), BF16),
            pltpu.VMEM((4 * width, width), F32),
        ],
        compiler_params=pltpu.CompilerParams(vmem_limit_bytes=VMEM_LIMIT),
        cost_estimate=cost(16 * sources * both * width * HEADS * live, sources * both * live),
        name="backward",
    )(total, part, expo, dots, rows, keys, values, cands, query, out, w_key, w_value)


def exchange(x, axes):
    return lax.all_to_all(x, axes, split_axis=0, concat_axis=0, tiled=True)


def swap_cores(x):
    return lax.ppermute(x, "core", [(0, 1), (1, 0)])


def swap_halves(x):
    return lax.ppermute(x, "hi", [(0, 1), (1, 0)])


def gather_line(mine):
    peers = lax.axis_size(PEERS)
    return jnp.stack(
        [mine]
        + [lax.ppermute(mine, PEERS, [(i, i ^ k) for i in range(peers)]) for k in range(1, peers)]
    )


def gather_column(line):
    groups = lax.axis_size("ga")
    return [line] + [
        lax.ppermute(line, "ga", [(i, i ^ k) for i in range(groups)]) for k in range(1, groups)
    ]


def local(
    table, behaviour_ids, lengths, candidates, labels, cand_counts, w_query, w_key, w_value, w_out
):
    shards, peers = lax.axis_size(ALL), lax.axis_size(PEERS)
    sources = shards // 2
    first = lax.axis_index("core") == 0
    users, seq = behaviour_ids.shape
    rows_dev, width = table.shape
    total = users * seq
    capacity = total // shards + total // (2 * shards)
    held = candidates.shape[1]
    num = held * peers

    requests = plan(behaviour_ids, lengths, rows_dev, shards, peers, capacity)
    wanted = exchange(requests, BY_CORE).reshape(2, sources, capacity + LINE)
    wanted = jnp.where(first, wanted, wanted[::-1])
    other_lists = lax.shift_right_logical(wanted[0], 16)
    wanted = wanted & 65535

    line = gather_line(candidates)
    wanted, line = lax.optimization_barrier((wanted, line))
    column = gather_column(line)

    keep, *sends = gather(wanted.reshape(-1), table, shards)
    other = [swap_cores(send).reshape(-1, capacity, width) for send in sends]
    keep = keep.reshape(sources, capacity, width)

    all_cands, query, out = prepare(column, lax.axis_size("lo"), w_query, w_out)
    keep, other, own_lists, other_lists = lax.optimization_barrier(
        (keep, other, wanted[0], other_lists)
    )
    expo, dots, part, rows, keys, values = forward(
        keep, other, own_lists, other_lists, query, out, labels, peers, w_key, w_value
    )
    summed = combine(exchange(part, COLUMN), cand_counts, float(width) ** 0.5)
    summed = exchange(summed, COLUMN)
    grad_keep, grad_other, weights = backward(
        summed, part, expo, dots, rows, keys, values, all_cands, query, out, w_key, w_value
    )
    shares = exchange(weights, HALF)
    shares, grad_other = lax.optimization_barrier((shares, grad_other))
    back = swap_cores(grad_other)
    slots = sources * capacity
    place = lax.shift_right_logical(wanted[:, :, :capacity], 2).reshape(1, 2 * slots)
    table_grad = scatter(place, grad_keep.reshape(slots, width), back.reshape(slots, width), rows_dev)

    part = jnp.sum(shares.astype(F32), axis=0).astype(BF16)
    weight_grads = exchange(spread(part, swap_halves(part), sources), HALF)
    return table_grad, weight_grads.reshape(4, width, width).astype(F32)


def solution(mesh):
    groups, peers = mesh.shape["group"], mesh.shape["peer"]
    mesh = Mesh(mesh.devices.reshape(groups // 2, 2, 2, peers // 2), ALL)
    in_specs = (
        P(ALL, None),
        P(ALL, None),
        P(ALL),
        P(("ga", "core"), PEERS, None),
        P(("ga", "core"), PEERS),
        P(ALL),
        P(),
        P(),
        P(),
        P(),
    )
    out_specs = (P(ALL, None), P())
    return jax.shard_map(local, mesh=mesh, in_specs=in_specs, out_specs=out_specs, check_vma=False)
```

```python
import functools
import math

import jax
import jax.numpy as jnp
from jax import lax
from jax.experimental import pallas as pl
from jax.experimental.pallas import tpu as pltpu
from jax.sharding import Mesh
from jax.sharding import PartitionSpec as P

HEADS = 4
USERS_DEV = 2
PEERS = ("hi", "lo")
ALL = ("ga", "core") + PEERS
COLUMN = ("ga",) + PEERS
BY_CORE = ("core",) + COLUMN
HALF = ("ga", "core", "lo")
BF16 = jnp.bfloat16
F32 = jnp.float32
VMEM_LIMIT = 16 * 1024 * 1024
LOWEST = -1e30
LINE = 8
TILE = 768
SENDS = 2


def nt(a, b):
    return lax.dot_general(a, b, (((1,), (1,)), ((), ())), preferred_element_type=F32)


def nn(a, b):
    return jnp.dot(a, b, preferred_element_type=F32)


def cost(flops, transcendentals):
    return pl.CostEstimate(flops=flops, bytes_accessed=0, transcendentals=transcendentals)


def log2(n):
    return n.bit_length() - 1


def plan_kernel(
    rows_dev, peers, lengths_hbm, ids_hbm, requests_ref, lengths_ref, ids_ref, sems
):
    copies = [
        pltpu.make_async_copy(source, target, sems.at[k])
        for k, (source, target) in enumerate(((lengths_hbm, lengths_ref), (ids_hbm, ids_ref)))
    ]
    for copy in copies:
        copy.start()
    for copy in copies:
        copy.wait()
    users, seq = ids_ref.shape
    shards = requests_ref.shape[0]
    capacity = requests_ref.shape[1] - LINE
    block = 256
    before = (
        lax.broadcasted_iota(jnp.int32, (block, block), 0)
        < lax.broadcasted_iota(jnp.int32, (block, block), 1)
    ).astype(BF16)
    device = lax.broadcasted_iota(jnp.int32, (shards, block), 0)
    place = lax.broadcasted_iota(jnp.int32, (capacity, block), 0).astype(F32)
    lane = lax.broadcasted_iota(jnp.int32, (1, block), 1)
    count = jnp.zeros((shards, 1), F32)
    rows = jnp.zeros((3 * shards, capacity), F32)
    for user in range(users):
        for start in range(0, seq, block):
            ids = ids_ref[user : user + 1, start : start + block]
            owner = lax.shift_right_logical(ids, log2(rows_dev))
            row = ids & (rows_dev - 1)
            group = lax.shift_right_logical(owner, log2(peers))
            owner = (
                (group & 1) * (shards // 2)
                + lax.shift_right_logical(group, 1) * peers
                + (owner & (peers - 1))
            )
            live = lane + start < lengths_ref[user]
            owner = jnp.where(live, owner, shards)
            hot = (device == owner).astype(F32)
            hot_b = hot.astype(BF16)
            earlier = nn(hot_b, before) + count
            count = count + jnp.sum(hot, axis=1, keepdims=True)
            rank = jnp.sum(hot * earlier, axis=0, keepdims=True)
            ranked = (place == rank).astype(F32).astype(BF16)
            upper = lax.shift_right_logical(row, 6).astype(F32)
            lower = (row & 63).astype(F32)
            parts = jnp.concatenate([hot * upper, hot * lower, hot * float(user + 1)], axis=0)
            rows = rows + nt(parts.astype(BF16), ranked)
    row = rows[:shards] * 64.0 + rows[shards : 2 * shards]
    requests = jnp.concatenate(
        [row * 4.0 + rows[2 * shards :], jnp.broadcast_to(count, (shards, LINE))], axis=1
    )
    other = jnp.concatenate([requests[shards // 2 :], requests[: shards // 2]], axis=0)
    requests_ref[...] = requests.astype(jnp.int32) + other.astype(jnp.int32) * 65536


def plan(behaviour_ids, lengths, rows_dev, shards, peers, capacity):
    operands = (lengths, behaviour_ids)
    return pl.pallas_call(
        functools.partial(plan_kernel, rows_dev, peers),
        out_shape=jax.ShapeDtypeStruct((shards, capacity + LINE), jnp.int32),
        in_specs=[pl.BlockSpec(memory_space=pltpu.HBM)] * 2,
        out_specs=pl.BlockSpec(memory_space=pltpu.VMEM),
        scratch_shapes=[
            pltpu.SMEM(lengths.shape, jnp.int32),
            pltpu.VMEM(behaviour_ids.shape, jnp.int32),
            pltpu.SemaphoreType.DMA((2,)),
        ],
        compiler_params=pltpu.CompilerParams(vmem_limit_bytes=VMEM_LIMIT),
        cost_estimate=cost(2**24, 0),
        name="plan",
    )(*(pltpu.with_memory_space_constraint(x, pltpu.HBM) for x in operands))


def gather_kernel(blocks, wanted_ref, table_hbm, *refs):
    keep, *sends, narrow, wide, in_sems = refs
    slots = 2 * keep.shape[0]
    capacity = slots // blocks
    line = capacity + LINE
    joint = 1 if capacity % 32 == 0 else math.lcm(capacity, 16) // capacity
    step = 32 if joint == 1 else joint * capacity
    halves, _, lanes = wide.shape
    loads = in_sems.shape[0]
    size = narrow.shape[0] // loads
    copies = []
    for k in range(loads):
        part = pl.ds(k * size, size)
        copies.append(pltpu.make_async_copy(table_hbm.at[part], narrow.at[part], in_sems.at[k]))
        copies[-1].start()
    for out in (keep, *sends):
        out[...] = jnp.zeros(out.shape, BF16)
    for k, copy in enumerate(copies):
        copy.wait()
        part = slice(k * size, (k + 1) * size)
        for h in range(halves):
            wide[h, part, :] = narrow[part, h * lanes : (h + 1) * lanes].astype(F32)

    def bucket(out, skip, b, carry):
        first = (skip + b) * joint * line

        def fetch(c, carry):
            at = c * step
            start = pl.multiple_of(b * joint * capacity + at, 16)
            for k in range(0, step, 16):
                ids = [wanted_ref[first + at + n + n // capacity * LINE] for n in range(k, k + 16)]
                ids = [lax.shift_right_logical(row, 2) for row in ids]
                for h in range(halves):
                    rows = [wide[h, pl.ds(row, 1), :] for row in ids]
                    out[pl.ds(start + k, 16), h * lanes : (h + 1) * lanes] = jnp.concatenate(
                        rows, axis=0
                    ).astype(BF16)
            return carry

        steps = 1 if joint > 1 else lax.div(wanted_ref[first + capacity] + step - 1, step)
        return lax.fori_loop(0, steps, fetch, carry)

    each = blocks // joint // 2
    some = each // len(sends)
    for k, send in enumerate(sends):
        lax.fori_loop(0, some, functools.partial(bucket, send, each + k * some), 0)
    lax.fori_loop(0, each, functools.partial(bucket, keep, 0), 0)


def gather(wanted, table, blocks):
    width = table.shape[1]
    slots = wanted.shape[0] - blocks * LINE
    half = jax.ShapeDtypeStruct((slots // 2, width), BF16)
    part = jax.ShapeDtypeStruct((slots // 2 // SENDS, width), BF16)
    vmem = pl.BlockSpec(memory_space=pltpu.VMEM)
    return pl.pallas_call(
        functools.partial(gather_kernel, blocks),
        out_shape=(half,) + (part,) * SENDS,
        in_specs=[
            pl.BlockSpec(memory_space=pltpu.SMEM),
            pl.BlockSpec(memory_space=pltpu.HBM),
        ],
        out_specs=(vmem,) * (1 + SENDS),
        scratch_shapes=[
            pltpu.VMEM(table.shape, BF16),
            pltpu.VMEM((width // 128, table.shape[0], 128), F32),
            pltpu.SemaphoreType.DMA((8,)),
        ],
        compiler_params=pltpu.CompilerParams(vmem_limit_bytes=VMEM_LIMIT),
        cost_estimate=cost(6 * 10**9, 0),
        name="gather_rows",
    )(wanted, pltpu.with_memory_space_constraint(table, pltpu.HBM))


def spread_kernel(own_ref, other_ref, out_ref):
    part = (own_ref[...].astype(F32) + other_ref[...].astype(F32)).astype(BF16)
    for k in range(out_ref.shape[0]):
        out_ref[k] = part


def spread(own, other, copies):
    vmem = pl.BlockSpec(memory_space=pltpu.VMEM)
    return pl.pallas_call(
        spread_kernel,
        out_shape=pltpu.VMEM((copies,) + own.shape, BF16),
        in_specs=[vmem, vmem],
        out_specs=vmem,
        compiler_params=pltpu.CompilerParams(vmem_limit_bytes=VMEM_LIMIT),
        cost_estimate=cost(own.size, 0),
        name="spread",
    )(own, other)


def scatter_kernel(wanted_ref, keep_ref, back_ref, out_ref):
    tile = out_ref.shape[0]
    block = 256
    row = lax.broadcasted_iota(jnp.int32, (tile, block), 0) + pl.program_id(0) * tile
    total = jnp.zeros(out_ref.shape, F32)
    for k, grads in enumerate((keep_ref, back_ref)):
        slots = grads.shape[0]
        for start in range(0, slots, block):
            at = k * slots + start
            hot = (row == wanted_ref[:, at : at + block]).astype(F32).astype(BF16)
            total = total + nn(hot, grads[start : start + block, :])
    out_ref[...] = total.astype(BF16)


def scatter(wanted, keep, back, rows_dev):
    slots, width = keep.shape
    tile = 1024
    return pl.pallas_call(
        scatter_kernel,
        grid=(rows_dev // tile,),
        out_shape=jax.ShapeDtypeStruct((rows_dev, width), BF16),
        in_specs=[
            pl.BlockSpec((1, 2 * slots), lambda t: (0, 0)),
            pl.BlockSpec((slots, width), lambda t: (0, 0)),
            pl.BlockSpec((slots, width), lambda t: (0, 0)),
        ],
        out_specs=pl.BlockSpec((tile, width), lambda t: (t, 0)),
        compiler_params=pltpu.CompilerParams(vmem_limit_bytes=VMEM_LIMIT),
        cost_estimate=cost(4 * rows_dev * slots * width, 0),
        name="scatter_rows",
    )(wanted, keep, back)


def by_head(x):
    head_size = x.shape[1] // HEADS
    head = lax.broadcasted_iota(jnp.int32, x.shape, 1) // head_size
    return jnp.concatenate([jnp.where(head == h, x, 0.0) for h in range(HEADS)], axis=0)


def head_sums(x):
    size = x.shape[0] // HEADS
    return jnp.concatenate(
        [jnp.sum(x[h * size : (h + 1) * size], axis=0, keepdims=True) for h in range(HEADS)], axis=0
    )


def stacked(x, live):
    return jnp.concatenate([x[:, h * live : (h + 1) * live] for h in range(HEADS)], axis=0)


def flat(x):
    return jnp.concatenate([x[h : h + 1, :] for h in range(HEADS)], axis=1)


def diagonal(x, live):
    size = x.shape[0] // HEADS
    return jnp.concatenate(
        [x[h * size : (h + 1) * size, h * live : (h + 1) * live] for h in range(HEADS)], axis=0
    )


def tn(a, b):
    return lax.dot_general(a, b, (((0,), (0,)), ((), ())), preferred_element_type=F32)


def prepare_kernel(low, *refs):
    *sources, wq_ref, wo_ref, all_ref, query_ref, out_ref, wide = refs
    groups = len(sources)
    peers, group_users, held, width = sources[0].shape
    users = group_users // peers
    num = peers * held
    scale = float(width // HEADS) ** (-0.5)
    ga = lax.axis_index("ga")
    peer = lax.axis_index("hi") * low + lax.axis_index("lo")
    for n, source in enumerate(sources):
        to = (ga ^ n) * peers
        for k in range(peers):
            first = pl.multiple_of((peer ^ k) * held, held)
            for owner in range(peers):
                for user in range(users):
                    wide[to + owner, pl.ds(first + user * num, held), :] = source[
                        k, owner * users + user
                    ].astype(F32)
    for r in range(groups * peers):
        cands = wide[r].astype(BF16)
        all_ref[r] = cands
        query_ref[r] = (nn(cands, wq_ref[...]).astype(BF16).astype(F32) * scale).astype(BF16)
        out_ref[r] = nt(cands, wo_ref[...]).astype(BF16)


def prepare(sources, low, w_query, w_out):
    groups = len(sources)
    peers, group_users, held, width = sources[0].shape
    live = group_users * held
    shape = (groups * peers, live, width)
    out = jax.ShapeDtypeStruct(shape, BF16)
    vmem = pl.BlockSpec(memory_space=pltpu.VMEM)
    return pl.pallas_call(
        functools.partial(prepare_kernel, low),
        out_shape=(out,) * 3,
        in_specs=[vmem] * (groups + 2),
        out_specs=(vmem,) * 3,
        scratch_shapes=[pltpu.VMEM(shape, F32)],
        compiler_params=pltpu.CompilerParams(vmem_limit_bytes=VMEM_LIMIT),
        cost_estimate=cost(4 * groups * peers * live * width * width, 0),
        name="prepare",
    )(*sources, w_query, w_out)


def forward_kernel(
    peers,
    low,
    keep_ref,
    lists_ref,
    other_lists_ref,
    query_ref,
    out_ref,
    labels_ref,
    wk_ref,
    wv_ref,
    *refs,
):
    *others, expo_ref, dots_ref, part_ref, rows_ref, keys_ref, values_ref = refs
    sources, both, width = rows_ref.shape
    capacity = both // 2
    live = query_ref.shape[1]
    cols = HEADS * live
    some = sources // len(others)
    group_users, held = labels_ref.shape
    users = group_users // peers
    num = peers * held
    ga = lax.axis_index("ga")
    peer = lax.axis_index("hi") * low + lax.axis_index("lo")
    here = lax.div(lax.rem(lax.broadcasted_iota(jnp.int32, (1, live), 1), num), held) == peer
    user_of = lax.rem(lax.broadcasted_iota(jnp.int32, (1, cols), 1), live) // num + 1
    user_of = user_of.astype(F32)
    flags = [
        (ref[:, :capacity] & 3).astype(F32).T if capacity % 128 == 0 else
        jnp.concatenate(
            [(ref[:, :capacity] & 3).astype(F32), jnp.zeros((sources, 128 - capacity), F32)], axis=1
        ).T
        for ref in (lists_ref, other_lists_ref)
    ]
    for r in range(sources):
        rows_ref[r, :capacity, :] = keep_ref[r]
        rows_ref[r, capacity:, :] = others[r // some][r % some]
    per_tile = TILE // both
    for t in range(sources // per_tile):
        part = slice(t * per_tile, (t + 1) * per_tile)
        rows = rows_ref[part].reshape(TILE, width)
        keys_ref[part] = nn(rows, wk_ref[...]).astype(BF16).reshape(per_tile, both, width)
        values_ref[part] = nn(rows, wv_ref[...]).astype(BF16).reshape(per_tile, both, width)
    for r in range(sources):
        query = by_head(query_ref[r].astype(F32)).astype(BF16)
        out = by_head(out_ref[r].astype(F32)).astype(BF16)
        flag = jnp.concatenate([f[:capacity, r : r + 1] for f in flags], axis=0)
        score = jnp.where(flag == user_of, nt(keys_ref[r], query), LOWEST)
        top = jnp.max(score, axis=0, keepdims=True)
        e = jnp.exp(score - top)
        norm = jnp.sum(e, axis=0, keepdims=True)
        dots = nt(values_ref[r], out)
        mixed = jnp.sum(e * dots, axis=0, keepdims=True) / norm
        expo_ref[r] = e.astype(BF16)
        dots_ref[r] = dots.astype(BF16)
        label = jnp.concatenate(
            [
                labels_ref[r % peers * users + user : r % peers * users + user + 1, :]
                for user in range(users)
                for _ in range(peers)
            ],
            axis=1,
        )
        label = jnp.where(here & (ga == r // peers), label, 0.0)
        part_ref[r] = jnp.concatenate(
            [stacked(x, live) for x in (mixed, top, norm)] + [jnp.broadcast_to(label, (4, live))], axis=0
        )


def forward(keep, other, lists, other_lists, query, out, labels, peers, w_key, w_value):
    sources, capacity, width = keep.shape
    live = query.shape[1]
    cols = HEADS * live
    both = 2 * capacity
    vmem = pl.BlockSpec(memory_space=pltpu.VMEM)
    shapes = (
        ((sources, both, cols), BF16),
        ((sources, both, cols), BF16),
        ((sources, 16, live), F32),
        ((sources, both, width), BF16),
        ((sources, both, width), BF16),
        ((sources, both, width), BF16),
    )
    return pl.pallas_call(
        functools.partial(forward_kernel, peers, peers // 2),
        out_shape=tuple(jax.ShapeDtypeStruct(*shape) for shape in shapes),
        in_specs=[vmem] * (8 + len(other)),
        out_specs=(vmem,) * len(shapes),
        compiler_params=pltpu.CompilerParams(vmem_limit_bytes=VMEM_LIMIT),
        cost_estimate=cost(8 * sources * both * width * cols, sources * both * cols),
        name="forward",
    )(keep, lists, other_lists, query, out, labels, w_key, w_value, *other)


def combine_kernel(users, root, counts_ref, parts_ref, out_ref):
    sources, _, live = parts_ref.shape
    num = live // users
    top = parts_ref[0, 4:8, :]
    for k in range(1, sources):
        top = jnp.maximum(top, parts_ref[k, 4:8, :])
    norm = jnp.zeros((HEADS, live), F32)
    dots = jnp.zeros((HEADS, live), F32)
    label = jnp.zeros((1, live), F32)
    for k in range(sources):
        label = label + parts_ref[k, 12:13, :]
        share = parts_ref[k, 8:12, :] * jnp.exp(parts_ref[k, 4:8, :] - top)
        norm = norm + share
        dots = dots + share * parts_ref[k, 0:4, :]
    inv = 1.0 / norm
    dots = dots * inv
    logit = jnp.sum(dots, axis=0, keepdims=True) / root
    index = lax.broadcasted_iota(jnp.int32, (1, live), 1)
    alive = index < 0
    for user in range(users):
        alive = alive | ((index >= user * num) & (index < user * num + counts_ref[user]))
    grad = jnp.where(alive, (jax.nn.sigmoid(logit) - label) / USERS_DEV, 0.0) / root
    result = jnp.concatenate([top, inv, dots, jnp.broadcast_to(grad, (HEADS, live))], axis=0)
    for k in range(sources):
        out_ref[k] = result


def combine(parts, cand_counts, root):
    vmem = pl.BlockSpec(memory_space=pltpu.VMEM)
    return pl.pallas_call(
        functools.partial(combine_kernel, cand_counts.shape[0], root),
        out_shape=jax.ShapeDtypeStruct(parts.shape, F32),
        in_specs=[pl.BlockSpec(memory_space=pltpu.SMEM), vmem],
        out_specs=vmem,
        compiler_params=pltpu.CompilerParams(vmem_limit_bytes=VMEM_LIMIT),
        cost_estimate=cost(64 * parts.size, parts.size),
        name="combine",
    )(cand_counts, parts)


def backward_kernel(
    total_ref,
    part_ref,
    expo_ref,
    dots_ref,
    rows_ref,
    keys_ref,
    values_ref,
    cands_ref,
    query_ref,
    out_ref,
    wk_ref,
    wv_ref,
    keep_ref,
    other_ref,
    weights_ref,
    grads,
    grad_query,
    grad_out,
    weights,
):
    sources, both, width = rows_ref.shape
    capacity = both // 2
    live = query_ref.shape[1]
    scale = float(width // HEADS) ** (-0.5)
    for r in range(sources):
        query = by_head(query_ref[r].astype(F32)).astype(BF16)
        out = by_head(out_ref[r].astype(F32)).astype(BF16)
        factor = jnp.exp(part_ref[r, 4:8, :] - total_ref[r, 0:4, :]) * total_ref[r, 4:8, :]
        factor = factor * total_ref[r, 12:16, :]
        inner = flat(total_ref[r, 8:12, :])
        probs = expo_ref[r].astype(F32) * flat(factor)
        score = (probs * (dots_ref[r].astype(F32) - inner)).astype(BF16)
        probs = probs.astype(BF16)
        grads[r * both : (r + 1) * both, :width] = nn(score, query).astype(BF16)
        grads[r * both : (r + 1) * both, width:] = nn(probs, out).astype(BF16)
        mine = slice(r * live, (r + 1) * live)
        grad_query[:, mine] = (diagonal(tn(keys_ref[r], score), live) * scale).astype(BF16)
        grad_out[:, mine] = diagonal(tn(values_ref[r], probs), live).astype(BF16)
    per_tile = TILE // both
    back = jnp.concatenate([wk_ref[...].T, wv_ref[...].T], axis=0)
    by_rows = jnp.zeros((width, 2 * width), F32)
    for t in range(sources // per_tile):
        part = grads[t * TILE : (t + 1) * TILE, :]
        rows = rows_ref[t * per_tile : (t + 1) * per_tile].reshape(TILE, width)
        by_rows = by_rows + nn(rows.T, part)
        result = nn(part, back).astype(BF16)
        for k in range(per_tile):
            at = k * both
            keep_ref[t * per_tile + k] = result[at : at + capacity]
            other_ref[t * per_tile + k] = result[at + capacity : at + both]
    cands = cands_ref[...].reshape(sources * live, width)
    weights[:width, :] = nn(grad_query[...], cands).T
    weights[width : 2 * width, :] = by_rows[:, :width]
    weights[2 * width : 3 * width, :] = by_rows[:, width:]
    weights[3 * width :, :] = nn(grad_out[...], cands)
    each = 4 * width // sources
    for k in range(sources):
        weights_ref[k] = weights[k * each : (k + 1) * each, :].astype(BF16)


def backward(total, part, expo, dots, rows, keys, values, cands, query, out, w_key, w_value):
    sources, both, width = rows.shape
    live = query.shape[1]
    vmem = pl.BlockSpec(memory_space=pltpu.VMEM)
    half = jax.ShapeDtypeStruct((sources, both // 2, width), BF16)
    weights = jax.ShapeDtypeStruct((sources, 4 * width // sources, width), BF16)
    return pl.pallas_call(
        backward_kernel,
        out_shape=(half, half, weights),
        in_specs=[vmem] * 12,
        out_specs=(vmem,) * 3,
        scratch_shapes=[
            pltpu.VMEM((sources * both, 2 * width), BF16),
            pltpu.VMEM((width, sources * live), BF16),
            pltpu.VMEM((width, sources * live), BF16),
            pltpu.VMEM((4 * width, width), F32),
        ],
        compiler_params=pltpu.CompilerParams(vmem_limit_bytes=VMEM_LIMIT),
        cost_estimate=cost(16 * sources * both * width * HEADS * live, sources * both * live),
        name="backward",
    )(total, part, expo, dots, rows, keys, values, cands, query, out, w_key, w_value)


def exchange(x, axes):
    return lax.all_to_all(x, axes, split_axis=0, concat_axis=0, tiled=True)


def swap_cores(x):
    return lax.ppermute(x, "core", [(0, 1), (1, 0)])


def swap_halves(x):
    return lax.ppermute(x, "hi", [(0, 1), (1, 0)])


def together_kernel(*refs):
    *pieces, out_ref = refs
    for k, piece in enumerate(pieces):
        out_ref[k] = piece[...]


def together(pieces):
    vmem = pl.BlockSpec(memory_space=pltpu.VMEM)
    return pl.pallas_call(
        together_kernel,
        out_shape=jax.ShapeDtypeStruct((len(pieces),) + pieces[0].shape, pieces[0].dtype),
        in_specs=[vmem] * len(pieces),
        out_specs=vmem,
        compiler_params=pltpu.CompilerParams(vmem_limit_bytes=VMEM_LIMIT),
        cost_estimate=cost(pieces[0].size, 0),
        name="together",
    )(*pieces)


def gather_line(mine):
    peers = lax.axis_size(PEERS)
    return together(
        [mine]
        + [lax.ppermute(mine, PEERS, [(i, i ^ k) for i in range(peers)]) for k in range(1, peers)]
    )


def gather_column(line):
    groups = lax.axis_size("ga")
    return [line] + [
        lax.ppermute(line, "ga", [(i, i ^ k) for i in range(groups)]) for k in range(1, groups)
    ]


def local(
    table, behaviour_ids, lengths, candidates, labels, cand_counts, w_query, w_key, w_value, w_out
):
    shards, peers = lax.axis_size(ALL), lax.axis_size(PEERS)
    sources = shards // 2
    first = lax.axis_index("core") == 0
    users, seq = behaviour_ids.shape
    rows_dev, width = table.shape
    total = users * seq
    capacity = total // shards + total // (2 * shards)
    held = candidates.shape[1]
    num = held * peers

    requests = plan(behaviour_ids, lengths, rows_dev, shards, peers, capacity)
    wanted = exchange(requests, BY_CORE).reshape(2, sources, capacity + LINE)
    wanted = jnp.where(first, wanted, wanted[::-1])
    other_lists = lax.shift_right_logical(wanted[0], 16)
    wanted = wanted & 65535

    line = gather_line(candidates)
    wanted, line = lax.optimization_barrier((wanted, line))
    column = gather_column(line)

    keep, *sends = gather(wanted.reshape(-1), table, shards)
    other = [swap_cores(send).reshape(-1, capacity, width) for send in sends]
    keep = keep.reshape(sources, capacity, width)

    all_cands, query, out = prepare(column, lax.axis_size("lo"), w_query, w_out)
    keep, other, own_lists, other_lists = lax.optimization_barrier(
        (keep, other, wanted[0], other_lists)
    )
    expo, dots, part, rows, keys, values = forward(
        keep, other, own_lists, other_lists, query, out, labels, peers, w_key, w_value
    )
    summed = combine(exchange(part, COLUMN), cand_counts, float(width) ** 0.5)
    summed = exchange(summed, COLUMN)
    grad_keep, grad_other, weights = backward(
        summed, part, expo, dots, rows, keys, values, all_cands, query, out, w_key, w_value
    )
    shares = exchange(weights, HALF)
    shares, grad_other = lax.optimization_barrier((shares, grad_other))
    back = swap_cores(grad_other)
    slots = sources * capacity
    place = lax.shift_right_logical(wanted[:, :, :capacity], 2).reshape(1, 2 * slots)
    table_grad = scatter(place, grad_keep.reshape(slots, width), back.reshape(slots, width), rows_dev)

    part = jnp.sum(shares.astype(F32), axis=0).astype(BF16)
    weight_grads = exchange(spread(part, swap_halves(part), sources), HALF)
    return table_grad, weight_grads.reshape(4, width, width).astype(F32)


def solution(mesh):
    groups, peers = mesh.shape["group"], mesh.shape["peer"]
    mesh = Mesh(mesh.devices.reshape(groups // 2, 2, 2, peers // 2), ALL)
    in_specs = (
        P(ALL, None),
        P(ALL, None),
        P(ALL),
        P(("ga", "core"), PEERS, None),
        P(("ga", "core"), PEERS),
        P(ALL),
        P(),
        P(),
        P(),
        P(),
    )
    out_specs = (P(ALL, None), P())
    return jax.shard_map(local, mesh=mesh, in_specs=in_specs, out_specs=out_specs, check_vma=False)
```
